256 devices in a mesh: outer: 8 (over x, core), inner: 4 (over y), heads: 8 (over z).
Axes of the slice: x: 4, y: 4, z: 8, core: 2. Of those that a mesh axis runs over, the one named last changes fastest.
Arguments:
- x_in: bfloat16 [8192, 8192], P(('outer', 'inner'), 'heads'), may hold values from -6 to 6
- b_in: bfloat16 [8192, 1024], P(('outer', 'inner'), 'heads'), may hold values from -1.796875 to 1.796875
- c_in: bfloat16 [8192, 1024], P(('outer', 'inner'), 'heads'), may hold values from -1.796875 to 1.796875
- decay_log: float32 [8192, 128], P(('outer', 'inner'), 'heads'), may hold values from -0.8 to 0, as said below
- d_skip: float32 [128], P('heads'), may hold values from 0.5 to 1.5
- gate: bfloat16 [8192, 8192], P(('outer', 'inner'), 'heads'), may hold values from -11 to 11
- norm_weight: float32 [8192], P('heads'), may hold values from 0.5 to 1.5
- d_out: bfloat16 [8192, 8192], P(('outer', 'inner'), 'heads'), may hold values from -40 to 40
Outputs:
- grad_x: bfloat16 [8192, 8192], P(('outer', 'inner'), 'heads')
- grad_b: float32 [8192, 1024], P(('outer', 'inner'), 'heads')
- grad_c: float32 [8192, 1024], P(('outer', 'inner'), 'heads')
- grad_decay: float32 [8192, 128], P(('outer', 'inner'), 'heads')
- grad_skip: float32 [128], P('heads')
- grad_gate: bfloat16 [8192, 8192], P(('outer', 'inner'), 'heads')
- grad_norm_weight: float32 [8192], P('heads')
The draws below stay inside these ranges and needn't reach their ends.
Inputs may be any that keep to these rules, and one draw needn't show every extreme that they name: `decay_log`: strictly negative.
All inputs are finite; a program needn't handle non-finite values.
Results may differ from the reference program's by a relative error of at most 0.0014.
Values sent between devices are 32-bit elements; how exact they have to be, the bound alone decides.
No kernel may reach another device: no remote copies, remote signals or barrier semaphores. Data moves between devices by JAX's collectives and lax.ppermute only.
A program may use at most 128 MiB of HBM per device.

```python
import jax
import jax.numpy as jnp
from jax import lax

HEADS = 128
P_SIZE = 64
STATE = 128
SHARED_BC_SETS = 8
SPAN = 256
L_DEV = 256
SPAN_POSITIONS = 8192


def draw_x_in(key, part):
    key = jax.random.fold_in(key, 19)
    width = HEADS * P_SIZE
    boundary = SPAN_POSITIONS // L_DEV // 2 * L_DEV
    positions = jnp.arange(SPAN_POSITIONS)
    row_level = jnp.where(positions >= boundary, 0.12, 1.0).astype(jnp.float32)
    values = jnp.clip(jax.random.normal(key, (SPAN_POSITIONS, width), jnp.float32), -6.0, 6.0)
    return (values * row_level[:, None]).astype(jnp.bfloat16)


def draw_decay_log(key, part):
    key = jax.random.fold_in(key, 11)
    seed_sequence = jax.random.split(key, 5)
    share = 0.5
    slow = jax.random.bernoulli(seed_sequence[0], share, (HEADS,))
    fast_rate = 1.0 / jax.random.uniform(seed_sequence[1], (HEADS,), jnp.float32, 30.0, 50.0)
    starting_shift = jnp.where(slow, 0.7 / SPAN_POSITIONS, fast_rate)
    approximate_guess = jnp.exp(jax.random.uniform(seed_sequence[2], (SPAN_POSITIONS, HEADS), jnp.float32, -0.7, 0.7))
    transfer_extent = jax.random.bernoulli(seed_sequence[3], 3.0 / SPAN_POSITIONS, (SPAN_POSITIONS, 1))
    nesting_tiers = jax.random.uniform(seed_sequence[4], (SPAN_POSITIONS, HEADS), jnp.float32, 0.22, 0.69)
    values = -(starting_shift[None, :] * approximate_guess) - jnp.where(transfer_extent, nesting_tiers, 0.0)
    boundary = SPAN_POSITIONS // L_DEV // 2 * L_DEV
    positions = jnp.arange(SPAN_POSITIONS)
    reset_rows = (positions >= boundary) & (positions < boundary + 9)
    return jnp.where(reset_rows[:, None], -0.8, values).astype(jnp.float32)


def draw_gate(key, part):
    key = jax.random.fold_in(key, 13)
    seed_sequence = jax.random.split(key, 2)
    width = HEADS * P_SIZE
    place = jnp.arange(width, dtype=jnp.float32) / width
    scale = jnp.exp(jnp.log(3.0) * place) * jnp.exp(jax.random.uniform(seed_sequence[0], (width,), jnp.float32, 0.0, 0.7)) / 1.7
    starting_shift = jnp.clip(jax.random.normal(seed_sequence[1], (SPAN_POSITIONS, width), jnp.float32), -3.0, 3.0)
    return (starting_shift * scale[None, :]).astype(jnp.bfloat16)


def draw_d_out(key, part):
    key = jax.random.fold_in(key, 17)
    seed_sequence = jax.random.split(key, 3)
    width = HEADS * P_SIZE
    place = jnp.arange(SPAN_POSITIONS, dtype=jnp.float32) / SPAN_POSITIONS
    rise = jnp.exp(jnp.log(3.0) * place) / jnp.sqrt(3.0)
    row_scale = jnp.exp(jax.random.uniform(seed_sequence[0], (SPAN_POSITIONS,), jnp.float32, -1.15, 1.15))
    column_factor = jnp.exp(jax.random.uniform(seed_sequence[1], (width,), jnp.float32, -0.6, 0.6))
    starting_shift = jnp.clip(jax.random.normal(seed_sequence[2], (SPAN_POSITIONS, width), jnp.float32), -4.0, 4.0)
    return (starting_shift * (rise * row_scale)[:, None] * column_factor[None, :]).astype(jnp.bfloat16)


def level_of(own_key, extent, cuts, low, high):
    factor_of, own = 1.0, jax.random.fold_in(own_key, 6)
    for dim, blocks in cuts:
        heights = jnp.exp(jax.random.uniform(jax.random.fold_in(own, dim), (blocks,), jnp.float32, low / len(cuts), high / len(cuts)))
        factor_of = factor_of * jnp.repeat(heights, extent[dim] // blocks).reshape([-1 if axis == dim else 1 for axis in range(len(extent))])
    return factor_of


def bell_draw(stream_key, extent, spread, limit, cuts=(), held_as=jnp.bfloat16):
    drawn = spread * jax.random.normal(stream_key, extent, jnp.float32)
    if cuts:
        drawn = drawn * level_of(stream_key, extent, cuts, -0.22, 0.18)
    return jnp.clip(drawn, -limit, limit).astype(held_as)


def setup_inputs(seed: int = 0) -> dict:
    streams_of = jax.random.split(jax.random.key(seed), 9)
    x_in = draw_x_in(jax.random.fold_in(streams_of[8], 71), 0)
    b_in = bell_draw(streams_of[1], (SPAN_POSITIONS, SHARED_BC_SETS * STATE), 0.3, 1.796875, ((0, 32), (1, 8)))
    c_in = bell_draw(streams_of[2], (SPAN_POSITIONS, SHARED_BC_SETS * STATE), 0.3, 1.796875, ((0, 32), (1, 8)))
    decay_log = draw_decay_log(jax.random.fold_in(streams_of[8], 71), 0)
    d_skip = jnp.clip(0.5 + 1.0 * jax.random.uniform(streams_of[4], (HEADS,), jnp.float32) ** level_of(streams_of[4], (HEADS,), ((0, 8),), -0.2, 0.2), 0.5, 1.5)
    gate = draw_gate(jax.random.fold_in(streams_of[8], 71), 0)
    norm_weight = jnp.clip(1.0 + 0.1 * jax.random.normal(streams_of[6], (HEADS * P_SIZE,), jnp.float32), 0.5, 1.5)
    d_out = draw_d_out(jax.random.fold_in(streams_of[8], 71), 0)
    return dict(x_in=x_in, b_in=b_in, c_in=c_in, decay_log=decay_log, d_skip=d_skip, gate=gate, norm_weight=norm_weight, d_out=d_out)


EPS = 1e-05
HIGH = lax.Precision.HIGHEST

def block_step(carried, pieces, d_skip, norm_weight):
    x_blk, b_blk, c_blk, l_blk, z_blk = pieces
    heads_per = HEADS // SHARED_BC_SETS
    cumul = jnp.cumsum(l_blk, axis=0)
    last = cumul[-1]
    rows = lax.broadcasted_iota(jnp.int32, (SPAN, SPAN), 0)
    cols = lax.broadcasted_iota(jnp.int32, (SPAN, SPAN), 1)
    lower = rows >= cols
    diff = cumul.T[:, :, None] - cumul.T[:, None, :]
    decay = jnp.where(lower, jnp.exp(jnp.where(lower, diff, 0.0)), 0.0)
    inner = jnp.einsum('ign,jgn->gij', c_blk, b_blk, precision=HIGH)
    weights = jnp.repeat(inner, heads_per, axis=0) * decay
    b_heads = jnp.repeat(b_blk, heads_per, axis=1)
    c_heads = jnp.repeat(c_blk, heads_per, axis=1)
    y_val = jnp.einsum('hij,jhp->ihp', weights, x_blk, precision=HIGH)
    y_val = y_val + jnp.exp(cumul)[:, :, None] * jnp.einsum('ihn,hnp->ihp', c_heads, carried, precision=HIGH)
    y_val = y_val + d_skip[None, :, None] * x_blk
    tail = jnp.exp(last[None, :] - cumul)
    new_state = jnp.exp(last)[:, None, None] * carried + jnp.einsum('jhn,jhp->hnp', b_heads * tail[:, :, None], x_blk, precision=HIGH)
    gated = (y_val * jax.nn.silu(z_blk)).reshape(SPAN, HEADS * P_SIZE)
    mean_sq = lax.optimization_barrier(jnp.mean(gated * gated, axis=1, keepdims=True))
    result = gated * lax.rsqrt(mean_sq + EPS) * norm_weight[None, :]
    return (new_state, result)

def forward(x_in, b_in, c_in, decay_log, d_skip, gate, norm_weight):
    blocks = SPAN_POSITIONS // SPAN
    x_all = x_in.reshape(blocks, SPAN, HEADS, P_SIZE)
    b_all = b_in.reshape(blocks, SPAN, SHARED_BC_SETS, STATE)
    c_all = c_in.reshape(blocks, SPAN, SHARED_BC_SETS, STATE)
    l_all = decay_log.reshape(blocks, SPAN, HEADS)
    z_all = gate.reshape(blocks, SPAN, HEADS, P_SIZE)

    def step(carried, pieces):
        return block_step(carried, pieces, d_skip, norm_weight)
    start = jnp.zeros((HEADS, STATE, P_SIZE), x_in.dtype)
    _, outputs = lax.scan(jax.checkpoint(step), start, (x_all, b_all, c_all, l_all, z_all))
    return outputs.reshape(SPAN_POSITIONS, HEADS * P_SIZE)

def reference(x_in, b_in, c_in, decay_log, d_skip, gate, norm_weight, d_out):
    primals = (x_in.astype(jnp.float32), b_in.astype(jnp.float32), c_in.astype(jnp.float32), decay_log, d_skip, gate.astype(jnp.float32), norm_weight)
    _, pullback = jax.vjp(forward, *primals)
    gx, gb, gc, gl, gd, gz, gw = pullback(d_out.astype(jnp.float32))
    return (gx.astype(jnp.bfloat16), gb, gc, gl, gd, gz.astype(jnp.bfloat16), gw)
```

```python
import jax
import jax.numpy as jnp
from jax import lax
from jax.experimental import pallas as pl
from jax.experimental.pallas import tpu as pltpu
from jax.sharding import PartitionSpec as P

P_SIZE = 64
EPS = 1e-05
F32 = jnp.float32
BF16 = jnp.bfloat16
CHUNKS = ("outer", "inner")
VMEM = pl.BlockSpec(memory_space=pltpu.VMEM)
HALF = 128


def mm(a, b, ca=1, cb=0):
    return lax.dot_general(a, b, (((ca,), (cb,)), ((), ())), preferred_element_type=F32)


def split2(a):
    hi = a.astype(BF16)
    return hi, (a - hi.astype(F32)).astype(BF16)


def split3(a):
    hi = a.astype(BF16)
    rest = a - hi.astype(F32)
    mid = rest.astype(BF16)
    return hi, mid, (rest - mid.astype(F32)).astype(BF16)


def mm2(a, b, ca=1, cb=0):
    hi, lo = split2(a)
    return mm(hi, b, ca, cb) + mm(lo, b, ca, cb)


def iota(shape, dim):
    return lax.broadcasted_iota(jnp.int32, shape, dim)


def head_map(heads, width):
    return jnp.where(iota((heads, width), 1) // P_SIZE == iota((heads, width), 0), 1.0, 0.0).astype(BF16)


def expand(a, spread):
    hi, mid, lo = split3(a)
    return mm(hi, spread) + mm(mid, spread) + mm(lo, spread)


def segment(a, spread):
    hi, lo = split2(a)
    return mm(hi, spread, 1, 1) + mm(lo, spread, 1, 1)


def triangle(n, keep):
    return jnp.where(keep(iota((n, n), 0), iota((n, n), 1)), 1.0, 0.0).astype(BF16)


def mm_tri(tri, a):
    hi, mid, lo = split3(a)
    return mm(tri, hi) + mm(tri, mid) + mm(tri, lo)


def store_state(out_ref, state):
    for r in range(16):
        for f in range(2):
            out_ref[2 * r + f, :, 0:512] = state[8 * r : 8 * r + 8, 512 * f : 512 * f + 512]


def load_state(ref):
    rows = []
    for r in range(16):
        rows.append(jnp.concatenate([ref[2 * r, :, 0:512], ref[2 * r + 1, :, 0:512]], axis=1))
    return jnp.concatenate(rows, axis=0)


def start_kernel(l_ref, x_ref, b_ref, pay_ref, cum_ref, tail_ref):
    length, heads = l_ref.shape
    width = x_ref.shape[1]
    spread = head_map(heads, width)
    cum = mm_tri(triangle(length, lambda i, j: i >= j), l_ref[...])
    cum_ref[...] = cum
    last = cum[length - 1 : length, :]
    tail = expand(jnp.exp(last - cum), spread)
    tail_ref[...] = tail
    hi, lo = split2(x_ref[...].astype(F32) * tail)
    b_val = b_ref[...]
    state = mm(b_val, hi, 0, 0) + mm(b_val, lo, 0, 0)
    store_state(pay_ref, state)
    whole = expand(jnp.broadcast_to(jnp.exp(last), (8, heads)), spread)[0:1, :]
    for f in range(2):
        rows = [whole[:, 512 * f + HALF * j : 512 * f + HALF * (j + 1)] for j in range(4)]
        tile = jnp.concatenate(rows + [jnp.zeros((4, HALF), F32)], axis=0)
        for r in range(16):
            pay_ref[2 * r + f, :, 512:640] = tile


def local_kernel(cum_ref, x_ref, b_ref, c_ref, z_ref, d_ref, yn_ref, base_ref, silu_ref, esilu_ref, ecum_ref):
    length, heads = cum_ref.shape
    width = x_ref.shape[1]
    spread = head_map(heads, width)
    cum = cum_ref[...]
    cum_t = cum.T
    ecum = expand(jnp.exp(cum), spread)
    ecum_ref[...] = ecum
    z_val = z_ref[...].astype(F32)
    silu = z_val * (1.0 / (1.0 + jnp.exp(-z_val)))
    silu_ref[...] = silu
    esilu_ref[...] = ecum * silu
    skip = expand(jnp.broadcast_to(d_ref[...], (8, heads)), spread)[0:1, :]
    inner = mm(c_ref[...], b_ref[...], 1, 1)
    top, left, right = inner[:HALF, :HALF], inner[HALF:, :HALF], inner[HALF:, HALF:]
    lower = iota((HALF, HALF), 0) >= iota((HALF, HALF), 1)
    first = iota((length, HALF), 1) < P_SIZE
    for q in range(width // HALF):
        cols = slice(HALF * q, HALF * (q + 1))
        x_pair = x_ref[:, cols]
        parts = []
        for h in (2 * q, 2 * q + 1):
            col, row = cum[:, h : h + 1], cum_t[h : h + 1, :]
            up = jnp.where(lower, jnp.exp(col[:HALF] - row[:, :HALF]), 0.0) * top
            dl = jnp.exp(col[HALF:] - row[:, :HALF]) * left
            dr = jnp.where(lower, jnp.exp(col[HALF:] - row[:, HALF:]), 0.0) * right
            down = jnp.concatenate([dl, dr], axis=1)
            parts.append(jnp.concatenate([mm2(up, x_pair[:HALF]), mm2(down, x_pair)], axis=0))
        yn = jnp.where(first, parts[0], parts[1])
        yn_ref[:, cols] = yn
        base_ref[:, cols] = (yn + skip[:, cols] * x_pair.astype(F32)) * silu_ref[:, cols]


def prefix_kernel(in_ref, out_ref, dec_ref):
    count = in_ref.shape[0]
    state = jnp.zeros((8, 512), F32)
    for p in range(count):
        out_ref[p] = state
        if p < count - 1:
            tile = in_ref[p, :, 512:640]
            decay = jnp.concatenate([tile[j : j + 1, :] for j in range(4)], axis=1)
            state = decay * state + in_ref[p, :, 0:512]
    dec_ref[...] = in_ref[:, :, 512:640]


def suffix_kernel(in_ref, dec_ref, skip_ref, out_ref, weight_ref):
    count = in_ref.shape[0]
    state = jnp.zeros((8, 512), F32)
    weight = jnp.zeros((8, HALF), F32)
    for p in range(count - 1, -1, -1):
        out_ref[p, :, 0:512] = state
        out_ref[p, :, 512:640] = skip_ref[...]
        weight = weight + in_ref[p, :, 512:640]
        if p > 0:
            tile = dec_ref[p]
            decay = jnp.concatenate([tile[j : j + 1, :] for j in range(4)], axis=1)
            state = decay * state + in_ref[p, :, 0:512]
    weight_ref[...] = weight


def gate_kernel(s_ref, c_ref, base_ref, esilu_ref, dout_ref, w_ref, gated_ref, cs_ref, sums_ref):
    hi, lo = split2(load_state(s_ref))
    c_val = c_ref[...]
    length, width = base_ref.shape
    squares = jnp.zeros((length, HALF), F32)
    products = jnp.zeros((length, HALF), F32)
    for q in range(width // 256):
        big = slice(256 * q, 256 * (q + 1))
        c_state = mm(c_val, hi[:, big]) + mm(c_val, lo[:, big])
        cs_ref[:, big] = c_state
        gated = base_ref[:, big] + esilu_ref[:, big] * c_state
        gated_ref[:, big] = gated
        sq = gated * gated
        pr = dout_ref[:, big].astype(F32) * w_ref[:, big] * gated
        squares = squares + sq[:, :HALF] + sq[:, HALF:]
        products = products + pr[:, :HALF] + pr[:, HALF:]
    sq_row = jnp.sum(squares.T, axis=0, keepdims=True)
    pr_row = jnp.sum(products.T, axis=0, keepdims=True)
    tile = jnp.concatenate([sq_row, pr_row, jnp.zeros((6, length), F32)], axis=0)
    for i in range(sums_ref.shape[0]):
        sums_ref[i] = tile


def back_kernel(channels, sums_ref, gated_ref, silu_ref, ecum_ref, dout_ref, w_ref, x_ref, c_ref, pay_ref, scal_ref, skip_ref):
    length, width = gated_ref.shape
    total = sums_ref[0]
    for i in range(1, sums_ref.shape[0]):
        total = total + sums_ref[i]
    squares, products = total[0:1, :], total[1:2, :]
    inv = lax.rsqrt(squares / channels + EPS)
    fall = inv * inv * inv * products / channels
    both = jnp.concatenate([inv, fall, jnp.zeros((HALF - 2, length), F32)], axis=0).T
    scal_ref[...] = both
    inv_col, fall_col = both[:, 0:1], both[:, 1:2]
    c_val = c_ref[...]
    weights, skips = [], []
    for q in range(width // 256):
        big = slice(256 * q, 256 * (q + 1))
        gated = gated_ref[:, big]
        d_inv = dout_ref[:, big].astype(F32) * inv_col
        dy = (d_inv * w_ref[:, big] - gated * fall_col) * silu_ref[:, big]
        weights.append(jnp.sum(d_inv * gated, axis=0, keepdims=True))
        skips.append(jnp.sum(dy * x_ref[:, big].astype(F32), axis=0, keepdims=True))
        hi, lo = split2(dy * ecum_ref[:, big])
        back = mm(c_val, hi, 0, 0) + mm(c_val, lo, 0, 0)
        f, off = q // 2, 256 * (q % 2)
        for r in range(16):
            pay_ref[2 * r + f, :, off : off + 256] = back[8 * r : 8 * r + 8, :]
    weight = jnp.concatenate(weights, axis=1)
    tile = jnp.concatenate([weight[:, HALF * j : HALF * (j + 1)] for j in range(8)], axis=0)
    for i in range(pay_ref.shape[0]):
        pay_ref[i, :, 512:640] = tile
    heads = width // P_SIZE
    skip = jnp.broadcast_to(jnp.concatenate(skips, axis=1), (8, width))
    spread = head_map(HALF, width)
    hi, mid, lo = split3(skip)
    skip_ref[...] = mm(hi, spread, 1, 1) + mm(mid, spread, 1, 1) + mm(lo, spread, 1, 1)


def grads_kernel(
    cum_ref, scal_ref, gated_ref, silu_ref, ecum_ref, dout_ref, w_ref, x_ref, z_ref, b_ref, c_ref, d_ref, yn_ref, cs_ref, s_ref,
    gx_ref, gz_ref, gb_ref, gc_ref, gl_ref, dy_ref, dot_ref,
):
    length, heads = cum_ref.shape
    width = x_ref.shape[1]
    spread = head_map(heads, width)
    cum = cum_ref[...]
    cum_t = cum.T
    inv_col, fall_col = scal_ref[:, 0:1], scal_ref[:, 1:2]
    skip = expand(jnp.broadcast_to(d_ref[...], (8, heads)), spread)[0:1, :]
    inner_t = mm(b_ref[...], c_ref[...], 1, 1)
    left, right, low = inner_t[:HALF, :HALF], inner_t[:HALF, HALF:], inner_t[HALF:, HALF:]
    upper = iota((HALF, HALF), 0) <= iota((HALF, HALF), 1)
    first = iota((length, HALF), 1) < P_SIZE
    w_left = jnp.zeros((HALF, HALF), F32)
    w_right = jnp.zeros((HALF, HALF), F32)
    w_low = jnp.zeros((HALF, HALF), F32)
    for q in range(width // HALF):
        cols = slice(HALF * q, HALF * (q + 1))
        gated, silu = gated_ref[:, cols], silu_ref[:, cols]
        d_gated = inv_col * (dout_ref[:, cols].astype(F32) * w_ref[:, cols]) - gated * fall_col
        dy = d_gated * silu
        dy_ref[:, cols] = dy * ecum_ref[:, cols]
        x_pair = x_ref[:, cols]
        x_val = x_pair.astype(F32)
        z_val = z_ref[:, cols].astype(F32)
        sig = 1.0 / (1.0 + jnp.exp(-z_val))
        y_near = yn_ref[:, cols] + ecum_ref[:, cols] * cs_ref[:, cols]
        y_val = y_near + skip[:, cols] * x_val
        gz_ref[:, cols] = (d_gated * y_val * sig * (1.0 + z_val * (1.0 - sig))).astype(BF16)
        hi, lo = split2(dy)
        parts = []
        for k in range(2):
            h = 2 * q + k
            col, row = cum[:, h : h + 1], cum_t[h : h + 1, :]
            x_one = jnp.where(first if k == 0 else ~first, x_val, 0.0).astype(BF16)
            dec_left = jnp.where(upper, jnp.exp(row[:, :HALF] - col[:HALF]), 0.0)
            dec_right = jnp.exp(row[:, HALF:] - col[:HALF])
            dec_low = jnp.where(upper, jnp.exp(row[:, HALF:] - col[HALF:]), 0.0)
            dot_up = mm(x_one[:HALF], hi, 1, 1) + mm(x_one[:HALF], lo, 1, 1)
            dot_low = mm(x_one[HALF:], hi[HALF:], 1, 1) + mm(x_one[HALF:], lo[HALF:], 1, 1)
            w_left = w_left + dec_left * dot_up[:, :HALF]
            w_right = w_right + dec_right * dot_up[:, HALF:]
            w_low = w_low + dec_low * dot_low
            mix_up = jnp.concatenate([dec_left * left, dec_right * right], axis=1)
            mix_low = dec_low * low
            up_hi, up_lo = split2(mix_up)
            low_hi, low_lo = split2(mix_low)
            g_up = mm(up_hi, hi) + mm(up_hi, lo) + mm(up_lo, hi)
            g_low = mm(low_hi, hi[HALF:]) + mm(low_hi, lo[HALF:]) + mm(low_lo, hi[HALF:])
            parts.append(jnp.concatenate([g_up, g_low], axis=0))
        g_near = jnp.where(first, parts[0], parts[1])
        gx_ref[:, cols] = g_near + skip[:, cols] * dy
        dot_ref[:, cols] = dy * y_near - x_val * g_near
    gl_ref[...] = mm_tri(triangle(length, lambda i, j: i <= j), segment(dot_ref[...], spread))
    e_hi, e_lo = split2(dy_ref[...])
    s_hi, s_lo = split2(load_state(s_ref))
    far = mm(e_hi, s_hi, 1, 1) + mm(e_hi, s_lo, 1, 1) + mm(e_lo, s_hi, 1, 1)
    w_up = jnp.concatenate([w_left, w_right], axis=1)
    b_val, c_val = b_ref[...], c_ref[...]
    gb_ref[:HALF, :] = mm2(w_up, c_val)
    gb_ref[HALF:, :] = mm2(w_low, c_val[HALF:])
    low_part = mm2(w_right.T, b_val[:HALF]) + mm2(w_low.T, b_val[HALF:])
    gc_ref[...] = far + jnp.concatenate([mm2(w_left.T, b_val[:HALF]), low_part], axis=0)


def final_kernel(a_ref, s_ref, cum_ref, tail_ref, x_ref, b_ref, gx_ref, gb_ref, gl_ref, ox_ref, ob_ref, ol_ref, skip_ref):
    length, heads = cum_ref.shape
    width = x_ref.shape[1]
    spread = head_map(heads, width)
    after = load_state(a_ref)
    a_hi, a_lo = split2(after)
    b_val = b_ref[...]
    tail = tail_ref[...]
    b_after = (mm(b_val, a_hi) + mm(b_val, a_lo)) * tail
    x_val = x_ref[...].astype(F32)
    ox_ref[...] = (gx_ref[...] + b_after).astype(BF16)
    late = segment(x_val * b_after, spread)
    x_hi, x_lo = split2(x_val * tail)
    ob_ref[...] = gb_ref[...] + (mm(x_hi, a_hi, 1, 1) + mm(x_hi, a_lo, 1, 1) + mm(x_lo, a_hi, 1, 1))
    start = jnp.broadcast_to(jnp.sum(load_state(s_ref) * after, axis=0, keepdims=True), (8, width))
    hi, mid, lo = split3(start)
    start = (mm(hi, spread, 1, 1) + mm(mid, spread, 1, 1) + mm(lo, spread, 1, 1))[0:1, :]
    whole = jnp.exp(cum_ref[length - 1 : length, :])
    ol_ref[...] = gl_ref[...] + mm_tri(triangle(length, lambda i, j: i > j), late) + whole * start
    total = a_ref[0, :, 512:640]
    for i in range(1, a_ref.shape[0]):
        total = total + a_ref[i, :, 512:640]
    skip_ref[...] = total


def call(kernel, name, outs, *args, flops=0, scratch=()):
    nbytes = sum(a.size * a.dtype.itemsize for a in (*args, *outs))
    return pl.pallas_call(
        kernel,
        name=name,
        out_shape=outs,
        in_specs=[VMEM] * len(args),
        out_specs=[VMEM] * len(outs),
        scratch_shapes=list(scratch),
        compiler_params=pltpu.CompilerParams(vmem_limit_bytes=48 * 1024 * 1024),
        cost_estimate=pl.CostEstimate(flops=flops, bytes_accessed=nbytes, transcendentals=0),
    )(*args)


def on_device(x_in, b_in, c_in, decay_log, d_skip, gate, norm_weight, d_out):
    length, heads = decay_log.shape
    width = x_in.shape[1]
    chunks = lax.axis_size(CHUNKS)
    groups = lax.axis_size("heads")
    shape = jax.ShapeDtypeStruct
    wide = shape((length, width), F32)
    small = shape((length, heads), F32)
    weight = norm_weight.reshape(1, width)
    d_row = d_skip.reshape(1, heads)

    pay, cum, tail = call(
        start_kernel, "start", [shape((chunks, 8, 640), F32), small, wide], decay_log, x_in, b_in, flops=10**9
    )
    got = lax.all_to_all(pay, CHUNKS, 0, 0)
    y_near, base, silu, esilu, ecum = call(
        local_kernel, "local", [wide] * 5, cum, x_in, b_in, c_in, gate, d_row, flops=8 * 10**9
    )
    spread, decays = call(
        prefix_kernel, "prefix", [shape((chunks, 8, 512), F32), shape((chunks, 8, HALF), F32)], got
    )
    before = lax.all_to_all(spread, CHUNKS, 0, 0)
    gated, c_state, sums = call(
        gate_kernel, "gated", [wide, wide, shape((groups, 8, length), F32)],
        before, c_in, base, esilu, d_out, weight, flops=10**9,
    )
    sums = lax.all_to_all(sums, "heads", 0, 0)

    def back(*refs):
        back_kernel(float(width * groups), *refs)

    pay, scalars, skip = call(
        back, "back", [shape((chunks, 8, 640), F32), shape((length, HALF), F32), shape((8, HALF), F32)],
        sums, gated, silu, ecum, d_out, weight, x_in, c_in, flops=10**9,
    )
    got = lax.all_to_all(pay, CHUNKS, 0, 0)
    gx, grad_gate, gb, grad_c, gl = call(
        grads_kernel, "grads",
        [wide, shape((length, width), BF16), shape(b_in.shape, F32), shape(c_in.shape, F32), small],
        cum, scalars, gated, silu, ecum, d_out, weight, x_in, gate, b_in, c_in, d_row, y_near, c_state, before,
        flops=16 * 10**9, scratch=[pltpu.VMEM((length, width), F32)] * 2,
    )
    spread, grad_weight = call(
        suffix_kernel, "suffix", [shape((chunks, 8, 640), F32), shape((8, HALF), F32)], got, decays, skip
    )
    after = lax.all_to_all(spread, CHUNKS, 0, 0)
    grad_x, grad_b, grad_decay, grad_skip = call(
        final_kernel, "final",
        [shape((length, width), BF16), shape(b_in.shape, F32), small, shape((8, HALF), F32)],
        after, before, cum, tail, x_in, b_in, gx, gb, gl, flops=2 * 10**9,
    )
    return (
        grad_x,
        grad_b,
        grad_c,
        grad_decay,
        grad_skip[0, :heads],
        grad_gate,
        grad_weight.reshape(width),
    )


def solution(mesh):
    tokens = P(CHUNKS, "heads")
    in_specs = (tokens, tokens, tokens, tokens, P("heads"), tokens, P("heads"), tokens)
    out_specs = (tokens, tokens, tokens, tokens, P("heads"), tokens, P("heads"))
    return jax.shard_map(on_device, mesh=mesh, in_specs=in_specs, out_specs=out_specs, check_vma=False)
```

```python
import jax
import jax.numpy as jnp
from jax import lax
from jax.experimental import pallas as pl
from jax.experimental.pallas import tpu as pltpu
from jax.sharding import PartitionSpec as P

P_SIZE = 64
EPS = 1e-05
F32 = jnp.float32
BF16 = jnp.bfloat16
CHUNKS = ("outer", "inner")
VMEM = pl.BlockSpec(memory_space=pltpu.VMEM)
HBM = pl.BlockSpec(memory_space=pltpu.HBM)
HALF = 128


def mm(a, b, ca=1, cb=0):
    return lax.dot_general(a, b, (((ca,), (cb,)), ((), ())), preferred_element_type=F32)


def split2(a):
    hi = a.astype(BF16)
    return hi, (a - hi.astype(F32)).astype(BF16)


def split3(a):
    hi = a.astype(BF16)
    rest = a - hi.astype(F32)
    mid = rest.astype(BF16)
    return hi, mid, (rest - mid.astype(F32)).astype(BF16)


def mm2(a, b, ca=1, cb=0):
    hi, lo = split2(a)
    return mm(hi, b, ca, cb) + mm(lo, b, ca, cb)


def iota(shape, dim):
    return lax.broadcasted_iota(jnp.int32, shape, dim)


def head_map(heads, width):
    return jnp.where(iota((heads, width), 1) // P_SIZE == iota((heads, width), 0), 1.0, 0.0).astype(BF16)


def expand(a, spread, ca=1):
    hi, mid, lo = split3(a)
    return mm(hi, spread, ca) + mm(mid, spread, ca) + mm(lo, spread, ca)


def segment(a, spread):
    hi, lo = split2(a)
    return mm(spread, hi, 1, 1) + mm(spread, lo, 1, 1)


def triangle(n, keep):
    return jnp.where(keep(iota((n, n), 0), iota((n, n), 1)), 1.0, 0.0).astype(BF16)


def mm_by(a, tri):
    hi, mid, lo = split3(a)
    return mm(hi, tri) + mm(mid, tri) + mm(lo, tri)


def store_state(out_ref, state, rows):
    for q in range(state.shape[1] // HALF):
        for r in range(4):
            at = rows * (4 * q + r)
            out_ref[at : at + 32, :] = state[32 * r : 32 * r + 32, HALF * q : HALF * (q + 1)]


def load_state(ref, rows):
    cols = []
    for q in range(8):
        at = [rows * (4 * q + r) for r in range(4)]
        cols.append(jnp.concatenate([ref[i : i + 32, :] for i in at], axis=0))
    return jnp.concatenate(cols, axis=1)


def start_kernel(lt_ref, x_hbm, b_ref, pay_ref, cum_ref, tail_ref, x_ref, sems):
    heads, length = lt_ref.shape
    width = x_hbm.shape[1]
    copies = []
    for k in range(4):
        cols = pl.ds(256 * k, 256)
        copies.append(pltpu.make_async_copy(x_hbm.at[:, cols], x_ref.at[:, cols], sems.at[k]))
        copies[-1].start()
    spread = head_map(heads, width)
    cum = mm_by(lt_ref[...], triangle(length, lambda i, j: i <= j))
    cum_ref[...] = cum
    last = cum[:, length - 1 : length]
    tail = expand(jnp.exp(last - cum), spread, 0)
    tail_ref[...] = tail
    whole = expand(jnp.broadcast_to(jnp.exp(last), (heads, HALF)), spread, 0)[0:1, :]
    b_val = b_ref[...]
    for k in range(4):
        copies[k].wait()
        big = slice(256 * k, 256 * (k + 1))
        hi, lo = split2(x_ref[:, big].astype(F32) * tail[:, big])
        state = mm(b_val, hi, 0, 0) + mm(b_val, lo, 0, 0)
        for q in (2 * k, 2 * k + 1):
            for r in range(4):
                at = 33 * (4 * q + r)
                off = HALF * (q - 2 * k)
                pay_ref[at : at + 32, :] = state[32 * r : 32 * r + 32, off : off + HALF]
                pay_ref[at + 32 : at + 33, :] = whole[:, HALF * q : HALF * (q + 1)]


def local_kernel(cum_ref, x_ref, b_ref, c_ref, z_ref, d_ref, yn_ref, base_ref, silu_ref, esilu_ref, ecum_ref):
    heads, length = cum_ref.shape
    width = x_ref.shape[1]
    spread = head_map(heads, width)
    cum_t = cum_ref[...]
    cum = cum_t.T
    ecum = expand(jnp.exp(cum_t), spread, 0)
    ecum_ref[...] = ecum
    z_val = z_ref[...].astype(F32)
    silu = z_val * (1.0 / (1.0 + jnp.exp(-z_val)))
    silu_ref[...] = silu
    esilu_ref[...] = ecum * silu
    skip = expand(jnp.broadcast_to(d_ref[...], (8, heads)), spread)[0:1, :]
    inner = mm(c_ref[...], b_ref[...], 1, 1)
    top, left, right = inner[:HALF, :HALF], inner[HALF:, :HALF], inner[HALF:, HALF:]
    lower = iota((HALF, HALF), 0) >= iota((HALF, HALF), 1)
    first = iota((length, HALF), 1) < P_SIZE
    for q in range(width // HALF):
        cols = slice(HALF * q, HALF * (q + 1))
        x_pair = x_ref[:, cols]
        parts = []
        for h in (2 * q, 2 * q + 1):
            col, row = cum[:, h : h + 1], cum_t[h : h + 1, :]
            up = jnp.where(lower, jnp.exp(col[:HALF] - row[:, :HALF]), 0.0) * top
            dl = jnp.exp(col[HALF:] - row[:, :HALF]) * left
            dr = jnp.where(lower, jnp.exp(col[HALF:] - row[:, HALF:]), 0.0) * right
            down = jnp.concatenate([dl, dr], axis=1)
            parts.append(jnp.concatenate([mm2(up, x_pair[:HALF]), mm2(down, x_pair)], axis=0))
        yn = jnp.where(first, parts[0], parts[1])
        yn_ref[:, cols] = yn
        base_ref[:, cols] = (yn + skip[:, cols] * x_pair.astype(F32)) * silu_ref[:, cols]


def prefix_kernel(in_ref, out_ref, dec_ref):
    count = dec_ref.shape[0]
    state = jnp.zeros((32, HALF), F32)
    for p in range(count):
        out_ref[32 * p : 32 * p + 32, :] = state
        decay = in_ref[33 * p + 32 : 33 * p + 33, :]
        dec_ref[p : p + 1, :] = decay
        if p < count - 1:
            state = decay * state + in_ref[33 * p : 33 * p + 32, :]


def suffix_kernel(in_ref, dec_ref, out_ref):
    count = dec_ref.shape[0]
    state = jnp.zeros((32, HALF), F32)
    sums = in_ref[32:34, :]
    for p in range(1, count):
        sums = sums + in_ref[34 * p + 32 : 34 * p + 34, :]
    for p in range(count - 1, -1, -1):
        out_ref[34 * p : 34 * p + 32, :] = state
        out_ref[34 * p + 32 : 34 * p + 34, :] = sums
        if p > 0:
            state = dec_ref[p : p + 1, :] * state + in_ref[34 * p : 34 * p + 32, :]


def gate_kernel(s_ref, c_ref, base_ref, esilu_ref, dout_ref, w_ref, gated_ref, cs_ref, sums_ref):
    hi, lo = split2(load_state(s_ref, 32))
    c_val = c_ref[...]
    length, width = base_ref.shape
    squares = jnp.zeros((length, HALF), F32)
    products = jnp.zeros((length, HALF), F32)
    for q in range(width // 256):
        big = slice(256 * q, 256 * (q + 1))
        c_state = mm(c_val, hi[:, big]) + mm(c_val, lo[:, big])
        cs_ref[:, big] = c_state
        gated = base_ref[:, big] + esilu_ref[:, big] * c_state
        gated_ref[:, big] = gated
        sq = gated * gated
        pr = dout_ref[:, big].astype(F32) * w_ref[:, big] * gated
        squares = squares + sq[:, :HALF] + sq[:, HALF:]
        products = products + pr[:, :HALF] + pr[:, HALF:]
    sq_row = jnp.sum(squares.T, axis=0, keepdims=True)
    pr_row = jnp.sum(products.T, axis=0, keepdims=True)
    tile = jnp.concatenate([sq_row, pr_row, jnp.zeros((6, length), F32)], axis=0)
    for i in range(sums_ref.shape[0]):
        sums_ref[i] = tile


def back_kernel(channels, sums_ref, gated_ref, silu_ref, ecum_ref, dout_ref, w_ref, x_ref, c_ref, pay_ref, scal_ref):
    length, width = gated_ref.shape
    total = sums_ref[0]
    for i in range(1, sums_ref.shape[0]):
        total = total + sums_ref[i]
    squares, products = total[0:1, :], total[1:2, :]
    inv = lax.rsqrt(squares / channels + EPS)
    fall = inv * inv * inv * products / channels
    both = jnp.concatenate([inv, fall, jnp.zeros((HALF - 2, length), F32)], axis=0).T
    scal_ref[...] = both
    inv_col, fall_col = both[:, 0:1], both[:, 1:2]
    c_val = c_ref[...]
    for k in range(width // 256):
        big = slice(256 * k, 256 * (k + 1))
        gated = gated_ref[:, big]
        d_inv = dout_ref[:, big].astype(F32) * inv_col
        dy = (d_inv * w_ref[:, big] - gated * fall_col) * silu_ref[:, big]
        weight = jnp.sum(d_inv * gated, axis=0, keepdims=True)
        skip = jnp.sum(dy * x_ref[:, big].astype(F32), axis=0, keepdims=True)
        hi, lo = split2(dy * ecum_ref[:, big])
        back = mm(c_val, hi, 0, 0) + mm(c_val, lo, 0, 0)
        for q in (2 * k, 2 * k + 1):
            off = HALF * (q - 2 * k)
            for r in range(4):
                at = 34 * (4 * q + r)
                pay_ref[at : at + 32, :] = back[32 * r : 32 * r + 32, off : off + HALF]
                pay_ref[at + 32 : at + 33, :] = weight[:, off : off + HALF]
                pay_ref[at + 33 : at + 34, :] = skip[:, off : off + HALF]


def grads_kernel(
    cum_ref, scal_ref, gated_ref, silu_ref, ecum_ref, dout_ref, w_ref, x_ref, z_ref, b_ref, c_ref, d_ref, yn_ref, cs_ref, s_ref,
    gx_ref, gz_ref, gb_ref, gc_ref, gl_ref, dy_ref, dot_ref,
):
    heads, length = cum_ref.shape
    width = x_ref.shape[1]
    spread = head_map(heads, width)
    cum_t = cum_ref[...]
    cum = cum_t.T
    inv_col, fall_col = scal_ref[:, 0:1], scal_ref[:, 1:2]
    skip = expand(jnp.broadcast_to(d_ref[...], (8, heads)), spread)[0:1, :]
    inner_t = mm(b_ref[...], c_ref[...], 1, 1)
    left, right, low = inner_t[:HALF, :HALF], inner_t[:HALF, HALF:], inner_t[HALF:, HALF:]
    upper = iota((HALF, HALF), 0) <= iota((HALF, HALF), 1)
    first = iota((length, HALF), 1) < P_SIZE
    w_left = jnp.zeros((HALF, HALF), F32)
    w_right = jnp.zeros((HALF, HALF), F32)
    w_low = jnp.zeros((HALF, HALF), F32)
    for q in range(width // HALF):
        cols = slice(HALF * q, HALF * (q + 1))
        gated, silu = gated_ref[:, cols], silu_ref[:, cols]
        d_gated = inv_col * (dout_ref[:, cols].astype(F32) * w_ref[:, cols]) - gated * fall_col
        dy = d_gated * silu
        dy_ref[:, cols] = dy * ecum_ref[:, cols]
        x_pair = x_ref[:, cols]
        x_val = x_pair.astype(F32)
        z_val = z_ref[:, cols].astype(F32)
        sig = 1.0 / (1.0 + jnp.exp(-z_val))
        y_near = yn_ref[:, cols] + ecum_ref[:, cols] * cs_ref[:, cols]
        y_val = y_near + skip[:, cols] * x_val
        gz_ref[:, cols] = (d_gated * y_val * sig * (1.0 + z_val * (1.0 - sig))).astype(BF16)
        hi, lo = split2(dy)
        parts = []
        for k in range(2):
            h = 2 * q + k
            col, row = cum[:, h : h + 1], cum_t[h : h + 1, :]
            x_one = jnp.where(first if k == 0 else ~first, x_val, 0.0).astype(BF16)
            dec_left = jnp.where(upper, jnp.exp(row[:, :HALF] - col[:HALF]), 0.0)
            dec_right = jnp.exp(row[:, HALF:] - col[:HALF])
            dec_low = jnp.where(upper, jnp.exp(row[:, HALF:] - col[HALF:]), 0.0)
            dot_up = mm(x_one[:HALF], hi, 1, 1) + mm(x_one[:HALF], lo, 1, 1)
            dot_low = mm(x_one[HALF:], hi[HALF:], 1, 1) + mm(x_one[HALF:], lo[HALF:], 1, 1)
            w_left = w_left + dec_left * dot_up[:, :HALF]
            w_right = w_right + dec_right * dot_up[:, HALF:]
            w_low = w_low + dec_low * dot_low
            mix_up = jnp.concatenate([dec_left * left, dec_right * right], axis=1)
            mix_low = dec_low * low
            up_hi, up_lo = split2(mix_up)
            low_hi, low_lo = split2(mix_low)
            g_up = mm(up_hi, hi) + mm(up_hi, lo) + mm(up_lo, hi)
            g_low = mm(low_hi, hi[HALF:]) + mm(low_hi, lo[HALF:]) + mm(low_lo, hi[HALF:])
            parts.append(jnp.concatenate([g_up, g_low], axis=0))
        g_near = jnp.where(first, parts[0], parts[1])
        gx_ref[:, cols] = g_near + skip[:, cols] * dy
        dot_ref[:, cols] = dy * y_near - x_val * g_near
    gl_ref[...] = mm_by(segment(dot_ref[...], spread), triangle(length, lambda i, j: i >= j))
    e_hi, e_lo = split2(dy_ref[...])
    s_hi, s_lo = split2(load_state(s_ref, 32))
    far = mm(e_hi, s_hi, 1, 1) + mm(e_hi, s_lo, 1, 1) + mm(e_lo, s_hi, 1, 1)
    w_up = jnp.concatenate([w_left, w_right], axis=1)
    b_val, c_val = b_ref[...], c_ref[...]
    gb_ref[:HALF, :] = mm2(w_up, c_val)
    gb_ref[HALF:, :] = mm2(w_low, c_val[HALF:])
    low_part = mm2(w_right.T, b_val[:HALF]) + mm2(w_low.T, b_val[HALF:])
    gc_ref[...] = far + jnp.concatenate([mm2(w_left.T, b_val[:HALF]), low_part], axis=0)


def final_kernel(
    a_ref, s_ref, cum_ref, tail_ref, x_ref, b_ref, gx_ref, gb_ref, gl_ref,
    ox_hbm, ob_ref, ol_ref, skip_ref, weight_ref, ox_ref, sems,
):
    heads, length = cum_ref.shape
    width = x_ref.shape[1]
    spread = head_map(heads, width)
    after = load_state(a_ref, 34)
    a_hi, a_lo = split2(after)
    b_val = b_ref[...]
    copies = []
    late = jnp.zeros((heads, length), F32)
    far = jnp.zeros(ob_ref.shape, F32)
    for k in range(width // 256):
        big = slice(256 * k, 256 * (k + 1))
        tail, x_val = tail_ref[:, big], x_ref[:, big].astype(F32)
        one_hi, one_lo = a_hi[:, big], a_lo[:, big]
        b_after = (mm(b_val, one_hi) + mm(b_val, one_lo)) * tail
        ox_ref[:, big] = (gx_ref[:, big] + b_after).astype(BF16)
        cols = pl.ds(256 * k, 256)
        copies.append(pltpu.make_async_copy(ox_ref.at[:, cols], ox_hbm.at[:, cols], sems.at[k]))
        copies[-1].start()
        late = late + segment(x_val * b_after, spread[:, big])
        x_hi, x_lo = split2(x_val * tail)
        far = far + (mm(x_hi, one_hi, 1, 1) + mm(x_hi, one_lo, 1, 1) + mm(x_lo, one_hi, 1, 1))
    ob_ref[...] = gb_ref[...] + far
    start = jnp.broadcast_to(jnp.sum(load_state(s_ref, 32) * after, axis=0, keepdims=True), (HALF, width))
    hi, mid, lo = split3(start)
    start = (mm(spread, hi, 1, 1) + mm(spread, mid, 1, 1) + mm(spread, lo, 1, 1))[:, 0:1]
    whole = jnp.exp(cum_ref[:, length - 1 : length])
    ol_ref[...] = gl_ref[...] + mm_by(late, triangle(length, lambda i, j: i < j)) + whole * start
    sums = [a_ref[34 * 4 * q + 32 : 34 * 4 * q + 34, :] for q in range(8)]
    weight_ref[...] = jnp.concatenate([one[0:1, :] for one in sums], axis=0)
    skip = jnp.concatenate([one[1:2, :] for one in sums], axis=0)
    halves = jnp.where(iota((HALF, heads), 0) // P_SIZE == iota((HALF, heads), 1) % 2, 1.0, 0.0).astype(BF16)
    skip = mm_by(skip, halves)
    skip = jnp.where(iota((8, heads), 1) // 2 == iota((8, heads), 0), skip, 0.0)
    skip_ref[...] = jnp.sum(skip, axis=0, keepdims=True)
    for copy in copies:
        copy.wait()


def call(kernel, name, outs, *args, flops=0, scratch=(), hbm_in=(), hbm_out=(), mib=16):
    nbytes = sum(a.size * a.dtype.itemsize for a in (*args, *outs))
    return pl.pallas_call(
        kernel,
        name=name,
        out_shape=outs,
        in_specs=[HBM if i in hbm_in else VMEM for i in range(len(args))],
        out_specs=[HBM if i in hbm_out else VMEM for i in range(len(outs))],
        scratch_shapes=list(scratch),
        compiler_params=pltpu.CompilerParams(vmem_limit_bytes=mib * 1024 * 1024),
        cost_estimate=pl.CostEstimate(flops=flops, bytes_accessed=nbytes, transcendentals=0),
    )(*args)


def exchange(messages, rows):
    count = lax.axis_size(CHUNKS)
    got = lax.all_to_all(messages.reshape(count, 1, rows * HALF), CHUNKS, 0, 0)
    return got.reshape(count * rows, HALF)


def on_device(x_in, b_in, c_in, decay_log, d_skip, gate, norm_weight, d_out):
    length, heads = decay_log.shape
    width = x_in.shape[1]
    chunks = lax.axis_size(CHUNKS)
    groups = lax.axis_size("heads")
    shape = jax.ShapeDtypeStruct
    wide = shape((length, width), F32)
    half_wide = shape((length, width), BF16)
    small = shape((heads, length), F32)
    weight = norm_weight.reshape(1, width)
    d_row = d_skip.reshape(1, heads)
    pieces = [pltpu.VMEM((length, width), BF16), pltpu.SemaphoreType.DMA((4,))]

    pay, cum, tail = call(
        start_kernel, "start", [shape((chunks * 33, HALF), F32), small, wide], decay_log.T, x_in, b_in,
        flops=10**9, scratch=pieces, hbm_in=(1,),
    )
    got = exchange(pay, 33)
    y_near, base, silu, esilu, ecum = call(
        local_kernel, "local", [wide] * 5, cum, x_in, b_in, c_in, gate, d_row, flops=8 * 10**9, mib=24
    )
    spread, decays = call(
        prefix_kernel, "prefix", [shape((chunks * 32, HALF), F32), shape((chunks, HALF), F32)], got
    )
    before = exchange(spread, 32)
    gated, c_state, sums = call(
        gate_kernel, "gated", [wide, wide, shape((groups, 8, length), F32)],
        before, c_in, base, esilu, d_out, weight, flops=10**9,
    )
    sums = lax.all_to_all(sums, "heads", 0, 0)

    def back(*refs):
        back_kernel(float(width * groups), *refs)

    pay, scalars = call(
        back, "back", [shape((chunks * 34, HALF), F32), shape((length, HALF), F32)],
        sums, gated, silu, ecum, d_out, weight, x_in, c_in, flops=10**9,
    )
    got = exchange(pay, 34)
    gx, grad_gate, gb, grad_c, gl = call(
        grads_kernel, "grads",
        [wide, half_wide, shape(b_in.shape, F32), shape(c_in.shape, F32), small],
        cum, scalars, gated, silu, ecum, d_out, weight, x_in, gate, b_in, c_in, d_row, y_near, c_state, before,
        flops=16 * 10**9, scratch=[pltpu.VMEM((length, width), F32)] * 2, mib=28,
    )
    (spread,) = call(suffix_kernel, "suffix", [shape((chunks * 34, HALF), F32)], got, decays)
    after = exchange(spread, 34)
    grad_x, grad_b, grad_decay, grad_skip, grad_weight = call(
        final_kernel, "final",
        [half_wide, shape(b_in.shape, F32), small, shape((1, heads), F32), shape((8, HALF), F32)],
        after, before, cum, tail, x_in, b_in, gx, gb, gl, flops=2 * 10**9, scratch=pieces, hbm_out=(0,),
    )
    return (
        grad_x,
        grad_b,
        grad_c,
        grad_decay.T,
        grad_skip.reshape(heads),
        grad_gate,
        grad_weight.reshape(width),
    )


def solution(mesh):
    tokens = P(CHUNKS, "heads")
    in_specs = (tokens, tokens, tokens, tokens, P("heads"), tokens, P("heads"), tokens)
    out_specs = (tokens, tokens, tokens, tokens, P("heads"), tokens, P("heads"))
    return jax.shard_map(on_device, mesh=mesh, in_specs=in_specs, out_specs=out_specs, check_vma=False)
```

```python
import jax
import jax.numpy as jnp
from jax import lax
from jax.experimental import pallas as pl
from jax.experimental.pallas import tpu as pltpu
from jax.sharding import PartitionSpec as P

P_SIZE = 64
EPS = 1e-05
F32 = jnp.float32
BF16 = jnp.bfloat16
CHUNKS = ("outer", "inner")
HALF = 128


def mm(a, b, ca=1, cb=0):
    return lax.dot_general(a, b, (((ca,), (cb,)), ((), ())), preferred_element_type=F32)


def split2(a):
    hi = a.astype(BF16)
    return hi, (a - hi.astype(F32)).astype(BF16)


def split3(a):
    hi = a.astype(BF16)
    rest = a - hi.astype(F32)
    mid = rest.astype(BF16)
    return hi, mid, (rest - mid.astype(F32)).astype(BF16)


def mm2(a, b, ca=1, cb=0):
    hi, lo = split2(a)
    return mm(hi, b, ca, cb) + mm(lo, b, ca, cb)


def iota(shape, dim):
    return lax.broadcasted_iota(jnp.int32, shape, dim)


def head_map(heads, width):
    return jnp.where(iota((heads, width), 1) // P_SIZE == iota((heads, width), 0), 1.0, 0.0).astype(BF16)


def expand(a, spread, ca=1):
    hi, mid, lo = split3(a)
    return mm(hi, spread, ca) + mm(mid, spread, ca) + mm(lo, spread, ca)


def segment(a, spread):
    hi, lo = split2(a)
    return mm(spread, hi, 1, 1) + mm(spread, lo, 1, 1)


def triangle(n, keep):
    return jnp.where(keep(iota((n, n), 0), iota((n, n), 1)), 1.0, 0.0).astype(BF16)


def mm_by(a, tri):
    hi, mid, lo = split3(a)
    return mm(hi, tri) + mm(mid, tri) + mm(lo, tri)


def load_block(ref, rows, k):
    cols = []
    for q in (2 * k, 2 * k + 1):
        at = [rows * (4 * q + r) for r in range(4)]
        cols.append(jnp.concatenate([ref[i : i + 32, :] for i in at], axis=0))
    return jnp.concatenate(cols, axis=1)


def load_state(ref, rows):
    return jnp.concatenate([load_block(ref, rows, k) for k in range(4)], axis=1)


def fetch(pairs, sems):
    copies = [pltpu.make_async_copy(src, dst, sems.at[i]) for i, (src, dst) in enumerate(pairs)]
    for copy in copies:
        copy.start()
    return copies


def quarters(ref):
    return [ref.at[:, pl.ds(256 * k, 256)] for k in range(4)]


def start_kernel(lt_hbm, x_hbm, b_hbm, pay_ref, cum_ref, tail_ref, x_ref, b_ref, lt_ref, sems):
    heads, length = lt_hbm.shape
    width = x_hbm.shape[1]
    pairs = [(lt_hbm, lt_ref), (b_hbm, b_ref)] + list(zip(quarters(x_hbm), quarters(x_ref)))
    first, second, *copies = fetch(pairs, sems)
    first.wait()
    spread = head_map(heads, width)
    cum = mm_by(lt_ref[...], triangle(length, lambda i, j: i <= j))
    cum_ref[...] = cum
    last = cum[:, length - 1 : length]
    tail = expand(jnp.exp(last - cum), spread, 0)
    tail_ref[...] = tail
    whole = expand(jnp.broadcast_to(jnp.exp(last), (heads, HALF)), spread, 0)[0:1, :]
    second.wait()
    b_val = b_ref[...]
    for k in range(4):
        copies[k].wait()
        big = slice(256 * k, 256 * (k + 1))
        hi, lo = split2(x_ref[:, big].astype(F32) * tail[:, big])
        state = mm(b_val, hi, 0, 0) + mm(b_val, lo, 0, 0)
        for q in (2 * k, 2 * k + 1):
            for r in range(4):
                at = 33 * (4 * q + r)
                off = HALF * (q - 2 * k)
                pay_ref[at : at + 32, :] = state[32 * r : 32 * r + 32, off : off + HALF]
                pay_ref[at + 32 : at + 33, :] = whole[:, HALF * q : HALF * (q + 1)]


def local_kernel(
    cum_ref, x_ref, b_ref, c_hbm, z_hbm, d_hbm, w_hbm, dout_hbm,
    yn_ref, base_ref, silu_ref, esilu_ref, ecum_ref, c_ref, z_ref, d_ref, w_ref, dout_ref, sems,
):
    copies = fetch([(c_hbm, c_ref), (z_hbm, z_ref), (d_hbm, d_ref), (w_hbm, w_ref), (dout_hbm, dout_ref)], sems)
    for copy in copies:
        copy.wait()
    heads, length = cum_ref.shape
    width = x_ref.shape[1]
    spread = head_map(heads, width)
    cum_t = cum_ref[...]
    cum = cum_t.T
    ecum = expand(jnp.exp(cum_t), spread, 0)
    ecum_ref[...] = ecum
    z_val = z_ref[...].astype(F32)
    silu = z_val * (1.0 / (1.0 + jnp.exp(-z_val)))
    silu_ref[...] = silu
    esilu_ref[...] = ecum * silu
    skip = expand(jnp.broadcast_to(d_ref[...], (8, heads)), spread)[0:1, :]
    inner = mm(c_ref[...], b_ref[...], 1, 1)
    top, left, right = inner[:HALF, :HALF], inner[HALF:, :HALF], inner[HALF:, HALF:]
    lower = iota((HALF, HALF), 0) >= iota((HALF, HALF), 1)
    first = iota((length, HALF), 1) < P_SIZE
    for q in range(width // HALF):
        cols = slice(HALF * q, HALF * (q + 1))
        x_pair = x_ref[:, cols]
        parts = []
        for h in (2 * q, 2 * q + 1):
            col, row = cum[:, h : h + 1], cum_t[h : h + 1, :]
            up = jnp.where(lower, jnp.exp(col[:HALF] - row[:, :HALF]), 0.0) * top
            dl = jnp.exp(col[HALF:] - row[:, :HALF]) * left
            dr = jnp.where(lower, jnp.exp(col[HALF:] - row[:, HALF:]), 0.0) * right
            down = jnp.concatenate([dl, dr], axis=1)
            parts.append(jnp.concatenate([mm2(up, x_pair[:HALF]), mm2(down, x_pair)], axis=0))
        yn = jnp.where(first, parts[0], parts[1])
        yn_ref[:, cols] = yn
        base_ref[:, cols] = (yn + skip[:, cols] * x_pair.astype(F32)) * silu_ref[:, cols]


def prefix_kernel(in_ref, out_ref, dec_ref):
    count = dec_ref.shape[0]
    state = jnp.zeros((32, HALF), F32)
    for p in range(count):
        out_ref[32 * p : 32 * p + 32, :] = state
        decay = in_ref[33 * p + 32 : 33 * p + 33, :]
        dec_ref[p : p + 1, :] = decay
        if p < count - 1:
            state = decay * state + in_ref[33 * p : 33 * p + 32, :]


def suffix_kernel(in_ref, dec_ref, out_ref):
    count = dec_ref.shape[0]
    state = jnp.zeros((32, HALF), F32)
    sums = in_ref[32:34, :]
    for p in range(1, count):
        sums = sums + in_ref[34 * p + 32 : 34 * p + 34, :]
    for p in range(count - 1, -1, -1):
        out_ref[34 * p : 34 * p + 32, :] = state
        out_ref[34 * p + 32 : 34 * p + 34, :] = sums
        if p > 0:
            state = dec_ref[p : p + 1, :] * state + in_ref[34 * p : 34 * p + 32, :]


def gate_kernel(s_ref, c_ref, base_ref, esilu_ref, dout_ref, w_ref, gated_ref, cs_ref, sums_ref):
    c_val = c_ref[...]
    length, width = base_ref.shape
    squares = jnp.zeros((length, HALF), F32)
    products = jnp.zeros((length, HALF), F32)
    for q in range(width // 256):
        big = slice(256 * q, 256 * (q + 1))
        hi, lo = split2(load_block(s_ref, 32, q))
        c_state = mm(c_val, hi) + mm(c_val, lo)
        cs_ref[:, big] = c_state
        gated = base_ref[:, big] + esilu_ref[:, big] * c_state
        gated_ref[:, big] = gated
        sq = gated * gated
        pr = dout_ref[:, big].astype(F32) * w_ref[:, big] * gated
        squares = squares + sq[:, :HALF] + sq[:, HALF:]
        products = products + pr[:, :HALF] + pr[:, HALF:]
    sq_row = jnp.sum(squares.T, axis=0, keepdims=True)
    pr_row = jnp.sum(products.T, axis=0, keepdims=True)
    tile = jnp.concatenate([sq_row, pr_row, jnp.zeros((6, length), F32)], axis=0)
    for i in range(sums_ref.shape[0]):
        sums_ref[i] = tile


def back_kernel(channels, sums_ref, gated_ref, silu_ref, ecum_ref, dout_ref, w_ref, x_ref, c_ref, pay_ref, scal_ref):
    length, width = gated_ref.shape
    total = sums_ref[0]
    for i in range(1, sums_ref.shape[0]):
        total = total + sums_ref[i]
    squares, products = total[0:1, :], total[1:2, :]
    inv = lax.rsqrt(squares / channels + EPS)
    fall = inv * inv * inv * products / channels
    both = jnp.concatenate([inv, fall, jnp.zeros((HALF - 2, length), F32)], axis=0).T
    scal_ref[...] = both
    inv_col, fall_col = both[:, 0:1], both[:, 1:2]
    c_val = c_ref[...]
    for k in range(width // 256):
        big = slice(256 * k, 256 * (k + 1))
        gated = gated_ref[:, big]
        d_inv = dout_ref[:, big].astype(F32) * inv_col
        dy = (d_inv * w_ref[:, big] - gated * fall_col) * silu_ref[:, big]
        weight = jnp.sum(d_inv * gated, axis=0, keepdims=True)
        skip = jnp.sum(dy * x_ref[:, big].astype(F32), axis=0, keepdims=True)
        hi, lo = split2(dy * ecum_ref[:, big])
        back = mm(c_val, hi, 0, 0) + mm(c_val, lo, 0, 0)
        for q in (2 * k, 2 * k + 1):
            off = HALF * (q - 2 * k)
            for r in range(4):
                at = 34 * (4 * q + r)
                pay_ref[at : at + 32, :] = back[32 * r : 32 * r + 32, off : off + HALF]
                pay_ref[at + 32 : at + 33, :] = weight[:, off : off + HALF]
                pay_ref[at + 33 : at + 34, :] = skip[:, off : off + HALF]


def grads_kernel(
    cum_ref, scal_ref, gated_ref, silu_ref, ecum_ref, dout_ref, w_ref, x_ref, z_ref, b_ref, c_ref, d_ref, yn_ref, cs_ref, s_ref,
    gx_ref, gz_hbm, gb_ref, gc_hbm, gl_ref, dy_ref, dot_ref, gz_ref, gc_ref, sems,
):
    heads, length = cum_ref.shape
    width = x_ref.shape[1]
    spread = head_map(heads, width)
    cum_t = cum_ref[...]
    cum = cum_t.T
    inv_col, fall_col = scal_ref[:, 0:1], scal_ref[:, 1:2]
    skip = expand(jnp.broadcast_to(d_ref[...], (8, heads)), spread)[0:1, :]
    inner_t = mm(b_ref[...], c_ref[...], 1, 1)
    left, right, low = inner_t[:HALF, :HALF], inner_t[:HALF, HALF:], inner_t[HALF:, HALF:]
    upper = iota((HALF, HALF), 0) <= iota((HALF, HALF), 1)
    first = iota((length, HALF), 1) < P_SIZE
    w_left = jnp.zeros((HALF, HALF), F32)
    w_right = jnp.zeros((HALF, HALF), F32)
    w_low = jnp.zeros((HALF, HALF), F32)
    for q in range(width // HALF):
        cols = slice(HALF * q, HALF * (q + 1))
        gated, silu = gated_ref[:, cols], silu_ref[:, cols]
        d_gated = inv_col * (dout_ref[:, cols].astype(F32) * w_ref[:, cols]) - gated * fall_col
        dy = d_gated * silu
        dy_ref[:, cols] = dy * ecum_ref[:, cols]
        x_pair = x_ref[:, cols]
        x_val = x_pair.astype(F32)
        z_val = z_ref[:, cols].astype(F32)
        sig = 1.0 / (1.0 + jnp.exp(-z_val))
        y_near = yn_ref[:, cols] + ecum_ref[:, cols] * cs_ref[:, cols]
        y_val = y_near + skip[:, cols] * x_val
        gz_ref[:, cols] = (d_gated * y_val * sig * (1.0 + z_val * (1.0 - sig))).astype(BF16)
        hi, lo = split2(dy)
        parts = []
        for k in range(2):
            h = 2 * q + k
            col, row = cum[:, h : h + 1], cum_t[h : h + 1, :]
            x_one = jnp.where(first if k == 0 else ~first, x_val, 0.0).astype(BF16)
            dec_left = jnp.where(upper, jnp.exp(row[:, :HALF] - col[:HALF]), 0.0)
            dec_right = jnp.exp(row[:, HALF:] - col[:HALF])
            dec_low = jnp.where(upper, jnp.exp(row[:, HALF:] - col[HALF:]), 0.0)
            dot_up = mm(x_one[:HALF], hi, 1, 1) + mm(x_one[:HALF], lo, 1, 1)
            dot_low = mm(x_one[HALF:], hi[HALF:], 1, 1) + mm(x_one[HALF:], lo[HALF:], 1, 1)
            w_left = w_left + dec_left * dot_up[:, :HALF]
            w_right = w_right + dec_right * dot_up[:, HALF:]
            w_low = w_low + dec_low * dot_low
            mix_up = jnp.concatenate([dec_left * left, dec_right * right], axis=1)
            mix_low = dec_low * low
            up_hi, up_lo = split2(mix_up)
            low_hi, low_lo = split2(mix_low)
            g_up = mm(up_hi, hi) + mm(up_hi, lo) + mm(up_lo, hi)
            g_low = mm(low_hi, hi[HALF:]) + mm(low_hi, lo[HALF:]) + mm(low_lo, hi[HALF:])
            parts.append(jnp.concatenate([g_up, g_low], axis=0))
        g_near = jnp.where(first, parts[0], parts[1])
        gx_ref[:, cols] = g_near + skip[:, cols] * dy
        dot_ref[:, cols] = dy * y_near - x_val * g_near
    gl_ref[...] = mm_by(segment(dot_ref[...], spread), triangle(length, lambda i, j: i >= j))
    e_hi, e_lo = split2(dy_ref[...])
    s_hi, s_lo = split2(load_state(s_ref, 32))
    far = mm(e_hi, s_hi, 1, 1) + mm(e_hi, s_lo, 1, 1) + mm(e_lo, s_hi, 1, 1)
    w_up = jnp.concatenate([w_left, w_right], axis=1)
    b_val, c_val = b_ref[...], c_ref[...]
    gb_ref[:HALF, :] = mm2(w_up, c_val)
    gb_ref[HALF:, :] = mm2(w_low, c_val[HALF:])
    low_part = mm2(w_right.T, b_val[:HALF]) + mm2(w_low.T, b_val[HALF:])
    gc_ref[...] = far + jnp.concatenate([mm2(w_left.T, b_val[:HALF]), low_part], axis=0)
    for copy in fetch([(gc_ref, gc_hbm), (gz_ref, gz_hbm)], sems):
        copy.wait()


def final_kernel(
    a_ref, s_ref, cum_ref, tail_ref, x_ref, b_ref, gx_ref, gb_ref, gl_ref,
    ox_hbm, ob_hbm, ol_hbm, skip_hbm, weight_hbm, ox_ref, ob_ref, ol_ref, skip_ref, weight_ref, sems,
):
    heads, length = cum_ref.shape
    width = x_ref.shape[1]
    spread = head_map(heads, width)
    outs = [(weight_ref, weight_hbm), (skip_ref, skip_hbm), (ol_ref, ol_hbm), (ob_ref, ob_hbm)]
    outs += zip(quarters(ox_ref), quarters(ox_hbm))
    copies = [pltpu.make_async_copy(src, dst, sems.at[i]) for i, (src, dst) in enumerate(outs)]
    sums = [a_ref[34 * 4 * q + 32 : 34 * 4 * q + 34, :] for q in range(8)]
    weight_ref[...] = jnp.concatenate([one[0:1, :] for one in sums], axis=0)
    copies[0].start()
    skip = jnp.concatenate([one[1:2, :] for one in sums], axis=0)
    halves = jnp.where(iota((HALF, heads), 0) // P_SIZE == iota((HALF, heads), 1) % 2, 1.0, 0.0).astype(BF16)
    skip = mm_by(skip, halves)
    skip = jnp.where(iota((8, heads), 1) // 2 == iota((8, heads), 0), skip, 0.0)
    skip_ref[...] = jnp.sum(skip, axis=0, keepdims=True)
    copies[1].start()
    b_val = b_ref[...]
    late = jnp.zeros((heads, length), F32)
    far = jnp.zeros(ob_ref.shape, F32)
    starts = []
    for k in range(width // 256):
        big = slice(256 * k, 256 * (k + 1))
        after = load_block(a_ref, 34, k)
        starts.append(jnp.sum(load_block(s_ref, 32, k) * after, axis=0, keepdims=True))
        tail, x_val = tail_ref[:, big], x_ref[:, big].astype(F32)
        a_hi, a_lo = split2(after)
        b_after = (mm(b_val, a_hi) + mm(b_val, a_lo)) * tail
        ox_ref[:, big] = (gx_ref[:, big] + b_after).astype(BF16)
        copies[4 + k].start()
        late = late + segment(x_val * b_after, spread[:, big])
        x_hi, x_lo = split2(x_val * tail)
        far = far + (mm(x_hi, a_hi, 1, 1) + mm(x_hi, a_lo, 1, 1) + mm(x_lo, a_hi, 1, 1))
    ob_ref[...] = gb_ref[...] + far
    copies[3].start()
    start = jnp.broadcast_to(jnp.concatenate(starts, axis=1), (HALF, width))
    hi, mid, lo = split3(start)
    start = (mm(spread, hi, 1, 1) + mm(spread, mid, 1, 1) + mm(spread, lo, 1, 1))[:, 0:1]
    whole = jnp.exp(cum_ref[:, length - 1 : length])
    ol_ref[...] = gl_ref[...] + mm_by(late, triangle(length, lambda i, j: i < j)) + whole * start
    copies[2].start()
    for copy in copies:
        copy.wait()


def call(kernel, name, outs, *args, flops=0, scratch=(), hbm_in=(), hbm_out=(), mib=16):
    nbytes = sum(a.size * a.dtype.itemsize for a in (*args, *outs))
    spaces = [pltpu.HBM if i in hbm_in else pltpu.VMEM for i in range(len(args))]
    out_spaces = [pltpu.HBM if i in hbm_out else pltpu.VMEM for i in range(len(outs))]
    return pl.pallas_call(
        kernel,
        name=name,
        out_shape=[space(o.shape, o.dtype) for space, o in zip(out_spaces, outs)],
        in_specs=[pl.BlockSpec(memory_space=space) for space in spaces],
        out_specs=[pl.BlockSpec(memory_space=space) for space in out_spaces],
        scratch_shapes=list(scratch),
        compiler_params=pltpu.CompilerParams(vmem_limit_bytes=mib * 1024 * 1024),
        cost_estimate=pl.CostEstimate(flops=flops, bytes_accessed=nbytes, transcendentals=0),
    )(*[pltpu.with_memory_space_constraint(a, space) for a, space in zip(args, spaces)])


def exchange(messages, rows):
    count = lax.axis_size(CHUNKS)
    got = lax.all_to_all(messages.reshape(count, 1, rows * HALF), CHUNKS, 0, 0)
    return got.reshape(count * rows, HALF)


def on_device(x_in, b_in, c_in, decay_log, d_skip, gate, norm_weight, d_out):
    length, heads = decay_log.shape
    width = x_in.shape[1]
    chunks = lax.axis_size(CHUNKS)
    groups = lax.axis_size("heads")
    shape = jax.ShapeDtypeStruct
    wide = shape((length, width), F32)
    half_wide = shape((length, width), BF16)
    small = shape((heads, length), F32)
    weight = norm_weight.reshape(1, width)
    d_row = d_skip.reshape(1, heads)
    sem = pltpu.SemaphoreType.DMA
    narrow = shape(b_in.shape, F32)
    half_narrow = shape(b_in.shape, BF16)

    pay, cum, tail, x_val, b_val = call(
        start_kernel, "start", [shape((chunks * 33, HALF), F32), small, wide, half_wide, half_narrow],
        decay_log.T, x_in, b_in,
        flops=10**9, scratch=[pltpu.VMEM((heads, length), F32), sem((6,))], hbm_in=(0, 1, 2),
    )
    got = exchange(pay, 33)
    y_near, base, silu, esilu, ecum, c_val, z_val, d_val, w_val, dout_val = call(
        local_kernel, "local",
        [wide] * 5 + [half_narrow, half_wide, shape(d_row.shape, F32), shape(weight.shape, F32), half_wide],
        cum, x_val, b_val, c_in, gate, d_row, weight, d_out,
        flops=8 * 10**9, scratch=[sem((5,))], hbm_in=(3, 4, 5, 6, 7), mib=24,
    )
    spread, decays = call(
        prefix_kernel, "prefix", [shape((chunks * 32, HALF), F32), shape((chunks, HALF), F32)], got
    )
    before = exchange(spread, 32)
    gated, c_state, sums = call(
        gate_kernel, "gated", [wide, wide, shape((groups, 8, length), F32)],
        before, c_val, base, esilu, dout_val, w_val, flops=10**9,
    )
    sums = lax.all_to_all(sums, "heads", 0, 0)

    def back(*refs):
        back_kernel(float(width * groups), *refs)

    pay, scalars = call(
        back, "back", [shape((chunks * 34, HALF), F32), shape((length, HALF), F32)],
        sums, gated, silu, ecum, dout_val, w_val, x_val, c_val, flops=10**9,
    )
    got = exchange(pay, 34)
    gx, grad_gate, gb, grad_c, gl = call(
        grads_kernel, "grads", [wide, half_wide, narrow, narrow, small],
        cum, scalars, gated, silu, ecum, dout_val, w_val, x_val, z_val, b_val, c_val, d_val, y_near, c_state, before,
        flops=16 * 10**9, hbm_out=(1, 3), mib=28,
        scratch=[pltpu.VMEM((length, width), F32)] * 2
        + [pltpu.VMEM((length, width), BF16), pltpu.VMEM(b_in.shape, F32), sem((2,))],
    )
    (spread,) = call(suffix_kernel, "suffix", [shape((chunks * 34, HALF), F32)], got, decays)
    after = exchange(spread, 34)
    outs = [half_wide, narrow, small, shape((1, heads), F32), shape((8, HALF), F32)]
    grad_x, grad_b, grad_decay, grad_skip, grad_weight = call(
        final_kernel, "final", outs,
        after, before, cum, tail, x_val, b_val, gx, gb, gl,
        flops=2 * 10**9, scratch=[pltpu.VMEM(o.shape, o.dtype) for o in outs] + [sem((8,))], hbm_out=range(5),
    )
    return (
        grad_x,
        grad_b,
        grad_c,
        grad_decay.T,
        grad_skip.reshape(heads),
        grad_gate,
        grad_weight.reshape(width),
    )


def solution(mesh):
    tokens = P(CHUNKS, "heads")
    in_specs = (tokens, tokens, tokens, tokens, P("heads"), tokens, P("heads"), tokens)
    out_specs = (tokens, tokens, tokens, tokens, P("heads"), tokens, P("heads"))
    return jax.shard_map(on_device, mesh=mesh, in_specs=in_specs, out_specs=out_specs, check_vma=False)
```

```python
import jax
import jax.numpy as jnp
from jax import lax
from jax.experimental import pallas as pl
from jax.experimental.pallas import tpu as pltpu
from jax.sharding import PartitionSpec as P

P_SIZE = 64
EPS = 1e-05
F32 = jnp.float32
BF16 = jnp.bfloat16
CHUNKS = ("outer", "inner")
HALF = 128


def mm(a, b, ca=1, cb=0):
    return lax.dot_general(a, b, (((ca,), (cb,)), ((), ())), preferred_element_type=F32)


def split2(a):
    hi = a.astype(BF16)
    return hi, (a - hi.astype(F32)).astype(BF16)


def split3(a):
    hi = a.astype(BF16)
    rest = a - hi.astype(F32)
    mid = rest.astype(BF16)
    return hi, mid, (rest - mid.astype(F32)).astype(BF16)


def mm2(a, b, ca=1, cb=0):
    hi, lo = split2(a)
    return mm(hi, b, ca, cb) + mm(lo, b, ca, cb)


def iota(shape, dim):
    return lax.broadcasted_iota(jnp.int32, shape, dim)


def head_map(heads, width):
    return jnp.where(iota((heads, width), 1) // P_SIZE == iota((heads, width), 0), 1.0, 0.0).astype(BF16)


def expand(a, spread, ca=1):
    hi, lo = split2(a)
    return mm(hi, spread, ca) + mm(lo, spread, ca)


def segment(a, spread):
    hi, lo = split2(a)
    return mm(spread, hi, 1, 1) + mm(spread, lo, 1, 1)


def triangle(n, keep):
    return jnp.where(keep(iota((n, n), 0), iota((n, n), 1)), 1.0, 0.0).astype(BF16)


def mm_by(a, tri):
    hi, mid, lo = split3(a)
    return mm(hi, tri) + mm(mid, tri) + mm(lo, tri)


def load_block(ref, rows, k):
    cols = []
    for q in (2 * k, 2 * k + 1):
        at = [rows * (4 * q + r) for r in range(4)]
        cols.append(jnp.concatenate([ref[i : i + 32, :] for i in at], axis=0))
    return jnp.concatenate(cols, axis=1)


def copies_of(pairs, sems):
    return [pltpu.make_async_copy(src, dst, sems.at[i]) for i, (src, dst) in enumerate(pairs)]


def fetch(pairs, sems):
    copies = copies_of(pairs, sems)
    for copy in copies:
        copy.start()
    return copies


def quarters(ref):
    return [ref.at[:, pl.ds(256 * k, 256)] for k in range(4)]


def block_sums(lt):
    return mm_by(lt, triangle(lt.shape[1], lambda i, j: i <= j))


def skip_row(d_ref, spread):
    heads, width = spread.shape
    hi, mid, lo = split3(jnp.broadcast_to(d_ref[...], (8, heads)))
    return (mm(hi, spread) + mm(mid, spread) + mm(lo, spread))[0:1, :]


def start_kernel(lt_hbm, x_hbm, b_hbm, pay_ref, lt_ref, b_ref, x_ref, sems):
    heads, length = lt_hbm.shape
    width = x_hbm.shape[1]
    pairs = [(lt_hbm, lt_ref), (b_hbm, b_ref)] + list(zip(quarters(x_hbm), quarters(x_ref)))
    first, second, *copies = fetch(pairs, sems)
    spread = head_map(heads, width)
    first.wait()
    cum = block_sums(lt_ref[...])
    last = cum[:, length - 1 : length]
    tail = expand(jnp.exp(last - cum), spread, 0)
    whole = expand(jnp.broadcast_to(jnp.exp(last), (heads, HALF)), spread, 0)[0:1, :]
    second.wait()
    b_val = b_ref[...]
    for k in range(4):
        copies[k].wait()
        big = slice(256 * k, 256 * (k + 1))
        hi, lo = split2(x_ref[:, big].astype(F32) * tail[:, big])
        state = mm(b_val, hi, 0, 0) + mm(b_val, lo, 0, 0)
        for q in (2 * k, 2 * k + 1):
            for r in range(4):
                at = 33 * (4 * q + r)
                off = HALF * (q - 2 * k)
                pay_ref[at : at + 32, :] = state[32 * r : 32 * r + 32, off : off + HALF]
                pay_ref[at + 32 : at + 33, :] = whole[:, HALF * q : HALF * (q + 1)]


def local_kernel(
    lt_hbm, x_hbm, b_hbm, c_hbm, z_hbm, d_hbm, w_hbm, dout_hbm,
    base_ref, esilu_ref, c_ref, w_ref, dout_ref, yn_hbm,
    lt_ref, x_ref, b_ref, z_ref, d_ref, yn_ref, sems,
):
    heads, length = lt_hbm.shape
    width = x_hbm.shape[1]
    copies = fetch(
        [(lt_hbm, lt_ref), (b_hbm, b_ref), (c_hbm, c_ref), (x_hbm, x_ref), (z_hbm, z_ref), (d_hbm, d_ref),
         (w_hbm, w_ref), (dout_hbm, dout_ref)],
        sems,
    )
    outs = [
        pltpu.make_async_copy(src, dst, sems.at[8 + k])
        for k, (src, dst) in enumerate(zip(quarters(yn_ref), quarters(yn_hbm)))
    ]
    spread = head_map(heads, width)
    for copy in copies[:3]:
        copy.wait()
    cum_t = block_sums(lt_ref[...])
    cum = cum_t.T
    ecum = expand(jnp.exp(cum_t), spread, 0)
    inner = mm(c_ref[...], b_ref[...], 1, 1)
    top, left, right = inner[:HALF, :HALF], inner[HALF:, :HALF], inner[HALF:, HALF:]
    lower = iota((HALF, HALF), 0) >= iota((HALF, HALF), 1)
    first = iota((length, HALF), 1) < P_SIZE
    for copy in copies[3:6]:
        copy.wait()
    skip = skip_row(d_ref, spread)
    for q in range(width // HALF):
        cols = slice(HALF * q, HALF * (q + 1))
        x_pair = x_ref[:, cols]
        parts = []
        for h in (2 * q, 2 * q + 1):
            col, row = cum[:, h : h + 1], cum_t[h : h + 1, :]
            up = jnp.where(lower, jnp.exp(col[:HALF] - row[:, :HALF]), 0.0) * top
            dl = jnp.exp(col[HALF:] - row[:, :HALF]) * left
            dr = jnp.where(lower, jnp.exp(col[HALF:] - row[:, HALF:]), 0.0) * right
            down = jnp.concatenate([dl, dr], axis=1)
            parts.append(jnp.concatenate([mm2(up, x_pair[:HALF]), mm2(down, x_pair)], axis=0))
        yn = jnp.where(first, parts[0], parts[1])
        yn_ref[:, cols] = yn
        if q % 2 == 1:
            outs[q // 2].start()
        z_val = z_ref[:, cols].astype(F32)
        silu = z_val * (1.0 / (1.0 + jnp.exp(-z_val)))
        esilu_ref[:, cols] = ecum[:, cols] * silu
        base_ref[:, cols] = (yn + skip[:, cols] * x_pair.astype(F32)) * silu
    for copy in copies[6:] + outs:
        copy.wait()


def prefix_kernel(in_ref, out_ref, dec_ref):
    count = dec_ref.shape[0]
    state = jnp.zeros((32, HALF), F32)
    for p in range(count):
        out_ref[32 * p : 32 * p + 32, :] = state
        decay = in_ref[33 * p + 32 : 33 * p + 33, :]
        dec_ref[p : p + 1, :] = decay
        if p < count - 1:
            state = decay * state + in_ref[33 * p : 33 * p + 32, :]


def gate_kernel(s_ref, c_ref, base_ref, esilu_ref, dout_ref, w_ref, gated_ref, sums_ref):
    c_val = c_ref[...]
    length, width = base_ref.shape
    squares = jnp.zeros((length, HALF), F32)
    products = jnp.zeros((length, HALF), F32)
    for q in range(width // 256):
        big = slice(256 * q, 256 * (q + 1))
        hi, lo = split2(load_block(s_ref, 32, q))
        c_state = mm(c_val, hi) + mm(c_val, lo)
        gated = base_ref[:, big] + esilu_ref[:, big] * c_state
        gated_ref[:, big] = gated
        sq = gated * gated
        pr = dout_ref[:, big].astype(F32) * w_ref[:, big] * gated
        squares = squares + sq[:, :HALF] + sq[:, HALF:]
        products = products + pr[:, :HALF] + pr[:, HALF:]
    sq_row = jnp.sum(squares.T, axis=0, keepdims=True)
    pr_row = jnp.sum(products.T, axis=0, keepdims=True)
    tile = jnp.concatenate([sq_row, pr_row, jnp.zeros((6, length), F32)], axis=0)
    for i in range(sums_ref.shape[0]):
        sums_ref[i] = tile


def back_kernel(
    channels, sums_ref, gated_ref, esilu_ref, dout_ref, w_ref, c_ref, s_ref,
    pay_ref, scal_hbm, s_hbm, scal_ref, sems,
):
    length, width = gated_ref.shape
    scal_copy, s_copy = copies_of([(scal_ref, scal_hbm), (s_ref, s_hbm)], sems)
    s_copy.start()
    total = sums_ref[0]
    for i in range(1, sums_ref.shape[0]):
        total = total + sums_ref[i]
    squares, products = total[0:1, :], total[1:2, :]
    inv = lax.rsqrt(squares / channels + EPS)
    fall = inv * inv * inv * products / channels
    rows = jnp.concatenate([inv, fall, jnp.zeros((6, length), F32)], axis=0)
    scal_ref[...] = rows
    scal_copy.start()
    both = jnp.concatenate([rows, jnp.zeros((HALF - 8, length), F32)], axis=0).T
    inv_col, fall_col = both[:, 0:1], both[:, 1:2]
    c_val = c_ref[...]
    for k in range(width // 256):
        big = slice(256 * k, 256 * (k + 1))
        gated = gated_ref[:, big]
        d_inv = dout_ref[:, big].astype(F32) * inv_col
        weight = jnp.sum(d_inv * gated, axis=0, keepdims=True)
        hi, lo = split2((d_inv * w_ref[:, big] - gated * fall_col) * esilu_ref[:, big])
        back = mm(c_val, hi, 0, 0) + mm(c_val, lo, 0, 0)
        for q in (2 * k, 2 * k + 1):
            off = HALF * (q - 2 * k)
            for r in range(4):
                at = 33 * (4 * q + r)
                pay_ref[at : at + 32, :] = back[32 * r : 32 * r + 32, off : off + HALF]
                pay_ref[at + 32 : at + 33, :] = weight[:, off : off + HALF]
    scal_copy.wait()
    s_copy.wait()


def grads_kernel(
    lt_hbm, scal_hbm, dout_hbm, w_hbm, x_hbm, z_hbm, b_hbm, c_hbm, d_hbm, yn_hbm, s_hbm,
    gx_ref, gb_ref, gl_ref, tail_ref, x_ref, s_ref, b_ref, skip_ref, gz_hbm, gc_hbm,
    lt_ref, scal_ref, dout_ref, w_ref, z_ref, c_ref, d_ref, yn_ref, dye_ref, dot_ref, gz_ref, gc_ref, sems,
):
    heads, length = lt_hbm.shape
    width = x_hbm.shape[1]
    copies = fetch(
        [(lt_hbm, lt_ref), (scal_hbm, scal_ref), (b_hbm, b_ref), (c_hbm, c_ref), (d_hbm, d_ref), (w_hbm, w_ref),
         (x_hbm, x_ref), (s_hbm, s_ref), (yn_hbm, yn_ref), (z_hbm, z_ref), (dout_hbm, dout_ref)],
        sems,
    )
    outs = [
        pltpu.make_async_copy(src, dst, sems.at[11 + k])
        for k, (src, dst) in enumerate([(gc_ref, gc_hbm), *zip(quarters(gz_ref), quarters(gz_hbm))])
    ]
    spread = head_map(heads, width)
    for copy in copies[:6]:
        copy.wait()
    cum_t = block_sums(lt_ref[...])
    cum = cum_t.T
    last = cum_t[:, length - 1 : length]
    ecum = expand(jnp.exp(cum_t), spread, 0)
    tail_ref[...] = expand(jnp.exp(last - cum_t), spread, 0)
    both = jnp.concatenate([scal_ref[...], jnp.zeros((HALF - 8, length), F32)], axis=0).T
    inv_col, fall_col = both[:, 0:1], both[:, 1:2]
    skip = skip_row(d_ref, spread)
    b_val, c_val = b_ref[...], c_ref[...]
    inner_t = mm(b_val, c_val, 1, 1)
    left, right, low = inner_t[:HALF, :HALF], inner_t[:HALF, HALF:], inner_t[HALF:, HALF:]
    upper = iota((HALF, HALF), 0) <= iota((HALF, HALF), 1)
    first = iota((length, HALF), 1) < P_SIZE
    w_left = jnp.zeros((HALF, HALF), F32)
    w_right = jnp.zeros((HALF, HALF), F32)
    w_low = jnp.zeros((HALF, HALF), F32)
    skips = []
    far = jnp.zeros((length, HALF), F32)
    for copy in copies[6:]:
        copy.wait()
    for q in range(width // HALF):
        cols = slice(HALF * q, HALF * (q + 1))
        x_pair = x_ref[:, cols]
        x_val = x_pair.astype(F32)
        z_val = z_ref[:, cols].astype(F32)
        sig = 1.0 / (1.0 + jnp.exp(-z_val))
        silu = z_val * sig
        if q % 2 == 0:
            s_hi, s_lo = split2(load_block(s_ref, 32, q // 2))
            c_state = mm(c_val, s_hi) + mm(c_val, s_lo)
        off = slice(HALF * (q % 2), HALF * (q % 2 + 1))
        y_near = yn_ref[:, cols] + ecum[:, cols] * c_state[:, off]
        y_val = y_near + skip[:, cols] * x_val
        d_gated = inv_col * (dout_ref[:, cols].astype(F32) * w_ref[:, cols]) - y_val * silu * fall_col
        dy = d_gated * silu
        dye_ref[:, cols] = dy * ecum[:, cols]
        gz_ref[:, cols] = (d_gated * y_val * sig * (1.0 + z_val * (1.0 - sig))).astype(BF16)
        if q % 2 == 1:
            outs[1 + q // 2].start()
            e_hi, e_lo = split2(dye_ref[:, 128 * q - 128 : 128 * q + 128])
            far = far + (mm(e_hi, s_hi, 1, 1) + mm(e_hi, s_lo, 1, 1) + mm(e_lo, s_hi, 1, 1))
        skips.append(jnp.sum(dy * x_val, axis=0, keepdims=True))
        hi, lo = split2(dy)
        parts = []
        for k in range(2):
            h = 2 * q + k
            col, row = cum[:, h : h + 1], cum_t[h : h + 1, :]
            x_one = jnp.where(first if k == 0 else ~first, x_val, 0.0).astype(BF16)
            dec_left = jnp.where(upper, jnp.exp(row[:, :HALF] - col[:HALF]), 0.0)
            dec_right = jnp.exp(row[:, HALF:] - col[:HALF])
            dec_low = jnp.where(upper, jnp.exp(row[:, HALF:] - col[HALF:]), 0.0)
            dot_up = mm(x_one[:HALF], hi, 1, 1) + mm(x_one[:HALF], lo, 1, 1)
            dot_low = mm(x_one[HALF:], hi[HALF:], 1, 1) + mm(x_one[HALF:], lo[HALF:], 1, 1)
            w_left = w_left + dec_left * dot_up[:, :HALF]
            w_right = w_right + dec_right * dot_up[:, HALF:]
            w_low = w_low + dec_low * dot_low
            mix_up = jnp.concatenate([dec_left * left, dec_right * right], axis=1)
            mix_low = dec_low * low
            up_hi, up_lo = split2(mix_up)
            low_hi, low_lo = split2(mix_low)
            g_up = mm(up_hi, hi) + mm(up_hi, lo) + mm(up_lo, hi)
            g_low = mm(low_hi, hi[HALF:]) + mm(low_hi, lo[HALF:]) + mm(low_lo, hi[HALF:])
            parts.append(jnp.concatenate([g_up, g_low], axis=0))
        g_near = jnp.where(first, parts[0], parts[1])
        gx_ref[:, cols] = g_near + skip[:, cols] * dy
        dot_ref[:, cols] = dy * y_near - x_val * g_near
    w_up = jnp.concatenate([w_left, w_right], axis=1)
    low_part = mm2(w_right.T, b_val[:HALF]) + mm2(w_low.T, b_val[HALF:])
    gc_ref[...] = far + jnp.concatenate([mm2(w_left.T, b_val[:HALF]), low_part], axis=0)
    outs[0].start()
    gl_ref[...] = mm_by(segment(dot_ref[...], spread), triangle(length, lambda i, j: i >= j))
    gb_ref[:HALF, :] = mm2(w_up, c_val)
    gb_ref[HALF:, :] = mm2(w_low, c_val[HALF:])
    hi, mid, lo = split3(jnp.broadcast_to(jnp.concatenate(skips, axis=1), (8, width)))
    wide = head_map(HALF, width)
    skip_ref[...] = mm(hi, wide, 1, 1) + mm(mid, wide, 1, 1) + mm(lo, wide, 1, 1)
    for copy in outs:
        copy.wait()


def suffix_kernel(in_ref, dec_ref, skip_ref, out_ref):
    count = dec_ref.shape[0]
    state = jnp.zeros((32, HALF), F32)
    sums = in_ref[32:33, :]
    for p in range(1, count):
        sums = sums + in_ref[33 * p + 32 : 33 * p + 33, :]
    rows = jnp.concatenate([sums, skip_ref[0:1, :]], axis=0)
    for p in range(count - 1, -1, -1):
        out_ref[34 * p : 34 * p + 32, :] = state
        out_ref[34 * p + 32 : 34 * p + 34, :] = rows
        if p > 0:
            state = dec_ref[p : p + 1, :] * state + in_ref[33 * p : 33 * p + 32, :]


def final_kernel(
    a_ref, s_ref, lt_hbm, tail_ref, x_ref, b_ref, gx_ref, gb_ref, gl_ref,
    ox_hbm, ob_hbm, ol_hbm, skip_hbm, weight_hbm, ox_ref, ob_ref, ol_ref, skip_ref, weight_ref, lt_ref, sems,
):
    heads, length = lt_hbm.shape
    width = x_ref.shape[1]
    spread = head_map(heads, width)
    outs = [(weight_ref, weight_hbm), (skip_ref, skip_hbm), (ol_ref, ol_hbm), (ob_ref, ob_hbm)]
    outs += zip(quarters(ox_ref), quarters(ox_hbm))
    copies = copies_of(outs + [(lt_hbm, lt_ref)], sems)
    copies[8].start()
    weight_ref[...] = jnp.concatenate([a_ref[136 * q + 32 : 136 * q + 33, :] for q in range(8)], axis=0)
    copies[0].start()
    skip = a_ref[33:34, :]
    for p in range(1, a_ref.shape[0] // 34):
        skip = skip + a_ref[34 * p + 33 : 34 * p + 34, :]
    skip_ref[...] = skip[:, :heads]
    copies[1].start()
    b_val = b_ref[...]
    late = jnp.zeros((heads, length), F32)
    far = jnp.zeros(ob_ref.shape, F32)
    starts = []
    for k in range(width // 256):
        big = slice(256 * k, 256 * (k + 1))
        after = load_block(a_ref, 34, k)
        starts.append(jnp.sum(load_block(s_ref, 32, k) * after, axis=0, keepdims=True))
        tail, x_val = tail_ref[:, big], x_ref[:, big].astype(F32)
        a_hi, a_lo = split2(after)
        b_after = (mm(b_val, a_hi) + mm(b_val, a_lo)) * tail
        ox_ref[:, big] = (gx_ref[:, big] + b_after).astype(BF16)
        copies[4 + k].start()
        late = late + segment(x_val * b_after, spread[:, big])
        x_hi, x_lo = split2(x_val * tail)
        far = far + (mm(x_hi, a_hi, 1, 1) + mm(x_hi, a_lo, 1, 1) + mm(x_lo, a_hi, 1, 1))
    ob_ref[...] = gb_ref[...] + far
    copies[3].start()
    start = jnp.broadcast_to(jnp.concatenate(starts, axis=1), (HALF, width))
    hi, mid, lo = split3(start)
    start = (mm(spread, hi, 1, 1) + mm(spread, mid, 1, 1) + mm(spread, lo, 1, 1))[:, 0:1]
    copies[8].wait()
    whole = jnp.exp(jnp.sum(lt_ref[...], axis=1, keepdims=True))
    ol_ref[...] = gl_ref[...] + mm_by(late, triangle(length, lambda i, j: i < j)) + whole * start
    copies[2].start()
    for copy in copies[:8]:
        copy.wait()


def call(kernel, name, outs, *args, flops=0, scratch=(), hbm_in=(), hbm_out=(), mib=16):
    nbytes = sum(a.size * a.dtype.itemsize for a in (*args, *outs))
    spaces = [pltpu.HBM if i in hbm_in else pltpu.VMEM for i in range(len(args))]
    out_spaces = [pltpu.HBM if i in hbm_out else pltpu.VMEM for i in range(len(outs))]
    return pl.pallas_call(
        kernel,
        name=name,
        out_shape=[space(o.shape, o.dtype) for space, o in zip(out_spaces, outs)],
        in_specs=[pl.BlockSpec(memory_space=space) for space in spaces],
        out_specs=[pl.BlockSpec(memory_space=space) for space in out_spaces],
        scratch_shapes=list(scratch),
        compiler_params=pltpu.CompilerParams(vmem_limit_bytes=mib * 1024 * 1024),
        cost_estimate=pl.CostEstimate(flops=flops, bytes_accessed=nbytes, transcendentals=0),
    )(*[pltpu.with_memory_space_constraint(a, space) for a, space in zip(args, spaces)])


def exchange(messages, rows):
    count = lax.axis_size(CHUNKS)
    got = lax.all_to_all(messages.reshape(count, 1, rows * HALF), CHUNKS, 0, 0)
    return got.reshape(count * rows, HALF)


def on_device(x_in, b_in, c_in, decay_log, d_skip, gate, norm_weight, d_out):
    length, heads = decay_log.shape
    width = x_in.shape[1]
    chunks = lax.axis_size(CHUNKS)
    groups = lax.axis_size("heads")
    shape = jax.ShapeDtypeStruct
    wide = shape((length, width), F32)
    half_wide = shape((length, width), BF16)
    small = shape((heads, length), F32)
    narrow = shape(b_in.shape, F32)
    half_narrow = shape(b_in.shape, BF16)
    state = shape((chunks * 32, HALF), F32)
    weight = norm_weight.reshape(1, width)
    d_row = d_skip.reshape(1, heads)
    w_row, one_row = shape(weight.shape, F32), shape(d_row.shape, F32)
    decay_t = decay_log.T
    sem = pltpu.SemaphoreType.DMA

    def vmem(*shapes):
        return [pltpu.VMEM(s.shape, s.dtype) for s in shapes]

    (pay,) = call(
        start_kernel, "start", [shape((chunks * 33, HALF), F32)], decay_t, x_in, b_in,
        flops=10**9, scratch=vmem(small, half_narrow, half_wide) + [sem((6,))], hbm_in=(0, 1, 2),
    )
    got = exchange(pay, 33)
    base, esilu, c_val, w_val, dout_val, y_near = call(
        local_kernel, "local", [wide, wide, half_narrow, w_row, half_wide, wide],
        decay_t, x_in, b_in, c_in, gate, d_row, weight, d_out,
        flops=8 * 10**9, hbm_in=range(8), hbm_out=(5,), mib=24,
        scratch=vmem(small, half_wide, half_narrow, half_wide, one_row, wide) + [sem((12,))],
    )
    spread, decays = call(prefix_kernel, "prefix", [state, shape((chunks, HALF), F32)], got)
    before = exchange(spread, 32)
    gated, sums = call(
        gate_kernel, "gated", [wide, shape((groups, 8, length), F32)],
        before, c_val, base, esilu, dout_val, w_val, flops=10**9,
    )
    sums = lax.all_to_all(sums, "heads", 0, 0)

    def back(*refs):
        back_kernel(float(width * groups), *refs)

    rows = shape((8, length), F32)
    pay, scalars, before = call(
        back, "back", [shape((chunks * 33, HALF), F32), rows, state],
        sums, gated, esilu, dout_val, w_val, c_val, before,
        flops=10**9, hbm_out=(1, 2), scratch=vmem(rows) + [sem((2,))],
    )
    got = exchange(pay, 33)
    gx, gb, gl, tail, x_val, before, b_val, skip, grad_gate, grad_c = call(
        grads_kernel, "grads",
        [wide, narrow, small, wide, half_wide, state, half_narrow, shape((8, HALF), F32), half_wide, narrow],
        decay_t, scalars, d_out, weight, x_in, gate, b_in, c_in, d_row, y_near, before,
        flops=16 * 10**9, hbm_in=range(11), hbm_out=(8, 9), mib=32,
        scratch=vmem(small, rows, half_wide, w_row, half_wide, half_narrow, one_row, wide, wide, wide, half_wide, narrow)
        + [sem((16,))],
    )
    (spread,) = call(suffix_kernel, "suffix", [shape((chunks * 34, HALF), F32)], got, decays, skip)
    after = exchange(spread, 34)
    outs = [half_wide, narrow, small, one_row, shape((8, HALF), F32)]
    grad_x, grad_b, grad_decay, grad_skip, grad_weight = call(
        final_kernel, "final", outs,
        after, before, decay_t, tail, x_val, b_val, gx, gb, gl,
        flops=2 * 10**9, scratch=vmem(*outs, small) + [sem((9,))], hbm_in=(2,), hbm_out=range(5),
    )
    return (
        grad_x,
        grad_b,
        grad_c,
        grad_decay.T,
        grad_skip.reshape(heads),
        grad_gate,
        grad_weight.reshape(width),
    )


def solution(mesh):
    tokens = P(CHUNKS, "heads")
    in_specs = (tokens, tokens, tokens, tokens, P("heads"), tokens, P("heads"), tokens)
    out_specs = (tokens, tokens, tokens, tokens, P("heads"), tokens, P("heads"))
    return jax.shard_map(on_device, mesh=mesh, in_specs=in_specs, out_specs=out_specs, check_vma=False)
```

```python
import jax
import jax.numpy as jnp
from jax import lax
from jax.experimental import pallas as pl
from jax.experimental.pallas import tpu as pltpu
from jax.sharding import PartitionSpec as P

P_SIZE = 64
EPS = 1e-05
F32 = jnp.float32
BF16 = jnp.bfloat16
CHUNKS = ("outer", "inner")
HALF = 128


def mm(a, b, ca=1, cb=0):
    return lax.dot_general(a, b, (((ca,), (cb,)), ((), ())), preferred_element_type=F32)


def split2(a):
    hi = a.astype(BF16)
    return hi, (a - hi.astype(F32)).astype(BF16)


def split3(a):
    hi = a.astype(BF16)
    rest = a - hi.astype(F32)
    mid = rest.astype(BF16)
    return hi, mid, (rest - mid.astype(F32)).astype(BF16)


def mm2(a, b, ca=1, cb=0):
    hi, lo = split2(a)
    return mm(hi, b, ca, cb) + mm(lo, b, ca, cb)


def mm_split(a, b):
    return mm(jnp.concatenate([a, a], axis=1), jnp.concatenate(split2(b), axis=0))


def iota(shape, dim):
    return lax.broadcasted_iota(jnp.int32, shape, dim)


def head_map(heads, width):
    return jnp.where(iota((heads, width), 1) // P_SIZE == iota((heads, width), 0), 1.0, 0.0).astype(BF16)


def expand(a, spread):
    hi, lo = split2(a)
    both = jnp.concatenate([hi.astype(F32), lo.astype(F32)], axis=0).T.astype(BF16)
    return mm(both, jnp.concatenate([spread, spread], axis=0))


def segment(a, spread):
    turned_map = turned(spread)
    hi, lo = split2(a)
    return (mm(hi, turned_map) + mm(lo, turned_map)).T


def triangle(n, keep):
    return jnp.where(keep(iota((n, n), 0), iota((n, n), 1)), 1.0, 0.0).astype(BF16)


def mm_by(a, tri):
    rows = a.shape[0]
    got = mm(jnp.concatenate(split3(a), axis=0), tri)
    return got[:rows] + got[rows : 2 * rows] + got[2 * rows :]


def load_state(ref, rows):
    return jnp.concatenate([load_block(ref, rows, k) for k in range(4)], axis=1)


def load_block(ref, rows, k):
    cols = []
    for q in (2 * k, 2 * k + 1):
        at = [rows * (4 * q + r) for r in range(4)]
        cols.append(jnp.concatenate([ref[i : i + 32, :] for i in at], axis=0))
    return jnp.concatenate(cols, axis=1)


def copies_of(pairs, sems):
    return [pltpu.make_async_copy(src, dst, sems.at[i]) for i, (src, dst) in enumerate(pairs)]


def fetch(pairs, sems):
    copies = copies_of(pairs, sems)
    for copy in copies:
        copy.start()
    return copies


def quarters(ref):
    return [ref.at[:, pl.ds(256 * k, 256)] for k in range(4)]


def turned(a):
    return a.astype(F32).T.astype(BF16)


def block_sums(lt):
    return mm_by(lt, triangle(lt.shape[1], lambda i, j: i <= j))


def below(up, zeros, left, right, i):
    return jnp.concatenate(
        [jnp.concatenate([up[i], zeros], axis=1), jnp.concatenate([left[i], right[i]], axis=1)], axis=0
    )


def skip_row(d_ref, spread):
    heads, width = spread.shape
    hi, mid, lo = split3(jnp.broadcast_to(d_ref[...], (8, heads)))
    return (mm(hi, spread) + mm(mid, spread) + mm(lo, spread))[0:1, :]


def start_kernel(lt_hbm, x_hbm, b_hbm, pay_ref, lt_ref, b_ref, x_ref, sems):
    heads, length = lt_hbm.shape
    width = x_hbm.shape[1]
    first, second, third = fetch([(lt_hbm, lt_ref), (b_hbm, b_ref), (x_hbm, x_ref)], sems)
    second.wait()
    b_turned = b_ref[...].astype(F32).T
    first.wait()
    cum = block_sums(lt_ref[...])
    last = cum[:, length - 1 : length]
    ends = jnp.concatenate([last - cum, jnp.broadcast_to(last, (heads, HALF))], axis=1)
    tail = expand(jnp.exp(ends), head_map(heads, width))
    whole = tail[length : length + 1, :]
    third.wait()
    state = mm_split(b_turned.astype(BF16), x_ref[...].astype(F32) * tail[:length])
    for q in range(width // HALF):
        for r in range(4):
            at = 33 * (4 * q + r)
            pay_ref[at : at + 32, :] = state[32 * r : 32 * r + 32, HALF * q : HALF * (q + 1)]
            pay_ref[at + 32 : at + 33, :] = whole[:, HALF * q : HALF * (q + 1)]


def local_kernel(
    lt_hbm, x_hbm, b_hbm, c_hbm, z_hbm, d_hbm, w_hbm, dout_hbm,
    base_ref, esilu_ref, c_ref, ct_ref, w_ref, dout_ref, yn_hbm,
    lt_ref, x_ref, b_ref, z_ref, d_ref, yn_ref, sems,
):
    heads, length = lt_hbm.shape
    width = x_hbm.shape[1]
    copies = fetch(
        [(lt_hbm, lt_ref), (b_hbm, b_ref), (c_hbm, c_ref), (x_hbm, x_ref), (z_hbm, z_ref), (d_hbm, d_ref),
         (w_hbm, w_ref), (dout_hbm, dout_ref)],
        sems,
    )
    spread = head_map(heads, width)
    for copy in copies[:3]:
        copy.wait()
    cum_t = block_sums(lt_ref[...])
    cum = cum_t.T
    ecum = expand(jnp.exp(cum_t), spread)
    ct_ref[...] = turned(c_ref[...])
    inner = mm(c_ref[...], b_ref[...], 1, 1)
    top, left, right = inner[:HALF, :HALF], inner[HALF:, :HALF], inner[HALF:, HALF:]
    lower = iota((HALF, HALF), 0) >= iota((HALF, HALF), 1)
    first = iota((length, HALF), 1) < P_SIZE
    zeros = jnp.zeros((HALF, HALF), BF16)
    for copy in copies[3:6]:
        copy.wait()
    skip = skip_row(d_ref, spread)
    for q in range(width // HALF):
        cols = slice(HALF * q, HALF * (q + 1))
        x_pair = x_ref[:, cols]
        mixes = []
        for h in (2 * q, 2 * q + 1):
            col, row = cum[:, h : h + 1], cum_t[h : h + 1, :]
            up = jnp.where(lower, jnp.exp(col[:HALF] - row[:, :HALF]), 0.0) * top
            dl = jnp.exp(col[HALF:] - row[:, :HALF]) * left
            dr = jnp.where(lower, jnp.exp(col[HALF:] - row[:, HALF:]), 0.0) * right
            mixes += [below(split2(up), zeros, split2(dl), split2(dr), i) for i in range(2)]
        got = mm(jnp.concatenate(mixes, axis=0), x_pair)
        yn = jnp.where(
            first, got[:length] + got[length : 2 * length], got[2 * length : 3 * length] + got[3 * length :]
        )
        yn_ref[:, cols] = yn
        z_val = z_ref[:, cols].astype(F32)
        silu = z_val * (1.0 / (1.0 + jnp.exp(-z_val)))
        esilu_ref[:, cols] = ecum[:, cols] * silu
        base_ref[:, cols] = (yn + skip[:, cols] * x_pair.astype(F32)) * silu
    for copy in copies[6:]:
        copy.wait()
    yn_copy = pltpu.make_async_copy(yn_ref, yn_hbm, sems.at[8])
    yn_copy.start()
    yn_copy.wait()


def prefix_kernel(in_ref, out_ref, dec_ref):
    count = dec_ref.shape[0]
    state = jnp.zeros((32, HALF), F32)
    for p in range(count):
        out_ref[32 * p : 32 * p + 32, :] = state
        decay = in_ref[33 * p + 32 : 33 * p + 33, :]
        dec_ref[p : p + 1, :] = decay
        if p < count - 1:
            state = decay * state + in_ref[33 * p : 33 * p + 32, :]


def gate_kernel(s_ref, c_ref, base_ref, esilu_ref, dout_ref, w_ref, gated_ref, sums_ref):
    c_val = c_ref[...]
    length, width = base_ref.shape
    squares = jnp.zeros((length, HALF), F32)
    products = jnp.zeros((length, HALF), F32)
    for q in range(width // 256):
        big = slice(256 * q, 256 * (q + 1))
        c_state = mm_split(c_val, load_block(s_ref, 32, q))
        gated = base_ref[:, big] + esilu_ref[:, big] * c_state
        gated_ref[:, big] = gated
        sq = gated * gated
        pr = dout_ref[:, big].astype(F32) * w_ref[:, big] * gated
        squares = squares + sq[:, :HALF] + sq[:, HALF:]
        products = products + pr[:, :HALF] + pr[:, HALF:]
    sq_row = jnp.sum(squares.T, axis=0, keepdims=True)
    pr_row = jnp.sum(products.T, axis=0, keepdims=True)
    tile = jnp.concatenate([sq_row, pr_row, jnp.zeros((6, length), F32)], axis=0)
    for i in range(sums_ref.shape[0]):
        sums_ref[i] = tile


def back_kernel(
    channels, sums_ref, gated_ref, esilu_ref, dout_ref, w_ref, ct_ref, s_ref,
    pay_ref, scal_hbm, s_hbm, scal_ref, sems,
):
    length, width = gated_ref.shape
    scal_copy, s_copy = copies_of([(scal_ref, scal_hbm), (s_ref, s_hbm)], sems)
    s_copy.start()
    total = sums_ref[0]
    for i in range(1, sums_ref.shape[0]):
        total = total + sums_ref[i]
    squares, products = total[0:1, :], total[1:2, :]
    inv = lax.rsqrt(squares / channels + EPS)
    fall = inv * inv * inv * products / channels
    rows = jnp.concatenate([inv, fall, jnp.zeros((6, length), F32)], axis=0)
    scal_ref[...] = rows
    scal_copy.start()
    both = jnp.concatenate([rows, jnp.zeros((HALF - 8, length), F32)], axis=0).T
    inv_col, fall_col = both[:, 0:1], both[:, 1:2]
    c_turned = ct_ref[...]
    for k in range(width // 256):
        big = slice(256 * k, 256 * (k + 1))
        gated = gated_ref[:, big]
        d_inv = dout_ref[:, big].astype(F32) * inv_col
        weight = jnp.sum(d_inv * gated, axis=0, keepdims=True)
        back = mm_split(c_turned, (d_inv * w_ref[:, big] - gated * fall_col) * esilu_ref[:, big])
        for q in (2 * k, 2 * k + 1):
            off = HALF * (q - 2 * k)
            for r in range(4):
                at = 33 * (4 * q + r)
                pay_ref[at : at + 32, :] = back[32 * r : 32 * r + 32, off : off + HALF]
                pay_ref[at + 32 : at + 33, :] = weight[:, off : off + HALF]
    scal_copy.wait()
    s_copy.wait()


def grads_kernel(
    lt_hbm, scal_hbm, dout_hbm, w_hbm, x_hbm, z_hbm, b_hbm, c_hbm, d_hbm, yn_hbm, s_hbm,
    gx_ref, gb_ref, gl_ref, tail_ref, x_ref, b_ref, skip_ref, gz_hbm, gc_hbm,
    s_ref, lt_ref, scal_ref, dout_ref, w_ref, z_ref, c_ref, d_ref, yn_ref, dye_ref, dot_ref, gz_ref, gc_ref, sems,
):
    heads, length = lt_hbm.shape
    width = x_hbm.shape[1]
    copies = fetch(
        [(lt_hbm, lt_ref), (scal_hbm, scal_ref), (b_hbm, b_ref), (c_hbm, c_ref), (d_hbm, d_ref), (w_hbm, w_ref),
         (x_hbm, x_ref), (s_hbm, s_ref), (yn_hbm, yn_ref), (z_hbm, z_ref), (dout_hbm, dout_ref)],
        sems,
    )
    spread = head_map(heads, width)
    for copy in copies[:6]:
        copy.wait()
    cum_t = block_sums(lt_ref[...])
    cum = cum_t.T
    last = cum_t[:, length - 1 : length]
    ecum = expand(jnp.exp(cum_t), spread)
    tail_ref[...] = expand(jnp.exp(last - cum_t), spread)
    both = jnp.concatenate([scal_ref[...], jnp.zeros((HALF - 8, length), F32)], axis=0).T
    inv_col, fall_col = both[:, 0:1], both[:, 1:2]
    skip = skip_row(d_ref, spread)
    b_val, c_val = b_ref[...], c_ref[...]
    inner_t = mm(b_val, c_val, 1, 1)
    left, right, low = inner_t[:HALF, :HALF], inner_t[:HALF, HALF:], inner_t[HALF:, HALF:]
    upper = iota((HALF, HALF), 0) <= iota((HALF, HALF), 1)
    first = iota((length, HALF), 1) < P_SIZE
    zeros = jnp.zeros((HALF, HALF), BF16)
    w_left = jnp.zeros((HALF, HALF), F32)
    w_right = jnp.zeros((HALF, HALF), F32)
    w_low = jnp.zeros((HALF, HALF), F32)
    skips = []
    far = jnp.zeros((length, HALF), F32)
    for copy in copies[6:]:
        copy.wait()
    for q in range(width // HALF):
        cols = slice(HALF * q, HALF * (q + 1))
        x_pair = x_ref[:, cols]
        x_val = x_pair.astype(F32)
        z_val = z_ref[:, cols].astype(F32)
        sig = 1.0 / (1.0 + jnp.exp(-z_val))
        silu = z_val * sig
        if q % 2 == 0:
            state = load_block(s_ref, 32, q // 2)
            c_state = mm_split(c_val, state)
        off = slice(HALF * (q % 2), HALF * (q % 2 + 1))
        y_near = yn_ref[:, cols] + ecum[:, cols] * c_state[:, off]
        y_val = y_near + skip[:, cols] * x_val
        d_gated = inv_col * (dout_ref[:, cols].astype(F32) * w_ref[:, cols]) - y_val * silu * fall_col
        dy = d_gated * silu
        dye_ref[:, cols] = dy * ecum[:, cols]
        gz_ref[:, cols] = (d_gated * y_val * sig * (1.0 + z_val * (1.0 - sig))).astype(BF16)
        if q % 2 == 1:
            e_hi, e_lo = split2(dye_ref[:, 128 * q - 128 : 128 * q + 128])
            both = mm(jnp.concatenate([e_hi, e_lo], axis=0), jnp.concatenate(split2(state.T), axis=1))
            far = far + both[:length, :HALF] + both[:length, HALF:] + both[length:, :HALF]
        skips.append(jnp.sum(dy * x_val, axis=0, keepdims=True))
        hi, lo = split2(dy)
        ones = jnp.concatenate([jnp.where(first, x_val, 0.0), jnp.where(first, 0.0, x_val)], axis=0).astype(BF16)
        both = jnp.concatenate([hi, lo], axis=1)
        dots = mm(jnp.concatenate([ones, ones], axis=1), both, 1, 1)
        mix_hi, mix_lo = [], []
        for k in range(2):
            h = 2 * q + k
            col, row = cum[:, h : h + 1], cum_t[h : h + 1, :]
            dot = dots[length * k : length * (k + 1)]
            dec_left = jnp.where(upper, jnp.exp(row[:, :HALF] - col[:HALF]), 0.0)
            dec_right = jnp.exp(row[:, HALF:] - col[:HALF])
            dec_low = jnp.where(upper, jnp.exp(row[:, HALF:] - col[HALF:]), 0.0)
            w_left = w_left + dec_left * dot[:HALF, :HALF]
            w_right = w_right + dec_right * dot[:HALF, HALF:]
            w_low = w_low + dec_low * dot[HALF:, HALF:]
            blocks = [split2(m) for m in (dec_left * left, dec_right * right, dec_low * low)]
            for i, mix in enumerate((mix_hi, mix_lo)):
                up = jnp.concatenate([blocks[0][i], blocks[1][i]], axis=1)
                mix.append(jnp.concatenate([up, jnp.concatenate([zeros, blocks[2][i]], axis=1)], axis=0))
        got = mm(jnp.concatenate(mix_hi + mix_lo, axis=0), both)
        got = got[: 2 * length, :HALF] + got[: 2 * length, HALF:] + got[2 * length :, :HALF]
        g_near = jnp.where(first, got[:length], got[length:])
        gx_ref[:, cols] = g_near + skip[:, cols] * dy
        dot_ref[:, cols] = dy * y_near - x_val * g_near
    w_up = jnp.concatenate([w_left, w_right], axis=1)
    low_part = mm2(w_right.T, b_val[:HALF]) + mm2(w_low.T, b_val[HALF:])
    gc_ref[...] = far + jnp.concatenate([mm2(w_left.T, b_val[:HALF]), low_part], axis=0)
    outs = fetch([(gc_ref, gc_hbm), (gz_ref, gz_hbm)], sems)
    gl_ref[...] = mm_by(segment(dot_ref[...], spread), triangle(length, lambda i, j: i >= j))
    gb_ref[:HALF, :] = mm2(w_up, c_val)
    gb_ref[HALF:, :] = mm2(w_low, c_val[HALF:])
    hi, mid, lo = split3(jnp.broadcast_to(jnp.concatenate(skips, axis=1), (8, width)))
    wide = head_map(HALF, width)
    skip_ref[...] = mm(hi, wide, 1, 1) + mm(mid, wide, 1, 1) + mm(lo, wide, 1, 1)
    for copy in outs:
        copy.wait()


def suffix_kernel(in_ref, dec_ref, skip_ref, out_ref):
    count = dec_ref.shape[0]
    state = jnp.zeros((32, HALF), F32)
    sums = in_ref[32:33, :]
    for p in range(1, count):
        sums = sums + in_ref[33 * p + 32 : 33 * p + 33, :]
    rows = jnp.concatenate([sums, skip_ref[0:1, :]], axis=0)
    for p in range(count - 1, -1, -1):
        out_ref[34 * p : 34 * p + 32, :] = state
        out_ref[34 * p + 32 : 34 * p + 34, :] = rows
        if p > 0:
            state = dec_ref[p : p + 1, :] * state + in_ref[33 * p : 33 * p + 32, :]


def final_kernel(
    a_ref, s_hbm, lt_hbm, tail_ref, x_ref, b_ref, gx_ref, gb_ref, gl_ref,
    ox_hbm, ob_hbm, ol_hbm, skip_hbm, weight_hbm, ox_ref, ob_ref, ol_ref, skip_ref, weight_ref, lt_ref, s_ref, sems,
):
    heads, length = lt_hbm.shape
    width = x_ref.shape[1]
    spread = head_map(heads, width)
    outs = [(weight_ref, weight_hbm), (skip_ref, skip_hbm), (ol_ref, ol_hbm), (ob_ref, ob_hbm), (ox_ref, ox_hbm)]
    copies = copies_of(outs + [(lt_hbm, lt_ref), (s_hbm, s_ref)], sems)
    copies[6].start()
    copies[5].start()
    after = load_state(a_ref, 34)
    tail, x_val = tail_ref[...], x_ref[...].astype(F32)
    b_after = mm_split(b_ref[...], after) * tail
    ox_ref[...] = (gx_ref[...] + b_after).astype(BF16)
    copies[4].start()
    late = segment(x_val * b_after, spread)
    x_hi, x_lo = split2(x_val * tail)
    a_hi, a_lo = split2(after.T)
    both = mm(x_hi, jnp.concatenate([a_hi, a_lo], axis=1))
    ob_ref[...] = gb_ref[...] + both[:, :HALF] + both[:, HALF:] + mm(x_lo, a_hi)
    copies[3].start()
    weight_ref[...] = jnp.concatenate([a_ref[136 * q + 32 : 136 * q + 33, :] for q in range(8)], axis=0)
    skip = a_ref[33:34, :]
    for p in range(1, a_ref.shape[0] // 34):
        skip = skip + a_ref[34 * p + 33 : 34 * p + 34, :]
    skip_ref[...] = skip[:, :heads]
    copies[0].start()
    copies[1].start()
    copies[5].wait()
    copies[6].wait()
    start = jnp.sum(load_state(s_ref, 32) * after, axis=0, keepdims=True)
    mine = iota((heads, width), 1) // P_SIZE == iota((heads, width), 0)
    start = jnp.sum(jnp.where(mine, start, 0.0), axis=1, keepdims=True)
    whole = jnp.exp(jnp.sum(lt_ref[...], axis=1, keepdims=True))
    ol_ref[...] = gl_ref[...] + mm_by(late, triangle(length, lambda i, j: i < j)) + whole * start
    copies[2].start()
    for copy in copies[:5]:
        copy.wait()


def call(kernel, name, outs, *args, flops=0, scratch=(), hbm_in=(), hbm_out=(), mib=16):
    nbytes = sum(a.size * a.dtype.itemsize for a in (*args, *outs))
    spaces = [pltpu.HBM if i in hbm_in else pltpu.VMEM for i in range(len(args))]
    out_spaces = [pltpu.HBM if i in hbm_out else pltpu.VMEM for i in range(len(outs))]
    return pl.pallas_call(
        kernel,
        name=name,
        out_shape=[space(o.shape, o.dtype) for space, o in zip(out_spaces, outs)],
        in_specs=[pl.BlockSpec(memory_space=space) for space in spaces],
        out_specs=[pl.BlockSpec(memory_space=space) for space in out_spaces],
        scratch_shapes=list(scratch),
        compiler_params=pltpu.CompilerParams(vmem_limit_bytes=mib * 1024 * 1024),
        cost_estimate=pl.CostEstimate(flops=flops, bytes_accessed=nbytes, transcendentals=0),
    )(*[pltpu.with_memory_space_constraint(a, space) for a, space in zip(args, spaces)])


def exchange(messages, rows):
    count = lax.axis_size(CHUNKS)
    got = lax.all_to_all(messages.reshape(count, 1, rows * HALF), CHUNKS, 0, 0)
    return got.reshape(count * rows, HALF)


def on_device(x_in, b_in, c_in, decay_log, d_skip, gate, norm_weight, d_out):
    length, heads = decay_log.shape
    width = x_in.shape[1]
    chunks = lax.axis_size(CHUNKS)
    groups = lax.axis_size("heads")
    shape = jax.ShapeDtypeStruct
    wide = shape((length, width), F32)
    half_wide = shape((length, width), BF16)
    small = shape((heads, length), F32)
    narrow = shape(b_in.shape, F32)
    half_narrow = shape(b_in.shape, BF16)
    state = shape((chunks * 32, HALF), F32)
    weight = norm_weight.reshape(1, width)
    d_row = d_skip.reshape(1, heads)
    w_row, one_row = shape(weight.shape, F32), shape(d_row.shape, F32)
    decay_t = decay_log.T
    sem = pltpu.SemaphoreType.DMA

    def vmem(*shapes):
        return [pltpu.VMEM(s.shape, s.dtype) for s in shapes]

    (pay,) = call(
        start_kernel, "start", [shape((chunks * 33, HALF), F32)], decay_t, x_in, b_in,
        flops=10**9, scratch=vmem(small, half_narrow, half_wide) + [sem((3,))], hbm_in=(0, 1, 2),
    )
    got = exchange(pay, 33)
    base, esilu, c_val, c_turned, w_val, dout_val, y_near = call(
        local_kernel, "local", [wide, wide, half_narrow, shape(c_in.shape[::-1], BF16), w_row, half_wide, wide],
        decay_t, x_in, b_in, c_in, gate, d_row, weight, d_out,
        flops=8 * 10**9, hbm_in=range(8), hbm_out=(6,), mib=24,
        scratch=vmem(small, half_wide, half_narrow, half_wide, one_row, wide) + [sem((9,))],
    )
    spread, decays = call(prefix_kernel, "prefix", [state, shape((chunks, HALF), F32)], got)
    before = exchange(spread, 32)
    gated, sums = call(
        gate_kernel, "gated", [wide, shape((groups, 8, length), F32)],
        before, c_val, base, esilu, dout_val, w_val, flops=10**9,
    )
    sums = lax.all_to_all(sums, "heads", 0, 0)

    def back(*refs):
        back_kernel(float(width * groups), *refs)

    rows = shape((8, length), F32)
    pay, scalars, before = call(
        back, "back", [shape((chunks * 33, HALF), F32), rows, state],
        sums, gated, esilu, dout_val, w_val, c_turned, before,
        flops=10**9, hbm_out=(1, 2), scratch=vmem(rows) + [sem((2,))],
    )
    got = exchange(pay, 33)
    gx, gb, gl, tail, x_val, b_val, skip, grad_gate, grad_c = call(
        grads_kernel, "grads",
        [wide, narrow, small, wide, half_wide, half_narrow, shape((8, HALF), F32), half_wide, narrow],
        decay_t, scalars, d_out, weight, x_in, gate, b_in, c_in, d_row, y_near, before,
        flops=16 * 10**9, hbm_in=range(11), hbm_out=(7, 8), mib=32,
        scratch=vmem(state, small, rows, half_wide, w_row, half_wide, half_narrow, one_row, wide, wide, wide, half_wide, narrow)
        + [sem((16,))],
    )
    (spread,) = call(suffix_kernel, "suffix", [shape((chunks * 34, HALF), F32)], got, decays, skip)
    after = exchange(spread, 34)
    outs = [half_wide, narrow, small, one_row, shape((8, HALF), F32)]
    grad_x, grad_b, grad_decay, grad_skip, grad_weight = call(
        final_kernel, "final", outs,
        after, before, decay_t, tail, x_val, b_val, gx, gb, gl,
        flops=2 * 10**9, scratch=vmem(*outs, small, state) + [sem((7,))], hbm_in=(1, 2), hbm_out=range(5),
    )
    return (
        grad_x,
        grad_b,
        grad_c,
        grad_decay.T,
        grad_skip.reshape(heads),
        grad_gate,
        grad_weight.reshape(width),
    )


def solution(mesh):
    tokens = P(CHUNKS, "heads")
    in_specs = (tokens, tokens, tokens, tokens, P("heads"), tokens, P("heads"), tokens)
    out_specs = (tokens, tokens, tokens, tokens, P("heads"), tokens, P("heads"))
    return jax.shard_map(on_device, mesh=mesh, in_specs=in_specs, out_specs=out_specs, check_vma=False)
```

```python
import jax
import jax.numpy as jnp
from jax import lax
from jax.experimental import pallas as pl
from jax.experimental.pallas import tpu as pltpu
from jax.sharding import PartitionSpec as P

P_SIZE = 64
EPS = 1e-05
F32 = jnp.float32
BF16 = jnp.bfloat16
CHUNKS = ("outer", "inner")
HALF = 128


def mm(a, b, ca=1, cb=0):
    return lax.dot_general(a, b, (((ca,), (cb,)), ((), ())), preferred_element_type=F32)


def split2(a):
    hi = a.astype(BF16)
    return hi, (a - hi.astype(F32)).astype(BF16)


def split3(a):
    hi = a.astype(BF16)
    rest = a - hi.astype(F32)
    mid = rest.astype(BF16)
    return hi, mid, (rest - mid.astype(F32)).astype(BF16)


def mm2(a, b, ca=1, cb=0):
    hi, lo = split2(a)
    return mm(hi, b, ca, cb) + mm(lo, b, ca, cb)


def mm_split(a, b):
    return mm(jnp.concatenate([a, a], axis=1), jnp.concatenate(split2(b), axis=0))


def iota(shape, dim):
    return lax.broadcasted_iota(jnp.int32, shape, dim)


def head_map(heads, width):
    return jnp.where(iota((heads, width), 1) // P_SIZE == iota((heads, width), 0), 1.0, 0.0).astype(BF16)


def expand(a, spread, rows=None):
    hi, lo = split2(a)
    both = jnp.concatenate([hi.astype(F32), lo.astype(F32)], axis=0).T.astype(BF16)
    return mm(both[:rows], jnp.concatenate([spread, spread], axis=0))


def segment(a, spread):
    turned_map = turned(spread)
    hi, lo = split2(a)
    return (mm(hi, turned_map) + mm(lo, turned_map)).T


def triangle(n, keep):
    return jnp.where(keep(iota((n, n), 0), iota((n, n), 1)), 1.0, 0.0).astype(BF16)


def mm_by(a, tri):
    rows = a.shape[0]
    got = mm(jnp.concatenate(split3(a), axis=0), tri)
    return got[:rows] + got[rows : 2 * rows] + got[2 * rows :]


def load_state(ref, rows):
    return jnp.concatenate([load_block(ref, rows, k) for k in range(4)], axis=1)


def load_block(ref, rows, k):
    cols = []
    for q in (2 * k, 2 * k + 1):
        at = [rows * (4 * q + r) for r in range(4)]
        cols.append(jnp.concatenate([ref[i : i + 32, :] for i in at], axis=0))
    return jnp.concatenate(cols, axis=1)


def copies_of(pairs, sems):
    return [pltpu.make_async_copy(src, dst, sems.at[i]) for i, (src, dst) in enumerate(pairs)]


def fetch(pairs, sems):
    copies = copies_of(pairs, sems)
    for copy in copies:
        copy.start()
    return copies


def quarters(ref):
    return [ref.at[:, pl.ds(256 * k, 256)] for k in range(4)]


def turned(a):
    return a.astype(F32).T.astype(BF16)


def block_sums(lt):
    return mm_by(lt, triangle(lt.shape[1], lambda i, j: i <= j))


def below(up, zeros, left, right, i):
    return jnp.concatenate(
        [jnp.concatenate([up[i], zeros], axis=1), jnp.concatenate([left[i], right[i]], axis=1)], axis=0
    )


def skip_row(d_ref, spread):
    heads, width = spread.shape
    hi, mid, lo = split3(jnp.broadcast_to(d_ref[...], (8, heads)))
    return (mm(hi, spread) + mm(mid, spread) + mm(lo, spread))[0:1, :]


def start_kernel(lt_hbm, x_hbm, b_hbm, pay_ref, lt_ref, b_ref, x_ref, sems):
    heads, length = lt_hbm.shape
    width = x_hbm.shape[1]
    first, second, third = fetch([(lt_hbm, lt_ref), (b_hbm, b_ref), (x_hbm, x_ref)], sems)
    second.wait()
    b_turned = b_ref[...].astype(F32).T
    first.wait()
    cum = block_sums(lt_ref[...])
    last = cum[:, length - 1 : length]
    ends = jnp.concatenate([last - cum, jnp.broadcast_to(last, (heads, HALF))], axis=1)
    tail = expand(jnp.exp(ends), head_map(heads, width), length + 16)
    whole = tail[length : length + 1, :]
    third.wait()
    state = mm_split(b_turned.astype(BF16), x_ref[...].astype(F32) * tail[:length])
    for q in range(width // HALF):
        for r in range(4):
            at = 33 * (4 * q + r)
            pay_ref[at : at + 32, :] = state[32 * r : 32 * r + 32, HALF * q : HALF * (q + 1)]
            pay_ref[at + 32 : at + 33, :] = whole[:, HALF * q : HALF * (q + 1)]


def local_kernel(
    lt_hbm, x_hbm, b_hbm, c_hbm, z_hbm, d_hbm, w_hbm, dout_hbm,
    base_ref, esilu_ref, c_ref, ct_ref, w_ref, dout_ref, yn_hbm,
    lt_ref, x_ref, b_ref, z_ref, d_ref, yn_ref, sems,
):
    heads, length = lt_hbm.shape
    width = x_hbm.shape[1]
    copies = fetch(
        [(lt_hbm, lt_ref), (b_hbm, b_ref), (c_hbm, c_ref), (x_hbm, x_ref), (z_hbm, z_ref), (d_hbm, d_ref),
         (w_hbm, w_ref), (dout_hbm, dout_ref)],
        sems,
    )
    spread = head_map(heads, width)
    for copy in copies[:3]:
        copy.wait()
    cum_t = block_sums(lt_ref[...])
    cum = cum_t.T
    ecum = expand(jnp.exp(cum_t), spread)
    ct_ref[...] = turned(c_ref[...])
    inner = mm(c_ref[...], b_ref[...], 1, 1)
    top, left, right = inner[:HALF, :HALF], inner[HALF:, :HALF], inner[HALF:, HALF:]
    lower = iota((HALF, HALF), 0) >= iota((HALF, HALF), 1)
    first = iota((length, HALF), 1) < P_SIZE
    zeros = jnp.zeros((HALF, HALF), BF16)
    for copy in copies[3:6]:
        copy.wait()
    skip = skip_row(d_ref, spread)
    for q in range(width // HALF):
        cols = slice(HALF * q, HALF * (q + 1))
        x_pair = x_ref[:, cols]
        mixes = []
        for h in (2 * q, 2 * q + 1):
            col, row = cum[:, h : h + 1], cum_t[h : h + 1, :]
            up = jnp.where(lower, jnp.exp(col[:HALF] - row[:, :HALF]), 0.0) * top
            dl = jnp.exp(col[HALF:] - row[:, :HALF]) * left
            dr = jnp.where(lower, jnp.exp(col[HALF:] - row[:, HALF:]), 0.0) * right
            mixes += [below(split2(up), zeros, split2(dl), split2(dr), i) for i in range(2)]
        got = mm(jnp.concatenate(mixes, axis=0), x_pair)
        yn = jnp.where(
            first, got[:length] + got[length : 2 * length], got[2 * length : 3 * length] + got[3 * length :]
        )
        yn_ref[:, cols] = yn
        z_val = z_ref[:, cols].astype(F32)
        silu = z_val * (1.0 / (1.0 + jnp.exp(-z_val)))
        esilu_ref[:, cols] = ecum[:, cols] * silu
        base_ref[:, cols] = (yn + skip[:, cols] * x_pair.astype(F32)) * silu
    for copy in copies[6:]:
        copy.wait()
    yn_copy = pltpu.make_async_copy(yn_ref, yn_hbm, sems.at[8])
    yn_copy.start()
    yn_copy.wait()


def prefix_kernel(in_ref, out_ref, dec_ref):
    count = dec_ref.shape[0]
    state = jnp.zeros((32, HALF), F32)
    for p in range(count):
        out_ref[32 * p : 32 * p + 32, :] = state
        decay = in_ref[33 * p + 32 : 33 * p + 33, :]
        dec_ref[p : p + 1, :] = decay
        if p < count - 1:
            state = decay * state + in_ref[33 * p : 33 * p + 32, :]


def gate_kernel(s_ref, c_ref, base_ref, esilu_ref, dout_ref, w_ref, gated_ref, sums_ref):
    c_val = c_ref[...]
    length, width = base_ref.shape
    squares = jnp.zeros((length, HALF), F32)
    products = jnp.zeros((length, HALF), F32)
    for q in range(width // 256):
        big = slice(256 * q, 256 * (q + 1))
        c_state = mm_split(c_val, load_block(s_ref, 32, q))
        gated = base_ref[:, big] + esilu_ref[:, big] * c_state
        gated_ref[:, big] = gated
        sq = gated * gated
        pr = dout_ref[:, big].astype(F32) * w_ref[:, big] * gated
        squares = squares + sq[:, :HALF] + sq[:, HALF:]
        products = products + pr[:, :HALF] + pr[:, HALF:]
    rows = [jnp.sum(total.T, axis=0, keepdims=True) for total in (squares, products)]
    tile = jnp.concatenate([row[:, HALF * i : HALF * (i + 1)] for row in rows for i in range(2)], axis=0)
    sums_ref[...] = jnp.concatenate([tile] * (sums_ref.shape[0] // 4), axis=0)


def columns(rows):
    turned_rows = jnp.concatenate([rows, jnp.zeros((HALF - 8, HALF), F32)], axis=0).T
    return [jnp.concatenate([turned_rows[:, i : i + 1], turned_rows[:, i + 1 : i + 2]], axis=0) for i in (0, 2)]


def back_kernel(
    channels, sums_ref, gated_ref, esilu_ref, dout_ref, w_ref, ct_ref, s_ref,
    pay_hbm, scal_hbm, s_hbm, scal_ref, pay_ref, sems,
):
    length, width = gated_ref.shape
    scal_copy, s_copy = copies_of([(scal_ref, scal_hbm), (s_ref, s_hbm)], sems)
    s_copy.start()
    total = sums_ref[0:4, :]
    for i in range(1, sums_ref.shape[0] // 4):
        total = total + sums_ref[4 * i : 4 * i + 4, :]
    inv = lax.rsqrt(total[0:2] / channels + EPS)
    fall = inv * inv * inv * total[2:4] / channels
    rows = jnp.concatenate([inv, fall, jnp.zeros((4, HALF), F32)], axis=0)
    scal_ref[...] = rows
    scal_copy.start()
    inv_col, fall_col = columns(rows)
    outs = []
    c_turned = ct_ref[...]
    for k in range(width // 256):
        big = slice(256 * k, 256 * (k + 1))
        gated = gated_ref[:, big]
        d_inv = dout_ref[:, big].astype(F32) * inv_col
        weight = jnp.sum(d_inv * gated, axis=0, keepdims=True)
        back = mm_split(c_turned, (d_inv * w_ref[:, big] - gated * fall_col) * esilu_ref[:, big])
        for q in (2 * k, 2 * k + 1):
            off = HALF * (q - 2 * k)
            for r in range(4):
                at = 33 * (4 * q + r)
                pay_ref[at : at + 32, :] = back[32 * r : 32 * r + 32, off : off + HALF]
                pay_ref[at + 32 : at + 33, :] = weight[:, off : off + HALF]
        if k % 2 == 1:
            rows = pl.ds(528 * (k // 2), 528)
            outs.append(pltpu.make_async_copy(pay_ref.at[rows], pay_hbm.at[rows], sems.at[2 + k]))
            outs[-1].start()
    for copy in outs:
        copy.wait()
    scal_copy.wait()
    s_copy.wait()


def grads_kernel(
    lt_hbm, scal_hbm, dout_hbm, w_hbm, x_hbm, z_hbm, b_hbm, c_hbm, d_hbm, yn_hbm, s_hbm,
    gx_ref, gb_ref, gl_ref, tail_ref, x_ref, b_ref, skip_ref, gz_hbm, gc_hbm,
    s_ref, lt_ref, scal_ref, dout_ref, w_ref, z_ref, c_ref, d_ref, yn_ref, dye_ref, dot_ref, gz_ref, gc_ref, sems,
):
    heads, length = lt_hbm.shape
    width = x_hbm.shape[1]
    copies = fetch(
        [(lt_hbm, lt_ref), (scal_hbm, scal_ref), (b_hbm, b_ref), (c_hbm, c_ref), (d_hbm, d_ref), (w_hbm, w_ref),
         (x_hbm, x_ref), (s_hbm, s_ref), (yn_hbm, yn_ref), (z_hbm, z_ref), (dout_hbm, dout_ref)],
        sems,
    )
    spread = head_map(heads, width)
    for copy in copies[:6]:
        copy.wait()
    cum_t = block_sums(lt_ref[...])
    cum = cum_t.T
    last = cum_t[:, length - 1 : length]
    ecum = expand(jnp.exp(cum_t), spread)
    tail_ref[...] = expand(jnp.exp(last - cum_t), spread)
    inv_col, fall_col = columns(scal_ref[...])
    skip = skip_row(d_ref, spread)
    b_val, c_val = b_ref[...], c_ref[...]
    inner_t = mm(b_val, c_val, 1, 1)
    left, right, low = inner_t[:HALF, :HALF], inner_t[:HALF, HALF:], inner_t[HALF:, HALF:]
    upper = iota((HALF, HALF), 0) <= iota((HALF, HALF), 1)
    first = iota((length, HALF), 1) < P_SIZE
    zeros = jnp.zeros((HALF, HALF), BF16)
    w_left = jnp.zeros((HALF, HALF), F32)
    w_right = jnp.zeros((HALF, HALF), F32)
    w_low = jnp.zeros((HALF, HALF), F32)
    skips = []
    far = jnp.zeros((length, HALF), F32)
    for copy in copies[6:]:
        copy.wait()
    for q in range(width // HALF):
        cols = slice(HALF * q, HALF * (q + 1))
        x_pair = x_ref[:, cols]
        x_val = x_pair.astype(F32)
        z_val = z_ref[:, cols].astype(F32)
        sig = 1.0 / (1.0 + jnp.exp(-z_val))
        silu = z_val * sig
        if q % 2 == 0:
            state = load_block(s_ref, 32, q // 2)
            c_state = mm_split(c_val, state)
        off = slice(HALF * (q % 2), HALF * (q % 2 + 1))
        y_near = yn_ref[:, cols] + ecum[:, cols] * c_state[:, off]
        y_val = y_near + skip[:, cols] * x_val
        d_gated = inv_col * (dout_ref[:, cols].astype(F32) * w_ref[:, cols]) - y_val * silu * fall_col
        dy = d_gated * silu
        dye_ref[:, cols] = dy * ecum[:, cols]
        gz_ref[:, cols] = (d_gated * y_val * sig * (1.0 + z_val * (1.0 - sig))).astype(BF16)
        if q % 2 == 1:
            e_hi, e_lo = split2(dye_ref[:, 128 * q - 128 : 128 * q + 128])
            both = mm(jnp.concatenate([e_hi, e_lo], axis=0), jnp.concatenate(split2(state.T), axis=1))
            far = far + both[:length, :HALF] + both[:length, HALF:] + both[length:, :HALF]
        skips.append(jnp.sum(dy * x_val, axis=0, keepdims=True))
        hi, lo = split2(dy)
        ones = jnp.concatenate([jnp.where(first, x_val, 0.0), jnp.where(first, 0.0, x_val)], axis=0).astype(BF16)
        both = jnp.concatenate([hi, lo], axis=1)
        dots = mm(jnp.concatenate([ones, ones], axis=1), both, 1, 1)
        mix_hi, mix_lo = [], []
        for k in range(2):
            h = 2 * q + k
            col, row = cum[:, h : h + 1], cum_t[h : h + 1, :]
            dot = dots[length * k : length * (k + 1)]
            dec_left = jnp.where(upper, jnp.exp(row[:, :HALF] - col[:HALF]), 0.0)
            dec_right = jnp.exp(row[:, HALF:] - col[:HALF])
            dec_low = jnp.where(upper, jnp.exp(row[:, HALF:] - col[HALF:]), 0.0)
            w_left = w_left + dec_left * dot[:HALF, :HALF]
            w_right = w_right + dec_right * dot[:HALF, HALF:]
            w_low = w_low + dec_low * dot[HALF:, HALF:]
            blocks = [split2(m) for m in (dec_left * left, dec_right * right, dec_low * low)]
            for i, mix in enumerate((mix_hi, mix_lo)):
                up = jnp.concatenate([blocks[0][i], blocks[1][i]], axis=1)
                mix.append(jnp.concatenate([up, jnp.concatenate([zeros, blocks[2][i]], axis=1)], axis=0))
        got = mm(jnp.concatenate(mix_hi + mix_lo, axis=0), both)
        got = got[: 2 * length, :HALF] + got[: 2 * length, HALF:] + got[2 * length :, :HALF]
        g_near = jnp.where(first, got[:length], got[length:])
        gx_ref[:, cols] = g_near + skip[:, cols] * dy
        dot_ref[:, cols] = dy * y_near - x_val * g_near
    w_up = jnp.concatenate([w_left, w_right], axis=1)
    low_part = mm2(w_right.T, b_val[:HALF]) + mm2(w_low.T, b_val[HALF:])
    gc_ref[...] = far + jnp.concatenate([mm2(w_left.T, b_val[:HALF]), low_part], axis=0)
    outs = fetch([(gc_ref, gc_hbm), (gz_ref, gz_hbm)], sems)
    gl_ref[...] = mm_by(segment(dot_ref[...], spread), triangle(length, lambda i, j: i >= j))
    gb_ref[:HALF, :] = mm2(w_up, c_val)
    gb_ref[HALF:, :] = mm2(w_low, c_val[HALF:])
    hi, mid, lo = split3(jnp.broadcast_to(jnp.concatenate(skips, axis=1), (8, width)))
    wide = head_map(HALF, width)
    skip_ref[...] = mm(hi, wide, 1, 1) + mm(mid, wide, 1, 1) + mm(lo, wide, 1, 1)
    for copy in outs:
        copy.wait()


def suffix_kernel(in_ref, dec_ref, skip_ref, out_ref):
    count = dec_ref.shape[0]
    state = jnp.zeros((32, HALF), F32)
    sums = in_ref[32:33, :]
    for p in range(1, count):
        sums = sums + in_ref[33 * p + 32 : 33 * p + 33, :]
    rows = jnp.concatenate([sums, skip_ref[0:1, :]], axis=0)
    for p in range(count - 1, -1, -1):
        out_ref[34 * p : 34 * p + 32, :] = state
        out_ref[34 * p + 32 : 34 * p + 34, :] = rows
        if p > 0:
            state = dec_ref[p : p + 1, :] * state + in_ref[33 * p : 33 * p + 32, :]


def final_kernel(
    a_ref, s_hbm, lt_hbm, tail_ref, x_ref, b_ref, gx_ref, gb_ref, gl_ref,
    ox_hbm, ob_hbm, ol_hbm, skip_hbm, weight_hbm, ox_ref, ob_ref, ol_ref, skip_ref, weight_ref, lt_ref, s_ref, sems,
):
    heads, length = lt_hbm.shape
    width = x_ref.shape[1]
    spread = head_map(heads, width)
    outs = [(weight_ref, weight_hbm), (skip_ref, skip_hbm), (ol_ref, ol_hbm), (ob_ref, ob_hbm), (ox_ref, ox_hbm)]
    copies = copies_of(outs + [(lt_hbm, lt_ref), (s_hbm, s_ref)], sems)
    copies[6].start()
    copies[5].start()
    after = load_state(a_ref, 34)
    tail, x_val = tail_ref[...], x_ref[...].astype(F32)
    b_after = mm_split(b_ref[...], after) * tail
    ox_ref[...] = (gx_ref[...] + b_after).astype(BF16)
    copies[4].start()
    late = segment(x_val * b_after, spread)
    x_hi, x_lo = split2(x_val * tail)
    a_hi, a_lo = split2(after.T)
    both = mm(x_hi, jnp.concatenate([a_hi, a_lo], axis=1))
    ob_ref[...] = gb_ref[...] + both[:, :HALF] + both[:, HALF:] + mm(x_lo, a_hi)
    copies[3].start()
    weight_ref[...] = jnp.concatenate([a_ref[136 * q + 32 : 136 * q + 33, :] for q in range(8)], axis=0)
    skip = a_ref[33:34, :]
    for p in range(1, a_ref.shape[0] // 34):
        skip = skip + a_ref[34 * p + 33 : 34 * p + 34, :]
    skip_ref[...] = skip[:, :heads]
    copies[0].start()
    copies[1].start()
    copies[5].wait()
    copies[6].wait()
    start = jnp.sum(load_state(s_ref, 32) * after, axis=0, keepdims=True)
    mine = iota((heads, width), 1) // P_SIZE == iota((heads, width), 0)
    start = jnp.sum(jnp.where(mine, start, 0.0), axis=1, keepdims=True)
    whole = jnp.exp(jnp.sum(lt_ref[...], axis=1, keepdims=True))
    ol_ref[...] = gl_ref[...] + mm_by(late, triangle(length, lambda i, j: i < j)) + whole * start
    copies[2].start()
    for copy in copies[:5]:
        copy.wait()


def call(kernel, name, outs, *args, flops=0, scratch=(), hbm_in=(), hbm_out=(), mib=16):
    nbytes = sum(a.size * a.dtype.itemsize for a in (*args, *outs))
    spaces = [pltpu.HBM if i in hbm_in else pltpu.VMEM for i in range(len(args))]
    out_spaces = [pltpu.HBM if i in hbm_out else pltpu.VMEM for i in range(len(outs))]
    return pl.pallas_call(
        kernel,
        name=name,
        out_shape=[space(o.shape, o.dtype) for space, o in zip(out_spaces, outs)],
        in_specs=[pl.BlockSpec(memory_space=space) for space in spaces],
        out_specs=[pl.BlockSpec(memory_space=space) for space in out_spaces],
        scratch_shapes=list(scratch),
        compiler_params=pltpu.CompilerParams(vmem_limit_bytes=mib * 1024 * 1024),
        cost_estimate=pl.CostEstimate(flops=flops, bytes_accessed=nbytes, transcendentals=0),
    )(*[pltpu.with_memory_space_constraint(a, space) for a, space in zip(args, spaces)])


def exchange(messages, rows, axes=CHUNKS):
    count = lax.axis_size(axes)
    got = lax.all_to_all(messages.reshape(count, 1, rows * HALF), axes, 0, 0)
    return got.reshape(count * rows, HALF)


def on_device(x_in, b_in, c_in, decay_log, d_skip, gate, norm_weight, d_out):
    length, heads = decay_log.shape
    width = x_in.shape[1]
    chunks = lax.axis_size(CHUNKS)
    groups = lax.axis_size("heads")
    shape = jax.ShapeDtypeStruct
    wide = shape((length, width), F32)
    half_wide = shape((length, width), BF16)
    small = shape((heads, length), F32)
    narrow = shape(b_in.shape, F32)
    half_narrow = shape(b_in.shape, BF16)
    state = shape((chunks * 32, HALF), F32)
    weight = norm_weight.reshape(1, width)
    d_row = d_skip.reshape(1, heads)
    w_row, one_row = shape(weight.shape, F32), shape(d_row.shape, F32)
    decay_t = decay_log.T
    sem = pltpu.SemaphoreType.DMA

    def vmem(*shapes):
        return [pltpu.VMEM(s.shape, s.dtype) for s in shapes]

    (pay,) = call(
        start_kernel, "start", [shape((chunks * 33, HALF), F32)], decay_t, x_in, b_in,
        flops=10**9, scratch=vmem(small, half_narrow, half_wide) + [sem((3,))], hbm_in=(0, 1, 2),
    )
    got = exchange(pay, 33)
    base, esilu, c_val, c_turned, w_val, dout_val, y_near = call(
        local_kernel, "local", [wide, wide, half_narrow, shape(c_in.shape[::-1], BF16), w_row, half_wide, wide],
        decay_t, x_in, b_in, c_in, gate, d_row, weight, d_out,
        flops=8 * 10**9, hbm_in=range(8), hbm_out=(6,), mib=24,
        scratch=vmem(small, half_wide, half_narrow, half_wide, one_row, wide) + [sem((9,))],
    )
    spread, decays = call(prefix_kernel, "prefix", [state, shape((chunks, HALF), F32)], got)
    before = exchange(spread, 32)
    gated, sums = call(
        gate_kernel, "gated", [wide, shape((groups * 4, HALF), F32)],
        before, c_val, base, esilu, dout_val, w_val, flops=10**9,
    )
    sums = exchange(sums, 4, "heads")

    def back(*refs):
        back_kernel(float(width * groups), *refs)

    rows = shape((8, HALF), F32)
    pay, scalars, before = call(
        back, "back", [shape((chunks * 33, HALF), F32), rows, state],
        sums, gated, esilu, dout_val, w_val, c_turned, before,
        flops=10**9, hbm_out=(0, 1, 2), scratch=vmem(rows, shape((chunks * 33, HALF), F32)) + [sem((6,))],
    )
    got = exchange(pay, 33)
    gx, gb, gl, tail, x_val, b_val, skip, grad_gate, grad_c = call(
        grads_kernel, "grads",
        [wide, narrow, small, wide, half_wide, half_narrow, shape((8, HALF), F32), half_wide, narrow],
        decay_t, scalars, d_out, weight, x_in, gate, b_in, c_in, d_row, y_near, before,
        flops=16 * 10**9, hbm_in=range(11), hbm_out=(7, 8), mib=32,
        scratch=vmem(state, small, rows, half_wide, w_row, half_wide, half_narrow, one_row, wide, wide, wide, half_wide, narrow)
        + [sem((16,))],
    )
    (spread,) = call(suffix_kernel, "suffix", [shape((chunks * 34, HALF), F32)], got, decays, skip)
    after = exchange(spread, 34)
    outs = [half_wide, narrow, small, one_row, shape((8, HALF), F32)]
    grad_x, grad_b, grad_decay, grad_skip, grad_weight = call(
        final_kernel, "final", outs,
        after, before, decay_t, tail, x_val, b_val, gx, gb, gl,
        flops=2 * 10**9, scratch=vmem(*outs, small, state) + [sem((7,))], hbm_in=(1, 2), hbm_out=range(5),
    )
    return (
        grad_x,
        grad_b,
        grad_c,
        grad_decay.T,
        grad_skip.reshape(heads),
        grad_gate,
        grad_weight.reshape(width),
    )


def solution(mesh):
    tokens = P(CHUNKS, "heads")
    in_specs = (tokens, tokens, tokens, tokens, P("heads"), tokens, P("heads"), tokens)
    out_specs = (tokens, tokens, tokens, tokens, P("heads"), tokens, P("heads"))
    return jax.shard_map(on_device, mesh=mesh, in_specs=in_specs, out_specs=out_specs, check_vma=False)
```

```python
import jax
import jax.numpy as jnp
from jax import lax
from jax.experimental import pallas as pl
from jax.experimental.pallas import tpu as pltpu
from jax.sharding import PartitionSpec as P

P_SIZE = 64
EPS = 1e-05
F32 = jnp.float32
BF16 = jnp.bfloat16
CHUNKS = ("outer", "inner")
HALF = 128


def mm(a, b, ca=1, cb=0):
    return lax.dot_general(a, b, (((ca,), (cb,)), ((), ())), preferred_element_type=F32)


def split2(a):
    hi = a.astype(BF16)
    return hi, (a - hi.astype(F32)).astype(BF16)


def split3(a):
    hi = a.astype(BF16)
    rest = a - hi.astype(F32)
    mid = rest.astype(BF16)
    return hi, mid, (rest - mid.astype(F32)).astype(BF16)


def mm2(a, b, ca=1, cb=0):
    hi, lo = split2(a)
    return mm(hi, b, ca, cb) + mm(lo, b, ca, cb)


def mm_split(a, b):
    return mm(jnp.concatenate([a, a], axis=1), jnp.concatenate(split2(b), axis=0))


def iota(shape, dim):
    return lax.broadcasted_iota(jnp.int32, shape, dim)


def head_map(heads, width):
    return jnp.where(iota((heads, width), 1) // P_SIZE == iota((heads, width), 0), 1.0, 0.0).astype(BF16)


def expand(a, spread, rows=None):
    hi, lo = split2(a)
    both = jnp.concatenate([hi.astype(F32), lo.astype(F32)], axis=0).T.astype(BF16)
    return mm(both[:rows], jnp.concatenate([spread, spread], axis=0))


def segment(a, spread):
    turned_map = turned(spread)
    hi, lo = split2(a)
    return (mm(hi, turned_map) + mm(lo, turned_map)).T


def triangle(n, keep):
    return jnp.where(keep(iota((n, n), 0), iota((n, n), 1)), 1.0, 0.0).astype(BF16)


def mm_by(a, tri):
    rows = a.shape[0]
    got = mm(jnp.concatenate(split3(a), axis=0), tri)
    return got[:rows] + got[rows : 2 * rows] + got[2 * rows :]


def load_state(ref, rows):
    return jnp.concatenate([load_block(ref, rows, k) for k in range(4)], axis=1)


def load_block(ref, rows, k):
    cols = []
    for q in (2 * k, 2 * k + 1):
        at = [rows * (4 * q + r) for r in range(4)]
        cols.append(jnp.concatenate([ref[i : i + 32, :] for i in at], axis=0))
    return jnp.concatenate(cols, axis=1)


def copies_of(pairs, sems):
    return [pltpu.make_async_copy(src, dst, sems.at[i]) for i, (src, dst) in enumerate(pairs)]


def fetch(pairs, sems):
    copies = copies_of(pairs, sems)
    for copy in copies:
        copy.start()
    return copies


def quarters(ref):
    return [ref.at[:, pl.ds(256 * k, 256)] for k in range(4)]


def turned(a):
    return a.astype(F32).T.astype(BF16)


def block_sums(lt):
    return mm_by(lt, triangle(lt.shape[1], lambda i, j: i <= j))


def below(up, zeros, left, right, i):
    return jnp.concatenate(
        [jnp.concatenate([up[i], zeros], axis=1), jnp.concatenate([left[i], right[i]], axis=1)], axis=0
    )


def skip_row(d_ref, spread):
    heads, width = spread.shape
    hi, mid, lo = split3(jnp.broadcast_to(d_ref[...], (8, heads)))
    return (mm(hi, spread) + mm(mid, spread) + mm(lo, spread))[0:1, :]


def start_kernel(lt_hbm, x_hbm, b_hbm, pay_ref, lt_ref, b_ref, x_ref, sems):
    heads, length = lt_hbm.shape
    width = x_hbm.shape[1]
    first, second, third = fetch([(lt_hbm, lt_ref), (b_hbm, b_ref), (x_hbm, x_ref)], sems)
    second.wait()
    b_turned = turned(b_ref[...])
    first.wait()
    later = triangle(length, lambda i, j: i > j)
    ends = mm_by(lt_ref[...], jnp.concatenate([later, jnp.ones((length, HALF), BF16)], axis=1))
    hi, lo = split2(jnp.exp(ends))
    both = jnp.concatenate([hi.astype(F32), lo.astype(F32)], axis=0).T.astype(BF16)[: length + 16]
    spread = head_map(heads, width)
    spread = jnp.concatenate([spread, spread], axis=0)
    third.wait()
    for k in range(1):
        big = slice(1024 * k, 1024 * (k + 1))
        tail = mm(both, spread[:, big])
        state = mm_split(b_turned, x_ref[:, big].astype(F32) * tail[:length])
        whole = tail[length : length + 1, :]
        for q in range(8):
            cols = slice(HALF * q, HALF * (q + 1))
            for r in range(4):
                at = 33 * (4 * (q + 8 * k) + r)
                pay_ref[at : at + 32, :] = state[32 * r : 32 * r + 32, cols]
                pay_ref[at + 32 : at + 33, :] = whole[:, cols]


def local_kernel(
    lt_hbm, x_hbm, b_hbm, c_hbm, z_hbm, d_hbm, w_hbm, dout_hbm,
    base_ref, esilu_ref, c_ref, ct_ref, w_ref, dout_ref, yn_hbm,
    lt_ref, x_ref, b_ref, z_ref, d_ref, yn_ref, sems,
):
    heads, length = lt_hbm.shape
    width = x_hbm.shape[1]
    copies = fetch(
        [(lt_hbm, lt_ref), (b_hbm, b_ref), (c_hbm, c_ref), (x_hbm, x_ref), (z_hbm, z_ref), (d_hbm, d_ref),
         (w_hbm, w_ref), (dout_hbm, dout_ref)],
        sems,
    )
    spread = head_map(heads, width)
    for copy in copies[:3]:
        copy.wait()
    cum_t = block_sums(lt_ref[...])
    cum = cum_t.T
    ecum = expand(jnp.exp(cum_t), spread)
    ct_ref[...] = turned(c_ref[...])
    inner = mm(c_ref[...], b_ref[...], 1, 1)
    top, left, right = inner[:HALF, :HALF], inner[HALF:, :HALF], inner[HALF:, HALF:]
    lower = iota((HALF, HALF), 0) >= iota((HALF, HALF), 1)
    first = iota((length, HALF), 1) < P_SIZE
    zeros = jnp.zeros((HALF, HALF), BF16)
    for copy in copies[3:6]:
        copy.wait()
    skip = skip_row(d_ref, spread)
    for q in range(width // HALF):
        cols = slice(HALF * q, HALF * (q + 1))
        x_pair = x_ref[:, cols]
        mixes = []
        for h in (2 * q, 2 * q + 1):
            col, row = cum[:, h : h + 1], cum_t[h : h + 1, :]
            up = jnp.where(lower, jnp.exp(col[:HALF] - row[:, :HALF]), 0.0) * top
            dl = jnp.exp(col[HALF:] - row[:, :HALF]) * left
            dr = jnp.where(lower, jnp.exp(col[HALF:] - row[:, HALF:]), 0.0) * right
            mixes += [below(split2(up), zeros, split2(dl), split2(dr), i) for i in range(2)]
        got = mm(jnp.concatenate(mixes, axis=0), x_pair)
        yn = jnp.where(
            first, got[:length] + got[length : 2 * length], got[2 * length : 3 * length] + got[3 * length :]
        )
        yn_ref[:, cols] = yn
        z_val = z_ref[:, cols].astype(F32)
        silu = z_val * (1.0 / (1.0 + jnp.exp(-z_val)))
        esilu_ref[:, cols] = ecum[:, cols] * silu
        base_ref[:, cols] = (yn + skip[:, cols] * x_pair.astype(F32)) * silu
    for copy in copies[6:]:
        copy.wait()
    yn_copy = pltpu.make_async_copy(yn_ref, yn_hbm, sems.at[8])
    yn_copy.start()
    yn_copy.wait()


def prefix_kernel(in_ref, out_ref, dec_ref):
    count = dec_ref.shape[0]
    state = jnp.zeros((32, HALF), F32)
    for p in range(count):
        out_ref[32 * p : 32 * p + 32, :] = state
        decay = in_ref[33 * p + 32 : 33 * p + 33, :]
        dec_ref[p : p + 1, :] = decay
        if p < count - 1:
            state = decay * state + in_ref[33 * p : 33 * p + 32, :]


def gate_kernel(s_ref, c_ref, base_ref, esilu_ref, dout_ref, w_ref, gated_ref, sums_ref):
    c_val = c_ref[...]
    length, width = base_ref.shape
    squares = jnp.zeros((length, HALF), F32)
    products = jnp.zeros((length, HALF), F32)
    for q in range(width // 256):
        big = slice(256 * q, 256 * (q + 1))
        c_state = mm_split(c_val, load_block(s_ref, 32, q))
        gated = base_ref[:, big] + esilu_ref[:, big] * c_state
        gated_ref[:, big] = gated
        sq = gated * gated
        pr = dout_ref[:, big].astype(F32) * w_ref[:, big] * gated
        squares = squares + sq[:, :HALF] + sq[:, HALF:]
        products = products + pr[:, :HALF] + pr[:, HALF:]
    rows = [jnp.sum(total.T, axis=0, keepdims=True) for total in (squares, products)]
    tile = jnp.concatenate([row[:, HALF * i : HALF * (i + 1)] for row in rows for i in range(2)], axis=0)
    sums_ref[...] = jnp.concatenate([tile] * (sums_ref.shape[0] // 4), axis=0)


def columns(rows):
    turned_rows = jnp.concatenate([rows, jnp.zeros((HALF - 8, HALF), F32)], axis=0).T
    return [jnp.concatenate([turned_rows[:, i : i + 1], turned_rows[:, i + 1 : i + 2]], axis=0) for i in (0, 2)]


def back_kernel(
    channels, sums_ref, gated_ref, esilu_ref, dout_ref, w_ref, ct_ref, s_ref,
    pay_hbm, scal_hbm, s_hbm, scal_ref, pay_ref, sems,
):
    length, width = gated_ref.shape
    scal_copy, s_copy = copies_of([(scal_ref, scal_hbm), (s_ref, s_hbm)], sems)
    s_copy.start()
    total = sums_ref[0:4, :]
    for i in range(1, sums_ref.shape[0] // 4):
        total = total + sums_ref[4 * i : 4 * i + 4, :]
    inv = lax.rsqrt(total[0:2] / channels + EPS)
    fall = inv * inv * inv * total[2:4] / channels
    rows = jnp.concatenate([inv, fall, jnp.zeros((4, HALF), F32)], axis=0)
    scal_ref[...] = rows
    scal_copy.start()
    inv_col, fall_col = columns(rows)
    outs = []
    c_turned = ct_ref[...]
    for k in range(width // 256):
        big = slice(256 * k, 256 * (k + 1))
        gated = gated_ref[:, big]
        d_inv = dout_ref[:, big].astype(F32) * inv_col
        weight = jnp.sum(d_inv * gated, axis=0, keepdims=True)
        back = mm_split(c_turned, (d_inv * w_ref[:, big] - gated * fall_col) * esilu_ref[:, big])
        for q in (2 * k, 2 * k + 1):
            off = HALF * (q - 2 * k)
            for r in range(4):
                at = 33 * (4 * q + r)
                pay_ref[at : at + 32, :] = back[32 * r : 32 * r + 32, off : off + HALF]
                pay_ref[at + 32 : at + 33, :] = weight[:, off : off + HALF]
        if k % 2 == 1:
            rows = pl.ds(528 * (k // 2), 528)
            outs.append(pltpu.make_async_copy(pay_ref.at[rows], pay_hbm.at[rows], sems.at[2 + k]))
            outs[-1].start()
    for copy in outs:
        copy.wait()
    scal_copy.wait()
    s_copy.wait()


def grads_kernel(
    lt_hbm, scal_hbm, dout_hbm, w_hbm, x_hbm, z_hbm, b_hbm, c_hbm, d_hbm, yn_hbm, s_hbm,
    gx_ref, gb_ref, gl_ref, tail_ref, x_ref, b_ref, skip_ref, gz_hbm, gc_hbm,
    s_ref, lt_ref, scal_ref, dout_ref, w_ref, z_ref, c_ref, d_ref, yn_ref, dye_ref, dot_ref, gz_ref, gc_ref, sems,
):
    heads, length = lt_hbm.shape
    width = x_hbm.shape[1]
    copies = fetch(
        [(lt_hbm, lt_ref), (scal_hbm, scal_ref), (b_hbm, b_ref), (c_hbm, c_ref), (d_hbm, d_ref), (w_hbm, w_ref),
         (x_hbm, x_ref), (s_hbm, s_ref), (yn_hbm, yn_ref), (z_hbm, z_ref), (dout_hbm, dout_ref)],
        sems,
    )
    spread = head_map(heads, width)
    for copy in copies[:6]:
        copy.wait()
    cum_t = block_sums(lt_ref[...])
    cum = cum_t.T
    last = cum_t[:, length - 1 : length]
    ecum = expand(jnp.exp(cum_t), spread)
    tail_ref[...] = expand(jnp.exp(last - cum_t), spread)
    inv_col, fall_col = columns(scal_ref[...])
    skip = skip_row(d_ref, spread)
    b_val, c_val = b_ref[...], c_ref[...]
    inner_t = mm(b_val, c_val, 1, 1)
    left, right, low = inner_t[:HALF, :HALF], inner_t[:HALF, HALF:], inner_t[HALF:, HALF:]
    upper = iota((HALF, HALF), 0) <= iota((HALF, HALF), 1)
    first = iota((length, HALF), 1) < P_SIZE
    zeros = jnp.zeros((HALF, HALF), BF16)
    w_left = jnp.zeros((HALF, HALF), F32)
    w_right = jnp.zeros((HALF, HALF), F32)
    w_low = jnp.zeros((HALF, HALF), F32)
    skips = []
    far = jnp.zeros((length, HALF), F32)
    for copy in copies[6:]:
        copy.wait()
    for q in range(width // HALF):
        cols = slice(HALF * q, HALF * (q + 1))
        x_pair = x_ref[:, cols]
        x_val = x_pair.astype(F32)
        z_val = z_ref[:, cols].astype(F32)
        sig = 1.0 / (1.0 + jnp.exp(-z_val))
        silu = z_val * sig
        if q % 2 == 0:
            state = load_block(s_ref, 32, q // 2)
            c_state = mm_split(c_val, state)
        off = slice(HALF * (q % 2), HALF * (q % 2 + 1))
        y_near = yn_ref[:, cols] + ecum[:, cols] * c_state[:, off]
        y_val = y_near + skip[:, cols] * x_val
        d_gated = inv_col * (dout_ref[:, cols].astype(F32) * w_ref[:, cols]) - y_val * silu * fall_col
        dy = d_gated * silu
        dye_ref[:, cols] = dy * ecum[:, cols]
        gz_ref[:, cols] = (d_gated * y_val * sig * (1.0 + z_val * (1.0 - sig))).astype(BF16)
        if q % 2 == 1:
            e_hi, e_lo = split2(dye_ref[:, 128 * q - 128 : 128 * q + 128])
            both = mm(jnp.concatenate([e_hi, e_lo], axis=0), jnp.concatenate(split2(state.T), axis=1))
            far = far + both[:length, :HALF] + both[:length, HALF:] + both[length:, :HALF]
        skips.append(jnp.sum(dy * x_val, axis=0, keepdims=True))
        hi, lo = split2(dy)
        ones = jnp.concatenate([jnp.where(first, x_val, 0.0), jnp.where(first, 0.0, x_val)], axis=0).astype(BF16)
        both = jnp.concatenate([hi, lo], axis=1)
        dots = mm(jnp.concatenate([ones, ones], axis=1), both, 1, 1)
        mix_hi, mix_lo = [], []
        for k in range(2):
            h = 2 * q + k
            col, row = cum[:, h : h + 1], cum_t[h : h + 1, :]
            dot = dots[length * k : length * (k + 1)]
            dec_left = jnp.where(upper, jnp.exp(row[:, :HALF] - col[:HALF]), 0.0)
            dec_right = jnp.exp(row[:, HALF:] - col[:HALF])
            dec_low = jnp.where(upper, jnp.exp(row[:, HALF:] - col[HALF:]), 0.0)
            w_left = w_left + dec_left * dot[:HALF, :HALF]
            w_right = w_right + dec_right * dot[:HALF, HALF:]
            w_low = w_low + dec_low * dot[HALF:, HALF:]
            blocks = [split2(m) for m in (dec_left * left, dec_right * right, dec_low * low)]
            for i, mix in enumerate((mix_hi, mix_lo)):
                up = jnp.concatenate([blocks[0][i], blocks[1][i]], axis=1)
                mix.append(jnp.concatenate([up, jnp.concatenate([zeros, blocks[2][i]], axis=1)], axis=0))
        got = mm(jnp.concatenate(mix_hi + mix_lo, axis=0), both)
        got = got[: 2 * length, :HALF] + got[: 2 * length, HALF:] + got[2 * length :, :HALF]
        g_near = jnp.where(first, got[:length], got[length:])
        gx_ref[:, cols] = g_near + skip[:, cols] * dy
        dot_ref[:, cols] = dy * y_near - x_val * g_near
    w_up = jnp.concatenate([w_left, w_right], axis=1)
    low_part = mm2(w_right.T, b_val[:HALF]) + mm2(w_low.T, b_val[HALF:])
    gc_ref[...] = far + jnp.concatenate([mm2(w_left.T, b_val[:HALF]), low_part], axis=0)
    outs = fetch([(gc_ref, gc_hbm), (gz_ref, gz_hbm)], sems)
    gl_ref[...] = mm_by(segment(dot_ref[...], spread), triangle(length, lambda i, j: i >= j))
    gb_ref[:HALF, :] = mm2(w_up, c_val)
    gb_ref[HALF:, :] = mm2(w_low, c_val[HALF:])
    hi, mid, lo = split3(jnp.broadcast_to(jnp.concatenate(skips, axis=1), (8, width)))
    wide = head_map(HALF, width)
    skip_ref[...] = mm(hi, wide, 1, 1) + mm(mid, wide, 1, 1) + mm(lo, wide, 1, 1)
    for copy in outs:
        copy.wait()


def suffix_kernel(in_ref, dec_ref, skip_ref, out_ref):
    count = dec_ref.shape[0]
    state = jnp.zeros((32, HALF), F32)
    sums = in_ref[32:33, :]
    for p in range(1, count):
        sums = sums + in_ref[33 * p + 32 : 33 * p + 33, :]
    rows = jnp.concatenate([sums, skip_ref[0:1, :]], axis=0)
    for p in range(count - 1, -1, -1):
        out_ref[34 * p : 34 * p + 32, :] = state
        out_ref[34 * p + 32 : 34 * p + 34, :] = rows
        if p > 0:
            state = dec_ref[p : p + 1, :] * state + in_ref[33 * p : 33 * p + 32, :]


def final_kernel(
    a_ref, s_hbm, lt_hbm, tail_ref, x_ref, b_ref, gx_ref, gb_ref, gl_ref,
    ox_hbm, ob_hbm, ol_hbm, skip_hbm, weight_hbm, ox_ref, ob_ref, ol_ref, skip_ref, weight_ref, lt_ref, s_ref, sems,
):
    heads, length = lt_hbm.shape
    width = x_ref.shape[1]
    spread = head_map(heads, width)
    outs = [(weight_ref, weight_hbm), (skip_ref, skip_hbm), (ol_ref, ol_hbm), (ob_ref, ob_hbm), (ox_ref, ox_hbm)]
    copies = copies_of(outs + [(lt_hbm, lt_ref), (s_hbm, s_ref)], sems)
    copies[6].start()
    copies[5].start()
    after = load_state(a_ref, 34)
    tail, x_val = tail_ref[...], x_ref[...].astype(F32)
    b_after = mm_split(b_ref[...], after) * tail
    ox_ref[...] = (gx_ref[...] + b_after).astype(BF16)
    copies[4].start()
    late = segment(x_val * b_after, spread)
    x_hi, x_lo = split2(x_val * tail)
    a_hi, a_lo = split2(after.T)
    both = mm(x_hi, jnp.concatenate([a_hi, a_lo], axis=1))
    ob_ref[...] = gb_ref[...] + both[:, :HALF] + both[:, HALF:] + mm(x_lo, a_hi)
    copies[3].start()
    weight_ref[...] = jnp.concatenate([a_ref[136 * q + 32 : 136 * q + 33, :] for q in range(8)], axis=0)
    skip = a_ref[33:34, :]
    for p in range(1, a_ref.shape[0] // 34):
        skip = skip + a_ref[34 * p + 33 : 34 * p + 34, :]
    skip_ref[...] = skip[:, :heads]
    copies[0].start()
    copies[1].start()
    copies[5].wait()
    copies[6].wait()
    start = jnp.sum(load_state(s_ref, 32) * after, axis=0, keepdims=True)
    mine = iota((heads, width), 1) // P_SIZE == iota((heads, width), 0)
    start = jnp.sum(jnp.where(mine, start, 0.0), axis=1, keepdims=True)
    whole = jnp.exp(jnp.sum(lt_ref[...], axis=1, keepdims=True))
    ol_ref[...] = gl_ref[...] + mm_by(late, triangle(length, lambda i, j: i < j)) + whole * start
    copies[2].start()
    for copy in copies[:5]:
        copy.wait()


def call(kernel, name, outs, *args, flops=0, scratch=(), hbm_in=(), hbm_out=(), mib=16):
    nbytes = sum(a.size * a.dtype.itemsize for a in (*args, *outs))
    spaces = [pltpu.HBM if i in hbm_in else pltpu.VMEM for i in range(len(args))]
    out_spaces = [pltpu.HBM if i in hbm_out else pltpu.VMEM for i in range(len(outs))]
    return pl.pallas_call(
        kernel,
        name=name,
        out_shape=[space(o.shape, o.dtype) for space, o in zip(out_spaces, outs)],
        in_specs=[pl.BlockSpec(memory_space=space) for space in spaces],
        out_specs=[pl.BlockSpec(memory_space=space) for space in out_spaces],
        scratch_shapes=list(scratch),
        compiler_params=pltpu.CompilerParams(vmem_limit_bytes=mib * 1024 * 1024),
        cost_estimate=pl.CostEstimate(flops=flops, bytes_accessed=nbytes, transcendentals=0),
    )(*[pltpu.with_memory_space_constraint(a, space) for a, space in zip(args, spaces)])


def exchange(messages, rows, axes=CHUNKS):
    count = lax.axis_size(axes)
    got = lax.all_to_all(messages.reshape(count, 1, rows * HALF), axes, 0, 0)
    return got.reshape(count * rows, HALF)


def on_device(x_in, b_in, c_in, decay_log, d_skip, gate, norm_weight, d_out):
    length, heads = decay_log.shape
    width = x_in.shape[1]
    chunks = lax.axis_size(CHUNKS)
    groups = lax.axis_size("heads")
    shape = jax.ShapeDtypeStruct
    wide = shape((length, width), F32)
    half_wide = shape((length, width), BF16)
    small = shape((heads, length), F32)
    narrow = shape(b_in.shape, F32)
    half_narrow = shape(b_in.shape, BF16)
    state = shape((chunks * 32, HALF), F32)
    weight = norm_weight.reshape(1, width)
    d_row = d_skip.reshape(1, heads)
    w_row, one_row = shape(weight.shape, F32), shape(d_row.shape, F32)
    decay_t = decay_log.T
    sem = pltpu.SemaphoreType.DMA

    def vmem(*shapes):
        return [pltpu.VMEM(s.shape, s.dtype) for s in shapes]

    (pay,) = call(
        start_kernel, "start", [shape((chunks * 33, HALF), F32)], decay_t, x_in, b_in,
        flops=10**9, scratch=vmem(small, half_narrow, half_wide) + [sem((3,))], hbm_in=(0, 1, 2),
    )
    got = exchange(pay, 33)
    base, esilu, c_val, c_turned, w_val, dout_val, y_near = call(
        local_kernel, "local", [wide, wide, half_narrow, shape(c_in.shape[::-1], BF16), w_row, half_wide, wide],
        decay_t, x_in, b_in, c_in, gate, d_row, weight, d_out,
        flops=8 * 10**9, hbm_in=range(8), hbm_out=(6,), mib=24,
        scratch=vmem(small, half_wide, half_narrow, half_wide, one_row, wide) + [sem((9,))],
    )
    spread, decays = call(prefix_kernel, "prefix", [state, shape((chunks, HALF), F32)], got)
    before = exchange(spread, 32)
    gated, sums = call(
        gate_kernel, "gated", [wide, shape((groups * 4, HALF), F32)],
        before, c_val, base, esilu, dout_val, w_val, flops=10**9,
    )
    sums = exchange(sums, 4, "heads")

    def back(*refs):
        back_kernel(float(width * groups), *refs)

    rows = shape((8, HALF), F32)
    pay, scalars, before = call(
        back, "back", [shape((chunks * 33, HALF), F32), rows, state],
        sums, gated, esilu, dout_val, w_val, c_turned, before,
        flops=10**9, hbm_out=(0, 1, 2), scratch=vmem(rows, shape((chunks * 33, HALF), F32)) + [sem((6,))],
    )
    got = exchange(pay, 33)
    gx, gb, gl, tail, x_val, b_val, skip, grad_gate, grad_c = call(
        grads_kernel, "grads",
        [wide, narrow, small, wide, half_wide, half_narrow, shape((8, HALF), F32), half_wide, narrow],
        decay_t, scalars, d_out, weight, x_in, gate, b_in, c_in, d_row, y_near, before,
        flops=16 * 10**9, hbm_in=range(11), hbm_out=(7, 8), mib=32,
        scratch=vmem(state, small, rows, half_wide, w_row, half_wide, half_narrow, one_row, wide, wide, wide, half_wide, narrow)
        + [sem((16,))],
    )
    (spread,) = call(suffix_kernel, "suffix", [shape((chunks * 34, HALF), F32)], got, decays, skip)
    after = exchange(spread, 34)
    outs = [half_wide, narrow, small, one_row, shape((8, HALF), F32)]
    grad_x, grad_b, grad_decay, grad_skip, grad_weight = call(
        final_kernel, "final", outs,
        after, before, decay_t, tail, x_val, b_val, gx, gb, gl,
        flops=2 * 10**9, scratch=vmem(*outs, small, state) + [sem((7,))], hbm_in=(1, 2), hbm_out=range(5),
    )
    return (
        grad_x,
        grad_b,
        grad_c,
        grad_decay.T,
        grad_skip.reshape(heads),
        grad_gate,
        grad_weight.reshape(width),
    )


def solution(mesh):
    tokens = P(CHUNKS, "heads")
    in_specs = (tokens, tokens, tokens, tokens, P("heads"), tokens, P("heads"), tokens)
    out_specs = (tokens, tokens, tokens, tokens, P("heads"), tokens, P("heads"))
    return jax.shard_map(on_device, mesh=mesh, in_specs=in_specs, out_specs=out_specs, check_vma=False)
```

```python
import jax
import jax.numpy as jnp
from jax import lax
from jax.experimental import pallas as pl
from jax.experimental.pallas import tpu as pltpu
from jax.sharding import PartitionSpec as P

P_SIZE = 64
EPS = 1e-05
F32 = jnp.float32
BF16 = jnp.bfloat16
CHUNKS = ("outer", "inner")
HALF = 128


def mm(a, b, ca=1, cb=0):
    return lax.dot_general(a, b, (((ca,), (cb,)), ((), ())), preferred_element_type=F32)


def split2(a):
    hi = a.astype(BF16)
    return hi, (a - hi.astype(F32)).astype(BF16)


def split3(a):
    hi = a.astype(BF16)
    rest = a - hi.astype(F32)
    mid = rest.astype(BF16)
    return hi, mid, (rest - mid.astype(F32)).astype(BF16)


def mm2(a, b, ca=1, cb=0):
    hi, lo = split2(a)
    return mm(hi, b, ca, cb) + mm(lo, b, ca, cb)


def mm_split(a, b):
    return mm(jnp.concatenate([a, a], axis=1), jnp.concatenate(split2(b), axis=0))


def iota(shape, dim):
    return lax.broadcasted_iota(jnp.int32, shape, dim)


def head_map(heads, width):
    return jnp.where(iota((heads, width), 1) // P_SIZE == iota((heads, width), 0), 1.0, 0.0).astype(BF16)


def expand(a, spread, rows=None):
    hi, lo = split2(a)
    both = jnp.concatenate([hi.astype(F32), lo.astype(F32)], axis=0).T.astype(BF16)
    return mm(both[:rows], jnp.concatenate([spread, spread], axis=0))


def segment(a, spread):
    turned_map = turned(spread)
    hi, lo = split2(a)
    return (mm(hi, turned_map) + mm(lo, turned_map)).T


def triangle(n, keep):
    return jnp.where(keep(iota((n, n), 0), iota((n, n), 1)), 1.0, 0.0).astype(BF16)


def mm_by(a, tri):
    rows = a.shape[0]
    got = mm(jnp.concatenate(split3(a), axis=0), tri)
    return got[:rows] + got[rows : 2 * rows] + got[2 * rows :]


def load_state(ref, rows):
    return jnp.concatenate([load_block(ref, rows, k) for k in range(4)], axis=1)


def load_block(ref, rows, k):
    cols = []
    for q in (2 * k, 2 * k + 1):
        at = [rows * (4 * q + r) for r in range(4)]
        cols.append(jnp.concatenate([ref[i : i + 32, :] for i in at], axis=0))
    return jnp.concatenate(cols, axis=1)


def copies_of(pairs, sems):
    return [pltpu.make_async_copy(src, dst, sems.at[i]) for i, (src, dst) in enumerate(pairs)]


def fetch(pairs, sems):
    copies = copies_of(pairs, sems)
    for copy in copies:
        copy.start()
    return copies


def quarters(ref):
    return [ref.at[:, pl.ds(256 * k, 256)] for k in range(4)]


def turned(a):
    return a.astype(F32).T.astype(BF16)


def block_sums(lt):
    return mm_by(lt, triangle(lt.shape[1], lambda i, j: i <= j))


def below(up, zeros, left, right, i):
    return jnp.concatenate(
        [jnp.concatenate([up[i], zeros], axis=1), jnp.concatenate([left[i], right[i]], axis=1)], axis=0
    )


def skip_row(d_ref, spread):
    heads, width = spread.shape
    hi, mid, lo = split3(jnp.broadcast_to(d_ref[...], (8, heads)))
    return (mm(hi, spread) + mm(mid, spread) + mm(lo, spread))[0:1, :]


def start_kernel(lt_hbm, x_hbm, b_hbm, pay_ref, lt_ref, b_ref, x_ref, sems):
    heads, length = lt_hbm.shape
    width = x_hbm.shape[1]
    first, second, third = fetch([(lt_hbm, lt_ref), (b_hbm, b_ref), (x_hbm, x_ref)], sems)
    first.wait()
    later = triangle(length, lambda i, j: i > j)
    ends = mm_by(lt_ref[...], jnp.concatenate([later, jnp.ones((length, HALF), BF16)], axis=1))
    second.wait()
    b_turned = turned(b_ref[...])
    hi, lo = split2(jnp.exp(ends))
    both = jnp.concatenate([hi.astype(F32), lo.astype(F32)], axis=0).T.astype(BF16)[: length + 16]
    spread = head_map(heads, width)
    spread = jnp.concatenate([spread, spread], axis=0)
    third.wait()
    tail = mm(both, spread)
    state = mm_split(b_turned, x_ref[...].astype(F32) * tail[:length])
    for q in range(width // HALF):
        cols = slice(HALF * q, HALF * (q + 1))
        for r in range(4):
            at = 33 * (4 * q + r)
            pay_ref[at : at + 32, :] = state[32 * r : 32 * r + 32, cols]
            pay_ref[at + 32 : at + 33, :] = tail[length : length + 1, cols]


def local_kernel(
    lt_hbm, x_hbm, b_hbm, c_hbm, z_hbm, d_hbm, w_hbm, dout_hbm,
    base_ref, esilu_ref, c_ref, ct_ref, w_ref, dout_ref, yn_hbm,
    lt_ref, x_ref, b_ref, z_ref, d_ref, yn_ref, sems,
):
    heads, length = lt_hbm.shape
    width = x_hbm.shape[1]
    copies = fetch(
        [(lt_hbm, lt_ref), (b_hbm, b_ref), (c_hbm, c_ref), (x_hbm, x_ref), (z_hbm, z_ref), (d_hbm, d_ref),
         (w_hbm, w_ref), (dout_hbm, dout_ref)],
        sems,
    )
    spread = head_map(heads, width)
    for copy in copies[:3]:
        copy.wait()
    cum_t = block_sums(lt_ref[...])
    cum = cum_t.T
    ecum = expand(jnp.exp(cum_t), spread)
    ct_ref[...] = turned(c_ref[...])
    inner = mm(c_ref[...], b_ref[...], 1, 1)
    top, left, right = inner[:HALF, :HALF], inner[HALF:, :HALF], inner[HALF:, HALF:]
    lower = iota((HALF, HALF), 0) >= iota((HALF, HALF), 1)
    first = iota((length, HALF), 1) < P_SIZE
    zeros = jnp.zeros((HALF, HALF), BF16)
    for copy in copies[3:6]:
        copy.wait()
    skip = skip_row(d_ref, spread)
    for q in range(width // HALF):
        cols = slice(HALF * q, HALF * (q + 1))
        x_pair = x_ref[:, cols]
        mixes = []
        for h in (2 * q, 2 * q + 1):
            col, row = cum[:, h : h + 1], cum_t[h : h + 1, :]
            up = jnp.where(lower, jnp.exp(col[:HALF] - row[:, :HALF]), 0.0) * top
            dl = jnp.exp(col[HALF:] - row[:, :HALF]) * left
            dr = jnp.where(lower, jnp.exp(col[HALF:] - row[:, HALF:]), 0.0) * right
            mixes += [below(split2(up), zeros, split2(dl), split2(dr), i) for i in range(2)]
        got = mm(jnp.concatenate(mixes, axis=0), x_pair)
        yn = jnp.where(
            first, got[:length] + got[length : 2 * length], got[2 * length : 3 * length] + got[3 * length :]
        )
        yn_ref[:, cols] = yn
        z_val = z_ref[:, cols].astype(F32)
        silu = z_val * (1.0 / (1.0 + jnp.exp(-z_val)))
        esilu_ref[:, cols] = ecum[:, cols] * silu
        base_ref[:, cols] = (yn + skip[:, cols] * x_pair.astype(F32)) * silu
    for copy in copies[6:]:
        copy.wait()
    yn_copy = pltpu.make_async_copy(yn_ref, yn_hbm, sems.at[8])
    yn_copy.start()
    yn_copy.wait()


def prefix_kernel(in_ref, out_ref, dec_ref):
    count = dec_ref.shape[0]
    state = jnp.zeros((32, HALF), F32)
    for p in range(count):
        out_ref[32 * p : 32 * p + 32, :] = state
        decay = in_ref[33 * p + 32 : 33 * p + 33, :]
        dec_ref[p : p + 1, :] = decay
        if p < count - 1:
            state = decay * state + in_ref[33 * p : 33 * p + 32, :]


def gate_kernel(s_ref, c_ref, base_ref, esilu_ref, dout_ref, w_ref, gated_ref, sums_ref):
    c_val = c_ref[...]
    length, width = base_ref.shape
    squares = jnp.zeros((length, HALF), F32)
    products = jnp.zeros((length, HALF), F32)
    for q in range(width // 256):
        big = slice(256 * q, 256 * (q + 1))
        c_state = mm_split(c_val, load_block(s_ref, 32, q))
        gated = base_ref[:, big] + esilu_ref[:, big] * c_state
        gated_ref[:, big] = gated
        sq = gated * gated
        pr = dout_ref[:, big].astype(F32) * w_ref[:, big] * gated
        squares = squares + sq[:, :HALF] + sq[:, HALF:]
        products = products + pr[:, :HALF] + pr[:, HALF:]
    rows = [jnp.sum(total.T, axis=0, keepdims=True) for total in (squares, products)]
    tile = jnp.concatenate([row[:, HALF * i : HALF * (i + 1)] for row in rows for i in range(2)], axis=0)
    sums_ref[...] = jnp.concatenate([tile] * (sums_ref.shape[0] // 4), axis=0)


def columns(rows):
    turned_rows = jnp.concatenate([rows, jnp.zeros((HALF - 8, HALF), F32)], axis=0).T
    return [jnp.concatenate([turned_rows[:, i : i + 1], turned_rows[:, i + 1 : i + 2]], axis=0) for i in (0, 2)]


def back_kernel(
    channels, sums_ref, gated_ref, esilu_ref, dout_ref, w_ref, ct_ref, s_ref,
    pay_hbm, scal_hbm, s_hbm, scal_ref, pay_ref, sems,
):
    length, width = gated_ref.shape
    scal_copy, s_copy = copies_of([(scal_ref, scal_hbm), (s_ref, s_hbm)], sems)
    s_copy.start()
    total = sums_ref[0:4, :]
    for i in range(1, sums_ref.shape[0] // 4):
        total = total + sums_ref[4 * i : 4 * i + 4, :]
    inv = lax.rsqrt(total[0:2] / channels + EPS)
    fall = inv * inv * inv * total[2:4] / channels
    rows = jnp.concatenate([inv, fall, jnp.zeros((4, HALF), F32)], axis=0)
    scal_ref[...] = rows
    scal_copy.start()
    inv_col, fall_col = columns(rows)
    outs = []
    c_turned = ct_ref[...]
    for k in range(width // 256):
        big = slice(256 * k, 256 * (k + 1))
        gated = gated_ref[:, big]
        d_inv = dout_ref[:, big].astype(F32) * inv_col
        weight = jnp.sum(d_inv * gated, axis=0, keepdims=True)
        back = mm_split(c_turned, (d_inv * w_ref[:, big] - gated * fall_col) * esilu_ref[:, big])
        for q in (2 * k, 2 * k + 1):
            off = HALF * (q - 2 * k)
            for r in range(4):
                at = 33 * (4 * q + r)
                pay_ref[at : at + 32, :] = back[32 * r : 32 * r + 32, off : off + HALF]
                pay_ref[at + 32 : at + 33, :] = weight[:, off : off + HALF]
        if k % 2 == 1:
            rows = pl.ds(528 * (k // 2), 528)
            outs.append(pltpu.make_async_copy(pay_ref.at[rows], pay_hbm.at[rows], sems.at[2 + k]))
            outs[-1].start()
    for copy in outs:
        copy.wait()
    scal_copy.wait()
    s_copy.wait()


def grads_kernel(
    lt_hbm, scal_hbm, dout_hbm, w_hbm, x_hbm, z_hbm, b_hbm, c_hbm, d_hbm, yn_hbm, s_hbm,
    gx_ref, gb_ref, gl_ref, tail_ref, x_ref, b_ref, skip_ref, gz_hbm, gc_hbm,
    s_ref, lt_ref, scal_ref, dout_ref, w_ref, z_ref, c_ref, d_ref, yn_ref, dye_ref, dot_ref, gz_ref, gc_ref, sems,
):
    heads, length = lt_hbm.shape
    width = x_hbm.shape[1]
    copies = fetch(
        [(lt_hbm, lt_ref), (scal_hbm, scal_ref), (b_hbm, b_ref), (c_hbm, c_ref), (d_hbm, d_ref), (w_hbm, w_ref),
         (x_hbm, x_ref), (s_hbm, s_ref), (yn_hbm, yn_ref), (z_hbm, z_ref), (dout_hbm, dout_ref)],
        sems,
    )
    spread = head_map(heads, width)
    for copy in copies[:6]:
        copy.wait()
    cum_t = block_sums(lt_ref[...])
    cum = cum_t.T
    last = cum_t[:, length - 1 : length]
    ecum = expand(jnp.exp(cum_t), spread)
    tail_ref[...] = expand(jnp.exp(last - cum_t), spread)
    inv_col, fall_col = columns(scal_ref[...])
    skip = skip_row(d_ref, spread)
    b_val, c_val = b_ref[...], c_ref[...]
    inner_t = mm(b_val, c_val, 1, 1)
    left, right, low = inner_t[:HALF, :HALF], inner_t[:HALF, HALF:], inner_t[HALF:, HALF:]
    upper = iota((HALF, HALF), 0) <= iota((HALF, HALF), 1)
    first = iota((length, HALF), 1) < P_SIZE
    zeros = jnp.zeros((HALF, HALF), BF16)
    w_left = jnp.zeros((HALF, HALF), F32)
    w_right = jnp.zeros((HALF, HALF), F32)
    w_low = jnp.zeros((HALF, HALF), F32)
    skips = []
    far = jnp.zeros((length, HALF), F32)
    for copy in copies[6:]:
        copy.wait()
    for q in range(width // HALF):
        cols = slice(HALF * q, HALF * (q + 1))
        x_pair = x_ref[:, cols]
        x_val = x_pair.astype(F32)
        z_val = z_ref[:, cols].astype(F32)
        sig = 1.0 / (1.0 + jnp.exp(-z_val))
        silu = z_val * sig
        if q % 2 == 0:
            state = load_block(s_ref, 32, q // 2)
            c_state = mm_split(c_val, state)
        off = slice(HALF * (q % 2), HALF * (q % 2 + 1))
        y_near = yn_ref[:, cols] + ecum[:, cols] * c_state[:, off]
        y_val = y_near + skip[:, cols] * x_val
        d_gated = inv_col * (dout_ref[:, cols].astype(F32) * w_ref[:, cols]) - y_val * silu * fall_col
        dy = d_gated * silu
        dye_ref[:, cols] = dy * ecum[:, cols]
        gz_ref[:, cols] = (d_gated * y_val * sig * (1.0 + z_val * (1.0 - sig))).astype(BF16)
        if q % 2 == 1:
            e_hi, e_lo = split2(dye_ref[:, 128 * q - 128 : 128 * q + 128])
            both = mm(jnp.concatenate([e_hi, e_lo], axis=0), jnp.concatenate(split2(state.T), axis=1))
            far = far + both[:length, :HALF] + both[:length, HALF:] + both[length:, :HALF]
        skips.append(jnp.sum(dy * x_val, axis=0, keepdims=True))
        hi, lo = split2(dy)
        ones = jnp.concatenate([jnp.where(first, x_val, 0.0), jnp.where(first, 0.0, x_val)], axis=0).astype(BF16)
        both = jnp.concatenate([hi, lo], axis=1)
        dots = mm(jnp.concatenate([ones, ones], axis=1), both, 1, 1)
        mix_hi, mix_lo = [], []
        for k in range(2):
            h = 2 * q + k
            col, row = cum[:, h : h + 1], cum_t[h : h + 1, :]
            dot = dots[length * k : length * (k + 1)]
            dec_left = jnp.where(upper, jnp.exp(row[:, :HALF] - col[:HALF]), 0.0)
            dec_right = jnp.exp(row[:, HALF:] - col[:HALF])
            dec_low = jnp.where(upper, jnp.exp(row[:, HALF:] - col[HALF:]), 0.0)
            w_left = w_left + dec_left * dot[:HALF, :HALF]
            w_right = w_right + dec_right * dot[:HALF, HALF:]
            w_low = w_low + dec_low * dot[HALF:, HALF:]
            blocks = [split2(m) for m in (dec_left * left, dec_right * right, dec_low * low)]
            for i, mix in enumerate((mix_hi, mix_lo)):
                up = jnp.concatenate([blocks[0][i], blocks[1][i]], axis=1)
                mix.append(jnp.concatenate([up, jnp.concatenate([zeros, blocks[2][i]], axis=1)], axis=0))
        got = mm(jnp.concatenate(mix_hi + mix_lo, axis=0), both)
        got = got[: 2 * length, :HALF] + got[: 2 * length, HALF:] + got[2 * length :, :HALF]
        g_near = jnp.where(first, got[:length], got[length:])
        gx_ref[:, cols] = g_near + skip[:, cols] * dy
        dot_ref[:, cols] = dy * y_near - x_val * g_near
    w_up = jnp.concatenate([w_left, w_right], axis=1)
    low_part = mm2(w_right.T, b_val[:HALF]) + mm2(w_low.T, b_val[HALF:])
    gc_ref[...] = far + jnp.concatenate([mm2(w_left.T, b_val[:HALF]), low_part], axis=0)
    outs = fetch([(gc_ref, gc_hbm), (gz_ref, gz_hbm)], sems)
    gl_ref[...] = mm_by(segment(dot_ref[...], spread), triangle(length, lambda i, j: i >= j))
    gb_ref[:HALF, :] = mm2(w_up, c_val)
    gb_ref[HALF:, :] = mm2(w_low, c_val[HALF:])
    hi, mid, lo = split3(jnp.broadcast_to(jnp.concatenate(skips, axis=1), (8, width)))
    wide = head_map(HALF, width)
    skip_ref[...] = mm(hi, wide, 1, 1) + mm(mid, wide, 1, 1) + mm(lo, wide, 1, 1)
    for copy in outs:
        copy.wait()


def suffix_kernel(in_ref, dec_ref, skip_ref, out_ref):
    count = dec_ref.shape[0]
    state = jnp.zeros((32, HALF), F32)
    sums = in_ref[32:33, :]
    for p in range(1, count):
        sums = sums + in_ref[33 * p + 32 : 33 * p + 33, :]
    rows = jnp.concatenate([sums, skip_ref[0:1, :]], axis=0)
    for p in range(count - 1, -1, -1):
        out_ref[34 * p : 34 * p + 32, :] = state
        out_ref[34 * p + 32 : 34 * p + 34, :] = rows
        if p > 0:
            state = dec_ref[p : p + 1, :] * state + in_ref[33 * p : 33 * p + 32, :]


def final_kernel(
    a_ref, s_hbm, lt_hbm, tail_ref, x_ref, b_ref, gx_ref, gb_ref, gl_ref,
    ox_hbm, ob_hbm, ol_hbm, skip_hbm, weight_hbm, ox_ref, ob_ref, ol_ref, skip_ref, weight_ref, lt_ref, s_ref, sems,
):
    heads, length = lt_hbm.shape
    width = x_ref.shape[1]
    spread = head_map(heads, width)
    outs = [(weight_ref, weight_hbm), (skip_ref, skip_hbm), (ol_ref, ol_hbm), (ob_ref, ob_hbm), (ox_ref, ox_hbm)]
    copies = copies_of(outs + [(lt_hbm, lt_ref), (s_hbm, s_ref)], sems)
    copies[6].start()
    copies[5].start()
    after = load_state(a_ref, 34)
    tail, x_val = tail_ref[...], x_ref[...].astype(F32)
    b_after = mm_split(b_ref[...], after) * tail
    ox_ref[...] = (gx_ref[...] + b_after).astype(BF16)
    copies[4].start()
    late = segment(x_val * b_after, spread)
    x_hi, x_lo = split2(x_val * tail)
    a_hi, a_lo = split2(after.T)
    both = mm(x_hi, jnp.concatenate([a_hi, a_lo], axis=1))
    ob_ref[...] = gb_ref[...] + both[:, :HALF] + both[:, HALF:] + mm(x_lo, a_hi)
    copies[3].start()
    weight_ref[...] = jnp.concatenate([a_ref[136 * q + 32 : 136 * q + 33, :] for q in range(8)], axis=0)
    skip = a_ref[33:34, :]
    for p in range(1, a_ref.shape[0] // 34):
        skip = skip + a_ref[34 * p + 33 : 34 * p + 34, :]
    skip_ref[...] = skip[:, :heads]
    copies[0].start()
    copies[1].start()
    copies[5].wait()
    copies[6].wait()
    start = jnp.sum(load_state(s_ref, 32) * after, axis=0, keepdims=True)
    mine = iota((heads, width), 1) // P_SIZE == iota((heads, width), 0)
    start = jnp.sum(jnp.where(mine, start, 0.0), axis=1, keepdims=True)
    whole = jnp.exp(jnp.sum(lt_ref[...], axis=1, keepdims=True))
    ol_ref[...] = gl_ref[...] + mm_by(late, triangle(length, lambda i, j: i < j)) + whole * start
    copies[2].start()
    for copy in copies[:5]:
        copy.wait()


def call(kernel, name, outs, *args, flops=0, scratch=(), hbm_in=(), hbm_out=(), mib=16):
    nbytes = sum(a.size * a.dtype.itemsize for a in (*args, *outs))
    spaces = [pltpu.HBM if i in hbm_in else pltpu.VMEM for i in range(len(args))]
    out_spaces = [pltpu.HBM if i in hbm_out else pltpu.VMEM for i in range(len(outs))]
    return pl.pallas_call(
        kernel,
        name=name,
        out_shape=[space(o.shape, o.dtype) for space, o in zip(out_spaces, outs)],
        in_specs=[pl.BlockSpec(memory_space=space) for space in spaces],
        out_specs=[pl.BlockSpec(memory_space=space) for space in out_spaces],
        scratch_shapes=list(scratch),
        compiler_params=pltpu.CompilerParams(vmem_limit_bytes=mib * 1024 * 1024),
        cost_estimate=pl.CostEstimate(flops=flops, bytes_accessed=nbytes, transcendentals=0),
    )(*[pltpu.with_memory_space_constraint(a, space) for a, space in zip(args, spaces)])


def exchange(messages, rows, axes=CHUNKS):
    count = lax.axis_size(axes)
    got = lax.all_to_all(messages.reshape(count, 1, rows * HALF), axes, 0, 0)
    return got.reshape(count * rows, HALF)


def on_device(x_in, b_in, c_in, decay_log, d_skip, gate, norm_weight, d_out):
    length, heads = decay_log.shape
    width = x_in.shape[1]
    chunks = lax.axis_size(CHUNKS)
    groups = lax.axis_size("heads")
    shape = jax.ShapeDtypeStruct
    wide = shape((length, width), F32)
    half_wide = shape((length, width), BF16)
    small = shape((heads, length), F32)
    narrow = shape(b_in.shape, F32)
    half_narrow = shape(b_in.shape, BF16)
    state = shape((chunks * 32, HALF), F32)
    weight = norm_weight.reshape(1, width)
    d_row = d_skip.reshape(1, heads)
    w_row, one_row = shape(weight.shape, F32), shape(d_row.shape, F32)
    decay_t = decay_log.T
    sem = pltpu.SemaphoreType.DMA

    def vmem(*shapes):
        return [pltpu.VMEM(s.shape, s.dtype) for s in shapes]

    (pay,) = call(
        start_kernel, "start", [shape((chunks * 33, HALF), F32)], decay_t, x_in, b_in,
        flops=10**9, scratch=vmem(small, half_narrow, half_wide) + [sem((3,))], hbm_in=(0, 1, 2),
    )
    got = exchange(pay, 33)
    base, esilu, c_val, c_turned, w_val, dout_val, y_near = call(
        local_kernel, "local", [wide, wide, half_narrow, shape(c_in.shape[::-1], BF16), w_row, half_wide, wide],
        decay_t, x_in, b_in, c_in, gate, d_row, weight, d_out,
        flops=8 * 10**9, hbm_in=range(8), hbm_out=(6,), mib=24,
        scratch=vmem(small, half_wide, half_narrow, half_wide, one_row, wide) + [sem((9,))],
    )
    spread, decays = call(prefix_kernel, "prefix", [state, shape((chunks, HALF), F32)], got)
    before = exchange(spread, 32)
    gated, sums = call(
        gate_kernel, "gated", [wide, shape((groups * 4, HALF), F32)],
        before, c_val, base, esilu, dout_val, w_val, flops=10**9,
    )
    sums = exchange(sums, 4, "heads")

    def back(*refs):
        back_kernel(float(width * groups), *refs)

    rows = shape((8, HALF), F32)
    pay, scalars, before = call(
        back, "back", [shape((chunks * 33, HALF), F32), rows, state],
        sums, gated, esilu, dout_val, w_val, c_turned, before,
        flops=10**9, hbm_out=(0, 1, 2), scratch=vmem(rows, shape((chunks * 33, HALF), F32)) + [sem((6,))],
    )
    got = exchange(pay, 33)
    gx, gb, gl, tail, x_val, b_val, skip, grad_gate, grad_c = call(
        grads_kernel, "grads",
        [wide, narrow, small, wide, half_wide, half_narrow, shape((8, HALF), F32), half_wide, narrow],
        decay_t, scalars, d_out, weight, x_in, gate, b_in, c_in, d_row, y_near, before,
        flops=16 * 10**9, hbm_in=range(11), hbm_out=(7, 8), mib=32,
        scratch=vmem(state, small, rows, half_wide, w_row, half_wide, half_narrow, one_row, wide, wide, wide, half_wide, narrow)
        + [sem((16,))],
    )
    (spread,) = call(suffix_kernel, "suffix", [shape((chunks * 34, HALF), F32)], got, decays, skip)
    after = exchange(spread, 34)
    outs = [half_wide, narrow, small, one_row, shape((8, HALF), F32)]
    grad_x, grad_b, grad_decay, grad_skip, grad_weight = call(
        final_kernel, "final", outs,
        after, before, decay_t, tail, x_val, b_val, gx, gb, gl,
        flops=2 * 10**9, scratch=vmem(*outs, small, state) + [sem((7,))], hbm_in=(1, 2), hbm_out=range(5),
    )
    return (
        grad_x,
        grad_b,
        grad_c,
        grad_decay.T,
        grad_skip.reshape(heads),
        grad_gate,
        grad_weight.reshape(width),
    )


def solution(mesh):
    tokens = P(CHUNKS, "heads")
    in_specs = (tokens, tokens, tokens, tokens, P("heads"), tokens, P("heads"), tokens)
    out_specs = (tokens, tokens, tokens, tokens, P("heads"), tokens, P("heads"))
    return jax.shard_map(on_device, mesh=mesh, in_specs=in_specs, out_specs=out_specs, check_vma=False)
```

```python
import jax
import jax.numpy as jnp
from jax import lax
from jax.experimental import pallas as pl
from jax.experimental.pallas import tpu as pltpu
from jax.sharding import PartitionSpec as P

P_SIZE = 64
EPS = 1e-05
F32 = jnp.float32
BF16 = jnp.bfloat16
CHUNKS = ("outer", "inner")
HALF = 128


def mm(a, b, ca=1, cb=0):
    return lax.dot_general(a, b, (((ca,), (cb,)), ((), ())), preferred_element_type=F32)


def split2(a):
    hi = a.astype(BF16)
    return hi, (a - hi.astype(F32)).astype(BF16)


def split3(a):
    hi = a.astype(BF16)
    rest = a - hi.astype(F32)
    mid = rest.astype(BF16)
    return hi, mid, (rest - mid.astype(F32)).astype(BF16)


def mm2(a, b, ca=1, cb=0):
    hi, lo = split2(a)
    return mm(hi, b, ca, cb) + mm(lo, b, ca, cb)


def mm_split(a, b):
    return mm(jnp.concatenate([a, a], axis=1), jnp.concatenate(split2(b), axis=0))


def iota(shape, dim):
    return lax.broadcasted_iota(jnp.int32, shape, dim)


def head_map(heads, width):
    return jnp.where(iota((heads, width), 1) // P_SIZE == iota((heads, width), 0), 1.0, 0.0).astype(BF16)


def expand(a, spread, rows=None):
    hi, lo = split2(a)
    both = jnp.concatenate([hi.astype(F32), lo.astype(F32)], axis=0).T.astype(BF16)
    return mm(both[:rows], jnp.concatenate([spread, spread], axis=0))


def segment(a, spread):
    turned_map = turned(spread)
    hi, lo = split2(a)
    return (mm(hi, turned_map) + mm(lo, turned_map)).T


def triangle(n, keep):
    return jnp.where(keep(iota((n, n), 0), iota((n, n), 1)), 1.0, 0.0).astype(BF16)


def mm_by_two(a, tri):
    rows = a.shape[0]
    got = mm(jnp.concatenate(split2(a), axis=0), tri)
    return got[:rows] + got[rows:]


def mm_by(a, tri):
    rows = a.shape[0]
    got = mm(jnp.concatenate(split3(a), axis=0), tri)
    return got[:rows] + got[rows : 2 * rows] + got[2 * rows :]


def load_state(ref, rows):
    return jnp.concatenate([load_block(ref, rows, k) for k in range(4)], axis=1)


def load_block(ref, rows, k):
    cols = []
    for q in (2 * k, 2 * k + 1):
        at = [rows * (4 * q + r) for r in range(4)]
        cols.append(jnp.concatenate([ref[i : i + 32, :] for i in at], axis=0))
    return jnp.concatenate(cols, axis=1)


def copies_of(pairs, sems):
    return [pltpu.make_async_copy(src, dst, sems.at[i]) for i, (src, dst) in enumerate(pairs)]


def fetch(pairs, sems):
    copies = copies_of(pairs, sems)
    for copy in copies:
        copy.start()
    return copies


def quarters(ref):
    return [ref.at[:, pl.ds(256 * k, 256)] for k in range(4)]


def turned(a):
    return a.astype(F32).T.astype(BF16)


def block_sums(lt):
    return mm_by(lt, triangle(lt.shape[1], lambda i, j: i <= j))


def below(up, zeros, left, right, i):
    return jnp.concatenate(
        [jnp.concatenate([up[i], zeros], axis=1), jnp.concatenate([left[i], right[i]], axis=1)], axis=0
    )


def skip_row(d_ref, spread):
    heads, width = spread.shape
    hi, mid, lo = split3(jnp.broadcast_to(d_ref[...], (8, heads)))
    return (mm(hi, spread) + mm(mid, spread) + mm(lo, spread))[0:1, :]


def start_kernel(lt_hbm, x_hbm, b_hbm, pay_ref, lt_ref, b_ref, x_ref, sems):
    heads, length = lt_hbm.shape
    width = x_hbm.shape[1]
    first, second, third = fetch([(lt_hbm, lt_ref), (b_hbm, b_ref), (x_hbm, x_ref)], sems)
    first.wait()
    later = triangle(length, lambda i, j: i > j)
    ends = mm_by_two(lt_ref[...], jnp.concatenate([later, jnp.ones((length, HALF), BF16)], axis=1))
    second.wait()
    b_turned = turned(b_ref[...])
    hi, lo = split2(jnp.exp(ends))
    both = jnp.concatenate([hi.astype(F32), lo.astype(F32)], axis=0).T.astype(BF16)[: length + 16]
    spread = head_map(heads, width)
    spread = jnp.concatenate([spread, spread], axis=0)
    third.wait()
    tail = mm(both, spread)
    state = mm_split(b_turned, x_ref[...].astype(F32) * tail[:length])
    for q in range(width // HALF):
        cols = slice(HALF * q, HALF * (q + 1))
        for r in range(4):
            at = 33 * (4 * q + r)
            pay_ref[at : at + 32, :] = state[32 * r : 32 * r + 32, cols]
            pay_ref[at + 32 : at + 33, :] = tail[length : length + 1, cols]


def local_kernel(
    lt_hbm, x_hbm, b_hbm, c_hbm, z_hbm, d_hbm, w_hbm, dout_hbm,
    base_ref, esilu_ref, c_ref, ct_ref, w_ref, dout_ref, yn_hbm,
    lt_ref, x_ref, b_ref, z_ref, d_ref, yn_ref, sems,
):
    heads, length = lt_hbm.shape
    width = x_hbm.shape[1]
    copies = fetch(
        [(lt_hbm, lt_ref), (b_hbm, b_ref), (c_hbm, c_ref), (x_hbm, x_ref), (z_hbm, z_ref), (d_hbm, d_ref),
         (w_hbm, w_ref), (dout_hbm, dout_ref)],
        sems,
    )
    spread = head_map(heads, width)
    for copy in copies[:3]:
        copy.wait()
    cum_t = block_sums(lt_ref[...])
    cum = cum_t.T
    ecum = expand(jnp.exp(cum_t), spread)
    ct_ref[...] = turned(c_ref[...])
    inner = mm(c_ref[...], b_ref[...], 1, 1)
    top, left, right = inner[:HALF, :HALF], inner[HALF:, :HALF], inner[HALF:, HALF:]
    lower = iota((HALF, HALF), 0) >= iota((HALF, HALF), 1)
    first = iota((length, HALF), 1) < P_SIZE
    zeros = jnp.zeros((HALF, HALF), BF16)
    for copy in copies[3:6]:
        copy.wait()
    skip = skip_row(d_ref, spread)
    for q in range(width // HALF):
        cols = slice(HALF * q, HALF * (q + 1))
        x_pair = x_ref[:, cols]
        mixes = []
        for h in (2 * q, 2 * q + 1):
            col, row = cum[:, h : h + 1], cum_t[h : h + 1, :]
            up = jnp.where(lower, jnp.exp(col[:HALF] - row[:, :HALF]), 0.0) * top
            dl = jnp.exp(col[HALF:] - row[:, :HALF]) * left
            dr = jnp.where(lower, jnp.exp(col[HALF:] - row[:, HALF:]), 0.0) * right
            mixes += [below(split2(up), zeros, split2(dl), split2(dr), i) for i in range(2)]
        got = mm(jnp.concatenate(mixes, axis=0), x_pair)
        yn = jnp.where(
            first, got[:length] + got[length : 2 * length], got[2 * length : 3 * length] + got[3 * length :]
        )
        yn_ref[:, cols] = yn
        z_val = z_ref[:, cols].astype(F32)
        silu = z_val * (1.0 / (1.0 + jnp.exp(-z_val)))
        esilu_ref[:, cols] = ecum[:, cols] * silu
        base_ref[:, cols] = (yn + skip[:, cols] * x_pair.astype(F32)) * silu
    for copy in copies[6:]:
        copy.wait()
    yn_copy = pltpu.make_async_copy(yn_ref, yn_hbm, sems.at[8])
    yn_copy.start()
    yn_copy.wait()


def prefix_kernel(in_ref, out_ref, dec_ref):
    count = dec_ref.shape[0]
    state = jnp.zeros((32, HALF), F32)
    for p in range(count):
        out_ref[32 * p : 32 * p + 32, :] = state
        decay = in_ref[33 * p + 32 : 33 * p + 33, :]
        dec_ref[p : p + 1, :] = decay
        if p < count - 1:
            state = decay * state + in_ref[33 * p : 33 * p + 32, :]


def gate_kernel(s_ref, c_ref, base_ref, esilu_ref, dout_ref, w_ref, gated_ref, sums_ref):
    c_val = c_ref[...]
    length, width = base_ref.shape
    squares = jnp.zeros((length, HALF), F32)
    products = jnp.zeros((length, HALF), F32)
    for q in range(width // 256):
        big = slice(256 * q, 256 * (q + 1))
        c_state = mm_split(c_val, load_block(s_ref, 32, q))
        gated = base_ref[:, big] + esilu_ref[:, big] * c_state
        gated_ref[:, big] = gated
        sq = gated * gated
        pr = dout_ref[:, big].astype(F32) * w_ref[:, big] * gated
        squares = squares + sq[:, :HALF] + sq[:, HALF:]
        products = products + pr[:, :HALF] + pr[:, HALF:]
    rows = [jnp.sum(total.T, axis=0, keepdims=True) for total in (squares, products)]
    tile = jnp.concatenate([row[:, HALF * i : HALF * (i + 1)] for row in rows for i in range(2)], axis=0)
    sums_ref[...] = jnp.concatenate([tile] * (sums_ref.shape[0] // 4), axis=0)


def columns(rows):
    turned_rows = jnp.concatenate([rows, jnp.zeros((HALF - 8, HALF), F32)], axis=0).T
    return [jnp.concatenate([turned_rows[:, i : i + 1], turned_rows[:, i + 1 : i + 2]], axis=0) for i in (0, 2)]


def back_kernel(
    channels, sums_ref, gated_ref, esilu_ref, dout_ref, w_ref, ct_ref, s_ref,
    pay_hbm, scal_hbm, s_hbm, scal_ref, pay_ref, sems,
):
    length, width = gated_ref.shape
    scal_copy, s_copy = copies_of([(scal_ref, scal_hbm), (s_ref, s_hbm)], sems)
    s_copy.start()
    total = sums_ref[0:4, :]
    for i in range(1, sums_ref.shape[0] // 4):
        total = total + sums_ref[4 * i : 4 * i + 4, :]
    inv = lax.rsqrt(total[0:2] / channels + EPS)
    fall = inv * inv * inv * total[2:4] / channels
    rows = jnp.concatenate([inv, fall, jnp.zeros((4, HALF), F32)], axis=0)
    scal_ref[...] = rows
    scal_copy.start()
    inv_col, fall_col = columns(rows)
    outs = []
    c_turned = ct_ref[...]
    for k in range(width // 256):
        big = slice(256 * k, 256 * (k + 1))
        gated = gated_ref[:, big]
        d_inv = dout_ref[:, big].astype(F32) * inv_col
        weight = jnp.sum(d_inv * gated, axis=0, keepdims=True)
        back = mm_split(c_turned, (d_inv * w_ref[:, big] - gated * fall_col) * esilu_ref[:, big])
        for q in (2 * k, 2 * k + 1):
            off = HALF * (q - 2 * k)
            for r in range(4):
                at = 33 * (4 * q + r)
                pay_ref[at : at + 32, :] = back[32 * r : 32 * r + 32, off : off + HALF]
                pay_ref[at + 32 : at + 33, :] = weight[:, off : off + HALF]
        if k % 2 == 1:
            rows = pl.ds(528 * (k // 2), 528)
            outs.append(pltpu.make_async_copy(pay_ref.at[rows], pay_hbm.at[rows], sems.at[2 + k]))
            outs[-1].start()
    for copy in outs:
        copy.wait()
    scal_copy.wait()
    s_copy.wait()


def grads_kernel(
    lt_hbm, scal_hbm, dout_hbm, w_hbm, x_hbm, z_hbm, b_hbm, c_hbm, d_hbm, yn_hbm, s_hbm,
    gx_ref, gb_ref, gl_ref, tail_ref, x_ref, b_ref, skip_ref, gz_hbm, gc_hbm,
    s_ref, lt_ref, scal_ref, dout_ref, w_ref, z_ref, c_ref, d_ref, yn_ref, dye_ref, dot_ref, gz_ref, gc_ref, sems,
):
    heads, length = lt_hbm.shape
    width = x_hbm.shape[1]
    copies = fetch(
        [(lt_hbm, lt_ref), (scal_hbm, scal_ref), (b_hbm, b_ref), (c_hbm, c_ref), (d_hbm, d_ref), (w_hbm, w_ref),
         (x_hbm, x_ref), (s_hbm, s_ref), (yn_hbm, yn_ref), (z_hbm, z_ref), (dout_hbm, dout_ref)],
        sems,
    )
    spread = head_map(heads, width)
    for copy in copies[:6]:
        copy.wait()
    cum_t = block_sums(lt_ref[...])
    cum = cum_t.T
    last = cum_t[:, length - 1 : length]
    ecum = expand(jnp.exp(cum_t), spread)
    tail_ref[...] = expand(jnp.exp(last - cum_t), spread)
    inv_col, fall_col = columns(scal_ref[...])
    skip = skip_row(d_ref, spread)
    b_val, c_val = b_ref[...], c_ref[...]
    inner_t = mm(b_val, c_val, 1, 1)
    left, right, low = inner_t[:HALF, :HALF], inner_t[:HALF, HALF:], inner_t[HALF:, HALF:]
    upper = iota((HALF, HALF), 0) <= iota((HALF, HALF), 1)
    first = iota((length, HALF), 1) < P_SIZE
    zeros = jnp.zeros((HALF, HALF), BF16)
    w_left = jnp.zeros((HALF, HALF), F32)
    w_right = jnp.zeros((HALF, HALF), F32)
    w_low = jnp.zeros((HALF, HALF), F32)
    skips = []
    far = jnp.zeros((length, HALF), F32)
    for copy in copies[6:]:
        copy.wait()
    for q in range(width // HALF):
        cols = slice(HALF * q, HALF * (q + 1))
        x_pair = x_ref[:, cols]
        x_val = x_pair.astype(F32)
        z_val = z_ref[:, cols].astype(F32)
        sig = 1.0 / (1.0 + jnp.exp(-z_val))
        silu = z_val * sig
        if q % 2 == 0:
            state = load_block(s_ref, 32, q // 2)
            c_state = mm_split(c_val, state)
        off = slice(HALF * (q % 2), HALF * (q % 2 + 1))
        y_near = yn_ref[:, cols] + ecum[:, cols] * c_state[:, off]
        y_val = y_near + skip[:, cols] * x_val
        d_gated = inv_col * (dout_ref[:, cols].astype(F32) * w_ref[:, cols]) - y_val * silu * fall_col
        dy = d_gated * silu
        dye_ref[:, cols] = dy * ecum[:, cols]
        gz_ref[:, cols] = (d_gated * y_val * sig * (1.0 + z_val * (1.0 - sig))).astype(BF16)
        if q % 2 == 1:
            e_hi, e_lo = split2(dye_ref[:, 128 * q - 128 : 128 * q + 128])
            both = mm(jnp.concatenate([e_hi, e_lo], axis=0), jnp.concatenate(split2(state.T), axis=1))
            far = far + both[:length, :HALF] + both[:length, HALF:] + both[length:, :HALF]
        skips.append(jnp.sum(dy * x_val, axis=0, keepdims=True))
        hi, lo = split2(dy)
        ones = jnp.concatenate([jnp.where(first, x_val, 0.0), jnp.where(first, 0.0, x_val)], axis=0).astype(BF16)
        both = jnp.concatenate([hi, lo], axis=1)
        dots = mm(jnp.concatenate([ones, ones], axis=1), both, 1, 1)
        mix_hi, mix_lo = [], []
        for k in range(2):
            h = 2 * q + k
            col, row = cum[:, h : h + 1], cum_t[h : h + 1, :]
            dot = dots[length * k : length * (k + 1)]
            dec_left = jnp.where(upper, jnp.exp(row[:, :HALF] - col[:HALF]), 0.0)
            dec_right = jnp.exp(row[:, HALF:] - col[:HALF])
            dec_low = jnp.where(upper, jnp.exp(row[:, HALF:] - col[HALF:]), 0.0)
            w_left = w_left + dec_left * dot[:HALF, :HALF]
            w_right = w_right + dec_right * dot[:HALF, HALF:]
            w_low = w_low + dec_low * dot[HALF:, HALF:]
            blocks = [split2(m) for m in (dec_left * left, dec_right * right, dec_low * low)]
            for i, mix in enumerate((mix_hi, mix_lo)):
                up = jnp.concatenate([blocks[0][i], blocks[1][i]], axis=1)
                mix.append(jnp.concatenate([up, jnp.concatenate([zeros, blocks[2][i]], axis=1)], axis=0))
        got = mm(jnp.concatenate(mix_hi + mix_lo, axis=0), both)
        got = got[: 2 * length, :HALF] + got[: 2 * length, HALF:] + got[2 * length :, :HALF]
        g_near = jnp.where(first, got[:length], got[length:])
        gx_ref[:, cols] = g_near + skip[:, cols] * dy
        dot_ref[:, cols] = dy * y_near - x_val * g_near
    w_up = jnp.concatenate([w_left, w_right], axis=1)
    low_part = mm2(w_right.T, b_val[:HALF]) + mm2(w_low.T, b_val[HALF:])
    gc_ref[...] = far + jnp.concatenate([mm2(w_left.T, b_val[:HALF]), low_part], axis=0)
    outs = fetch([(gc_ref, gc_hbm), (gz_ref, gz_hbm)], sems)
    gl_ref[...] = mm_by(segment(dot_ref[...], spread), triangle(length, lambda i, j: i >= j))
    gb_ref[:HALF, :] = mm2(w_up, c_val)
    gb_ref[HALF:, :] = mm2(w_low, c_val[HALF:])
    hi, mid, lo = split3(jnp.broadcast_to(jnp.concatenate(skips, axis=1), (8, width)))
    wide = head_map(HALF, width)
    skip_ref[...] = mm(hi, wide, 1, 1) + mm(mid, wide, 1, 1) + mm(lo, wide, 1, 1)
    for copy in outs:
        copy.wait()


def suffix_kernel(in_ref, dec_ref, skip_ref, out_ref):
    count = dec_ref.shape[0]
    state = jnp.zeros((32, HALF), F32)
    sums = in_ref[32:33, :]
    for p in range(1, count):
        sums = sums + in_ref[33 * p + 32 : 33 * p + 33, :]
    rows = jnp.concatenate([sums, skip_ref[0:1, :]], axis=0)
    for p in range(count - 1, -1, -1):
        out_ref[34 * p : 34 * p + 32, :] = state
        out_ref[34 * p + 32 : 34 * p + 34, :] = rows
        if p > 0:
            state = dec_ref[p : p + 1, :] * state + in_ref[33 * p : 33 * p + 32, :]


def final_kernel(
    a_ref, s_hbm, lt_hbm, tail_ref, x_ref, b_ref, gx_ref, gb_ref, gl_ref,
    ox_hbm, ob_hbm, ol_hbm, skip_hbm, weight_hbm, ox_ref, ob_ref, ol_ref, skip_ref, weight_ref, lt_ref, s_ref, sems,
):
    heads, length = lt_hbm.shape
    width = x_ref.shape[1]
    spread = head_map(heads, width)
    outs = [(weight_ref, weight_hbm), (skip_ref, skip_hbm), (ol_ref, ol_hbm), (ob_ref, ob_hbm), (ox_ref, ox_hbm)]
    copies = copies_of(outs + [(lt_hbm, lt_ref), (s_hbm, s_ref)], sems)
    copies[6].start()
    copies[5].start()
    after = load_state(a_ref, 34)
    tail, x_val = tail_ref[...], x_ref[...].astype(F32)
    b_after = mm_split(b_ref[...], after) * tail
    ox_ref[...] = (gx_ref[...] + b_after).astype(BF16)
    copies[4].start()
    late = segment(x_val * b_after, spread)
    x_hi, x_lo = split2(x_val * tail)
    a_hi, a_lo = split2(after.T)
    both = mm(x_hi, jnp.concatenate([a_hi, a_lo], axis=1))
    ob_ref[...] = gb_ref[...] + both[:, :HALF] + both[:, HALF:] + mm(x_lo, a_hi)
    copies[3].start()
    weight_ref[...] = jnp.concatenate([a_ref[136 * q + 32 : 136 * q + 33, :] for q in range(8)], axis=0)
    skip = a_ref[33:34, :]
    for p in range(1, a_ref.shape[0] // 34):
        skip = skip + a_ref[34 * p + 33 : 34 * p + 34, :]
    skip_ref[...] = skip[:, :heads]
    copies[0].start()
    copies[1].start()
    copies[5].wait()
    copies[6].wait()
    start = jnp.sum(load_state(s_ref, 32) * after, axis=0, keepdims=True)
    mine = iota((heads, width), 1) // P_SIZE == iota((heads, width), 0)
    start = jnp.sum(jnp.where(mine, start, 0.0), axis=1, keepdims=True)
    whole = jnp.exp(jnp.sum(lt_ref[...], axis=1, keepdims=True))
    ol_ref[...] = gl_ref[...] + mm_by_two(late, triangle(length, lambda i, j: i < j)) + whole * start
    copies[2].start()
    for copy in copies[:5]:
        copy.wait()


def call(kernel, name, outs, *args, flops=0, scratch=(), hbm_in=(), hbm_out=(), mib=16):
    nbytes = sum(a.size * a.dtype.itemsize for a in (*args, *outs))
    spaces = [pltpu.HBM if i in hbm_in else pltpu.VMEM for i in range(len(args))]
    out_spaces = [pltpu.HBM if i in hbm_out else pltpu.VMEM for i in range(len(outs))]
    return pl.pallas_call(
        kernel,
        name=name,
        out_shape=[space(o.shape, o.dtype) for space, o in zip(out_spaces, outs)],
        in_specs=[pl.BlockSpec(memory_space=space) for space in spaces],
        out_specs=[pl.BlockSpec(memory_space=space) for space in out_spaces],
        scratch_shapes=list(scratch),
        compiler_params=pltpu.CompilerParams(vmem_limit_bytes=mib * 1024 * 1024),
        cost_estimate=pl.CostEstimate(flops=flops, bytes_accessed=nbytes, transcendentals=0),
    )(*[pltpu.with_memory_space_constraint(a, space) for a, space in zip(args, spaces)])


def exchange(messages, rows, axes=CHUNKS):
    count = lax.axis_size(axes)
    got = lax.all_to_all(messages.reshape(count, 1, rows * HALF), axes, 0, 0)
    return got.reshape(count * rows, HALF)


def on_device(x_in, b_in, c_in, decay_log, d_skip, gate, norm_weight, d_out):
    length, heads = decay_log.shape
    width = x_in.shape[1]
    chunks = lax.axis_size(CHUNKS)
    groups = lax.axis_size("heads")
    shape = jax.ShapeDtypeStruct
    wide = shape((length, width), F32)
    half_wide = shape((length, width), BF16)
    small = shape((heads, length), F32)
    narrow = shape(b_in.shape, F32)
    half_narrow = shape(b_in.shape, BF16)
    state = shape((chunks * 32, HALF), F32)
    weight = norm_weight.reshape(1, width)
    d_row = d_skip.reshape(1, heads)
    w_row, one_row = shape(weight.shape, F32), shape(d_row.shape, F32)
    decay_t = decay_log.T
    sem = pltpu.SemaphoreType.DMA

    def vmem(*shapes):
        return [pltpu.VMEM(s.shape, s.dtype) for s in shapes]

    (pay,) = call(
        start_kernel, "start", [shape((chunks * 33, HALF), F32)], decay_t, x_in, b_in,
        flops=10**9, scratch=vmem(small, half_narrow, half_wide) + [sem((3,))], hbm_in=(0, 1, 2),
    )
    got = exchange(pay, 33)
    base, esilu, c_val, c_turned, w_val, dout_val, y_near = call(
        local_kernel, "local", [wide, wide, half_narrow, shape(c_in.shape[::-1], BF16), w_row, half_wide, wide],
        decay_t, x_in, b_in, c_in, gate, d_row, weight, d_out,
        flops=8 * 10**9, hbm_in=range(8), hbm_out=(6,), mib=24,
        scratch=vmem(small, half_wide, half_narrow, half_wide, one_row, wide) + [sem((9,))],
    )
    spread, decays = call(prefix_kernel, "prefix", [state, shape((chunks, HALF), F32)], got)
    before = exchange(spread, 32)
    gated, sums = call(
        gate_kernel, "gated", [wide, shape((groups * 4, HALF), F32)],
        before, c_val, base, esilu, dout_val, w_val, flops=10**9,
    )
    sums = exchange(sums, 4, "heads")

    def back(*refs):
        back_kernel(float(width * groups), *refs)

    rows = shape((8, HALF), F32)
    pay, scalars, before = call(
        back, "back", [shape((chunks * 33, HALF), F32), rows, state],
        sums, gated, esilu, dout_val, w_val, c_turned, before,
        flops=10**9, hbm_out=(0, 1, 2), scratch=vmem(rows, shape((chunks * 33, HALF), F32)) + [sem((6,))],
    )
    got = exchange(pay, 33)
    gx, gb, gl, tail, x_val, b_val, skip, grad_gate, grad_c = call(
        grads_kernel, "grads",
        [wide, narrow, small, wide, half_wide, half_narrow, shape((8, HALF), F32), half_wide, narrow],
        decay_t, scalars, d_out, weight, x_in, gate, b_in, c_in, d_row, y_near, before,
        flops=16 * 10**9, hbm_in=range(11), hbm_out=(7, 8), mib=32,
        scratch=vmem(state, small, rows, half_wide, w_row, half_wide, half_narrow, one_row, wide, wide, wide, half_wide, narrow)
        + [sem((16,))],
    )
    (spread,) = call(suffix_kernel, "suffix", [shape((chunks * 34, HALF), F32)], got, decays, skip)
    after = exchange(spread, 34)
    outs = [half_wide, narrow, small, one_row, shape((8, HALF), F32)]
    grad_x, grad_b, grad_decay, grad_skip, grad_weight = call(
        final_kernel, "final", outs,
        after, before, decay_t, tail, x_val, b_val, gx, gb, gl,
        flops=2 * 10**9, scratch=vmem(*outs, small, state) + [sem((7,))], hbm_in=(1, 2), hbm_out=range(5),
    )
    return (
        grad_x,
        grad_b,
        grad_c,
        grad_decay.T,
        grad_skip.reshape(heads),
        grad_gate,
        grad_weight.reshape(width),
    )


def solution(mesh):
    tokens = P(CHUNKS, "heads")
    in_specs = (tokens, tokens, tokens, tokens, P("heads"), tokens, P("heads"), tokens)
    out_specs = (tokens, tokens, tokens, tokens, P("heads"), tokens, P("heads"))
    return jax.shard_map(on_device, mesh=mesh, in_specs=in_specs, out_specs=out_specs, check_vma=False)
```
